32 devices in a mesh: dp: 8 (over z, core), mp: 4 (over y, x).
Axes of the slice: x: 2, y: 2, z: 4, core: 2. Of those that a mesh axis runs over, the one named last changes fastest.
Arguments:
- latents: bfloat16 [8192, 1024], P(('dp', 'mp')), may hold values from -6 to 6
- pixels: bfloat16 [16, 16384, 261], P('dp', 'mp'), may hold values from -6 to 6
- pixel_counts: int32 [16], P('dp'), may hold values from 1 to 16384, as said below
- cross_query: bfloat16 [1024, 1024], P(None, ('dp', 'mp')), may hold values from -0.1875 to 0.1875
- cross_key: bfloat16 [261, 1024], P(None, ('dp', 'mp')), may hold values from -0.375 to 0.375
- cross_value: bfloat16 [261, 1024], P(None, ('dp', 'mp')), may hold values from -0.375 to 0.375
- cross_out: bfloat16 [1024, 1024], P(None, ('dp', 'mp')), may hold values from -6 to 6
- cross_up: bfloat16 [1024, 1024], P(None, ('dp', 'mp')), may hold values from -0.1875 to 0.1875
- cross_down: bfloat16 [1024, 1024], P(None, ('dp', 'mp')), may hold values from -0.1875 to 0.1875
- block_qkv: bfloat16 [2, 1024, 3, 1024], P(None, 'dp', None, 'mp'), may hold values from -0.1875 to 0.1875
- block_out: bfloat16 [2, 1024, 1024], P(None, 'dp', 'mp'), may hold values from -3 to 3
- block_up: bfloat16 [2, 1024, 1024], P(None, 'dp', 'mp'), may hold values from -0.1875 to 0.1875
- block_down: bfloat16 [2, 1024, 1024], P(None, 'dp', 'mp'), may hold values from -0.1875 to 0.1875
- norm_gains: bfloat16 [6, 1024], P(None, ('dp', 'mp')), may hold values from 0.5 to 1.5
- norm_biases: bfloat16 [6, 1024], P(None, ('dp', 'mp')), may hold values from -1 to 1
- pixel_gain: bfloat16 [261], replicated, may hold values from 0.5 to 1.5
- pixel_bias: bfloat16 [261], replicated, may hold values from -1 to 1
- cotangent: bfloat16 [8192, 1024], P(('dp', 'mp')), may hold values from -6 to 6
Outputs:
- latents_out: bfloat16 [8192, 1024], P(('dp', 'mp'))
- latent_grad: bfloat16 [8192, 1024], P(('dp', 'mp'))
- pixel_grad: bfloat16 [16, 16384, 261], P('dp', 'mp')
- cross_query_grad: float32 [1024, 1024], P(None, ('dp', 'mp'))
- cross_key_grad: float32 [261, 1024], P(None, ('dp', 'mp'))
- cross_value_grad: float32 [261, 1024], P(None, ('dp', 'mp'))
- cross_out_grad: float32 [1024, 1024], P(None, ('dp', 'mp'))
- cross_up_grad: float32 [1024, 1024], P(None, ('dp', 'mp'))
- cross_down_grad: float32 [1024, 1024], P(None, ('dp', 'mp'))
- block_qkv_grad: float32 [2, 1024, 3, 1024], P(None, 'dp', None, 'mp')
- block_out_grad: float32 [2, 1024, 1024], P(None, 'dp', 'mp')
- block_up_grad: float32 [2, 1024, 1024], P(None, 'dp', 'mp')
- block_down_grad: float32 [2, 1024, 1024], P(None, 'dp', 'mp')
- norm_gain_grad: float32 [6, 1024], P(None, ('dp', 'mp'))
- norm_bias_grad: float32 [6, 1024], P(None, ('dp', 'mp'))
- pixel_gain_grad: float32 [261], replicated
- pixel_bias_grad: float32 [261], replicated
The draws below stay inside these ranges and needn't reach their ends.
Inputs may be any that keep to these rules, and one draw needn't show every extreme that they name: In each aligned group of 2 items one item, drawn from the seed, has exactly 16384 pixels; item i's pixels fill slots 0 to pixel_counts[i] - 1, the remaining slots are padding.
All inputs are finite; a program needn't handle non-finite values.
Results may differ from the reference program's by a relative error of at most 0.02.
Values may be sent and summed in bfloat16 or wider, within the bound.
A program may use at most 320 MiB of HBM per device.

```python
import math
import jax
import jax.numpy as jnp
from jax import lax

D = 1024
C = 261
LAT = 512
H = 8
HD = 128
F = 1024
ITEM_DP = 2
MAXPIX = 16384
LAYERS = 2
ITEMS = 16
ROWS = 8192
NORMS = 6


def draw_pixel_counts(key, part):
    key = jax.random.fold_in(key, 11)
    shift_key, lower_key, choose_key = jax.random.split(key, 3)
    halvings = jax.random.randint(shift_key, (ITEMS,), 0, 3)
    ceiling = jnp.right_shift(jnp.full((ITEMS,), MAXPIX, jnp.int32), halvings.astype(jnp.int32))
    lowered = jax.random.randint(lower_key, (ITEMS,), 0, ceiling // 2)
    counts = ceiling - lowered
    chosen = jax.random.randint(choose_key, (ITEMS // ITEM_DP,), 0, ITEM_DP)
    full_slot = jnp.arange(ITEMS) % ITEM_DP == jnp.repeat(chosen, ITEM_DP)
    return jnp.where(full_slot, MAXPIX, counts).astype(jnp.int32)


def shard_levels(stream_key, shape, cuts, smallest, high):
    loudness = 1.0
    for axis_at, parts in cuts:
        draws = jax.random.uniform(jax.random.fold_in(jax.random.fold_in(stream_key, 6), axis_at), (parts,), jnp.float32, smallest / len(cuts), high / len(cuts))
        loudness = loudness * jnp.repeat(jnp.exp(draws), shape[axis_at] // parts).reshape((-1,) + (1,) * (len(shape) - 1 - axis_at))
    return loudness


def scatter_about(stream_key, shape, deviation, reach, pieces=(), held_as=jnp.bfloat16):
    result = jax.random.normal(stream_key, shape, jnp.float32) * deviation
    if len(pieces) > 0:
        result = shard_levels(stream_key, shape, pieces, -0.22, 0.18) * result
    return jnp.clip(result, min=-reach, max=reach).astype(held_as)


def setup_inputs(seed: int = 0) -> dict:
    key_list = jax.random.split(jax.random.key(seed), 19)
    latents = scatter_about(key_list[0], (ROWS, D), 1.0, 6.0, ((0, 32),))
    pixels = scatter_about(key_list[1], (ITEMS, MAXPIX, C), 1.0, 6.0, ((0, 8), (1, 4)))
    pixel_counts = draw_pixel_counts(jax.random.fold_in(key_list[18], 71), 0)
    cross_query = scatter_about(key_list[3], (D, D), D ** -0.5, 0.1875, ((1, 32),))
    cross_key = scatter_about(key_list[4], (C, D), C ** -0.5, 0.375, ((1, 32),))
    cross_value = scatter_about(key_list[5], (C, D), C ** -0.5, 0.375, ((1, 32),))
    cross_out = scatter_about(key_list[6], (D, D), 1 ** -0.5, 6.0, ((1, 32),))
    cross_up = scatter_about(key_list[7], (D, F), D ** -0.5, 0.1875, ((1, 32),))
    cross_down = scatter_about(key_list[8], (F, D), F ** -0.5, 0.1875, ((1, 32),))
    block_qkv = scatter_about(key_list[9], (LAYERS, D, 3, D), D ** -0.5, 0.1875, ((1, 8), (3, 4)))
    block_out = scatter_about(key_list[10], (LAYERS, D, D), 4 ** -0.5, 3.0, ((1, 8), (2, 4)))
    block_up = scatter_about(key_list[11], (LAYERS, D, F), D ** -0.5, 0.1875, ((1, 8), (2, 4)))
    block_down = scatter_about(key_list[12], (LAYERS, D, F), F ** -0.5, 0.1875, ((1, 8), (2, 4)))
    norm_gains = jnp.clip(1.0 + 0.1 * jax.random.normal(key_list[13], (NORMS, D), jnp.float32), 0.5, 1.5).astype(jnp.bfloat16)
    norm_biases = scatter_about(key_list[14], (NORMS, D), 0.2, 1.0, ((1, 32),))
    pixel_gain = jnp.clip(1.0 + 0.1 * jax.random.normal(key_list[15], (C,), jnp.float32), 0.5, 1.5).astype(jnp.bfloat16)
    pixel_bias = scatter_about(key_list[16], (C,), 0.2, 1.0)
    cotangent = scatter_about(key_list[17], (ROWS, D), 1.0, 6.0, ((0, 32),))
    return dict(latents=latents, pixels=pixels, pixel_counts=pixel_counts, cross_query=cross_query, cross_key=cross_key, cross_value=cross_value, cross_out=cross_out, cross_up=cross_up, cross_down=cross_down, block_qkv=block_qkv, block_out=block_out, block_up=block_up, block_down=block_down, norm_gains=norm_gains, norm_biases=norm_biases, pixel_gain=pixel_gain, pixel_bias=pixel_bias, cotangent=cotangent)


@jax.custom_vjp
def low(v):
    return lax.optimization_barrier(v.astype(jnp.bfloat16)).astype(jnp.float32)

@jax.custom_vjp
def low_back(v):
    return v

def low_keep(v):
    return (low(v), None)

def low_pass(kept, grad):
    return (grad,)

def back_keep(v):
    return (v, None)

def back_low(kept, grad):
    return (low(grad),)
low.defvjp(low_keep, low_pass)
low_back.defvjp(back_keep, back_low)
norm_eps = 1e-05
masked_score = -1e+30
highest = lax.Precision.HIGHEST

def layer_norm(features, gain_row, offset):
    average = lax.optimization_barrier(jnp.mean(features, axis=-1, keepdims=True))
    centered = features - average
    variance = lax.optimization_barrier(jnp.mean(centered * centered, axis=-1, keepdims=True))
    return centered * lax.rsqrt(variance + norm_eps) * gain_row + offset

def product(left_side, right_side):
    return jnp.dot(left_side, right_side, precision=highest)

def self_block(current, qkv_weight, out_weight, up_weight, down_weight, gain_early, bias_early, gain_late, bias_late):
    row_count = current.shape[0]
    model_width = current.shape[1]
    block_scale = 1.0 / math.sqrt(HD)
    normed = low(layer_norm(current, gain_early, bias_early))
    projected = jnp.einsum('rd,dtk->rtk', normed, qkv_weight, precision=highest)
    queries = low_back(low(projected[:, 0])).reshape(row_count // LAT, LAT, H, HD)
    key_rows = low_back(low(projected[:, 1])).reshape(row_count // LAT, LAT, H, HD)
    value_rows = low_back(low(projected[:, 2])).reshape(row_count // LAT, LAT, H, HD)

    def one_item(inputs):
        item_queries, item_keys, item_values = inputs
        raw_scores = block_scale * low_back(jnp.einsum('qhe,khe->hqk', item_queries, item_keys, precision=highest))
        row_top = lax.optimization_barrier(jnp.max(raw_scores, axis=-1, keepdims=True))
        lifted = jnp.exp(raw_scores - row_top)
        attention = lifted / lax.optimization_barrier(jnp.sum(lifted, axis=-1, keepdims=True))
        return jnp.einsum('hqk,khe->qhe', low(attention), item_values, precision=highest)
    context = lax.map(jax.checkpoint(one_item), (queries, key_rows, value_rows))
    context = low_back(low(context.reshape(row_count, model_width)))
    middle = current + low_back(jnp.dot(context, out_weight.T, precision=highest))
    hidden = low_back(product(low(layer_norm(middle, gain_late, bias_late)), up_weight))
    return middle + low_back(jnp.dot(low(jax.nn.gelu(hidden)), down_weight.T, precision=highest))

def forward(latents, pixels, pixel_counts, cross_query, cross_key, cross_value, cross_out, cross_up, cross_down, block_qkv, block_out, block_up, block_down, norm_gains, norm_biases, pixel_gain, pixel_bias):
    row_count = latents.shape[0]
    model_width = latents.shape[1]
    item_count = pixels.shape[0]
    cross_scale = 1.0 / math.sqrt(model_width)
    query_in = low(layer_norm(latents, norm_gains[0], norm_biases[0]))
    queries = low_back(low(product(query_in, cross_query))).reshape(item_count, LAT, model_width)

    def one_item(inputs):
        item_queries, item_pixels, item_length = inputs
        present = jnp.arange(MAXPIX, dtype=jnp.int32) < item_length
        pixel_in = low(layer_norm(item_pixels, pixel_gain, pixel_bias))
        key_rows = low_back(low(product(pixel_in, cross_key)))
        value_rows = low_back(low(product(pixel_in, cross_value)))
        raw_scores = cross_scale * low_back(jnp.dot(item_queries, key_rows.T, precision=highest))
        masked = jnp.where(present[None, :], raw_scores, masked_score)
        row_top = lax.optimization_barrier(jnp.max(masked, axis=-1, keepdims=True))
        lifted = jnp.exp(masked - row_top) * present.astype(jnp.float32)[None, :]
        attention = lifted / lax.optimization_barrier(jnp.sum(lifted, axis=-1, keepdims=True))
        return product(low(attention), value_rows)
    attended = lax.map(jax.checkpoint(one_item), (queries, pixels, pixel_counts))
    context = low_back(low(attended.reshape(row_count, model_width)))
    after_cross = latents + low_back(product(context, cross_out))
    hidden = low_back(product(low(layer_norm(after_cross, norm_gains[1], norm_biases[1])), cross_up))
    current = after_cross + low_back(product(low(jax.nn.gelu(hidden)), cross_down))
    for layer_index in range(LAYERS):
        current = self_block(current, block_qkv[layer_index], block_out[layer_index], block_up[layer_index], block_down[layer_index], norm_gains[2 + 2 * layer_index], norm_biases[2 + 2 * layer_index], norm_gains[3 + 2 * layer_index], norm_biases[3 + 2 * layer_index])
    return current

def reference(latents, pixels, pixel_counts, cross_query, cross_key, cross_value, cross_out, cross_up, cross_down, block_qkv, block_out, block_up, block_down, norm_gains, norm_biases, pixel_gain, pixel_bias, cotangent):
    floats = (latents.astype(jnp.float32), pixels.astype(jnp.float32), cross_query.astype(jnp.float32), cross_key.astype(jnp.float32), cross_value.astype(jnp.float32), cross_out.astype(jnp.float32), cross_up.astype(jnp.float32), cross_down.astype(jnp.float32), block_qkv.astype(jnp.float32), block_out.astype(jnp.float32), block_up.astype(jnp.float32), block_down.astype(jnp.float32), norm_gains.astype(jnp.float32), norm_biases.astype(jnp.float32), pixel_gain.astype(jnp.float32), pixel_bias.astype(jnp.float32))

    def wrapped(operands):
        return forward(operands[0], operands[1], pixel_counts, operands[2], operands[3], operands[4], operands[5], operands[6], operands[7], operands[8], operands[9], operands[10], operands[11], operands[12], operands[13], operands[14], operands[15])
    output, pullback = jax.vjp(wrapped, floats)
    grads, = pullback(cotangent.astype(jnp.float32))
    return (output.astype(jnp.bfloat16), grads[0].astype(jnp.bfloat16), grads[1].astype(jnp.bfloat16), grads[2], grads[3], grads[4], grads[5], grads[6], grads[7], grads[8], grads[9], grads[10], grads[11], grads[12], grads[13], grads[14], grads[15])
```

```python
import functools
import math

import jax
import jax.numpy as jnp
from jax import lax
from jax.experimental import pallas as pl
from jax.experimental.pallas import tpu as pltpu
from jax.sharding import PartitionSpec as P

HD = 128


norm_eps = 1e-05
masked_score = -1e30


def joined(value, axis, join):
    pieces = jax.tree.map(lambda part: lax.all_gather(part, axis), value)
    head = jax.tree.map(lambda part: part[0], pieces)
    tail = jax.tree.map(lambda part: part[1:], pieces)
    running, _ = lax.scan(lambda running, share: (join(running, share), None), head, tail)
    return running


def layer_norm(features, gain_row, offset):
    average = jnp.mean(features, axis=-1, keepdims=True)
    centered = features - average
    variance = jnp.mean(centered * centered, axis=-1, keepdims=True)
    return centered * lax.rsqrt(variance + norm_eps) * gain_row + offset


def norm_back(features, gain_row, offset, upstream):
    _, pullback = jax.vjp(layer_norm, features, gain_row, offset)
    return pullback(upstream)


def gelu_back(hidden, upstream):
    _, pullback = jax.vjp(jax.nn.gelu, hidden)
    return pullback(upstream)[0]


def matmul(left_side, right_side):
    return jnp.dot(left_side, right_side, preferred_element_type=jnp.float32)


def times_transposed(left_side, right_side):
    return lax.dot_general(
        left_side, right_side, (((1,), (1,)), ((), ())), preferred_element_type=jnp.float32
    )


def transposed_times(left_side, right_side):
    return lax.dot_general(
        left_side, right_side, (((0,), (0,)), ((), ())), preferred_element_type=jnp.float32
    )


def gather_rows(payload):
    return lax.all_gather(payload, "mp", axis=0, tiled=True)


def gather_grads(payload):
    return lax.all_gather(payload, "mp", axis=0, tiled=True)


def sum_branch(row_term, own_rows):
    return lax.psum_scatter(
        row_term(jnp.int32(0), own_rows * lax.axis_size("mp")).astype(jnp.bfloat16),
        "mp",
        scatter_dimension=0,
        tiled=True,
    ).astype(jnp.float32)


def sum_inputs(row_term, own_rows):
    return lax.psum_scatter(
        row_term(jnp.int32(0), own_rows * lax.axis_size("mp")).astype(jnp.bfloat16),
        "mp",
        scatter_dimension=0,
        tiled=True,
    ).astype(jnp.float32)


def slicer(source):

    def row_term(first_row, row_count):
        return source

    return row_term


def product_term(source, weight, formula):

    def row_term(first_row, row_count):
        return jnp.einsum(formula, source, weight, preferred_element_type=jnp.float32)

    return row_term


def merge_stats(earlier, latter):
    row_top = jnp.maximum(earlier[0], latter[0])
    return (
        row_top,
        earlier[1] * jnp.exp(earlier[0] - row_top) + latter[1] * jnp.exp(latter[0] - row_top),
    )


def cross_params(
    cross_query, cross_key, cross_value, cross_out, cross_up, cross_down, norm_gains, norm_biases
):
    return (
        lax.all_gather(cross_query, ("dp", "mp"), axis=1, tiled=True),
        lax.all_gather(cross_key, ("dp", "mp"), axis=1, tiled=True),
        lax.all_gather(cross_value, ("dp", "mp"), axis=1, tiled=True),
        lax.all_gather(cross_out, ("dp", "mp"), axis=1, tiled=True),
        lax.all_gather(cross_up, ("dp", "mp"), axis=1, tiled=True),
        lax.all_gather(cross_down, ("dp", "mp"), axis=1, tiled=True),
        lax.all_gather(norm_gains, ("dp", "mp"), axis=1, tiled=True),
        lax.all_gather(norm_biases, ("dp", "mp"), axis=1, tiled=True),
    )


def block_weights(block_qkv, block_out, block_up, block_down, layer_index):
    return (
        lax.all_gather(block_qkv[layer_index], "dp", axis=0, tiled=True),
        lax.all_gather(block_out[layer_index], "dp", axis=0, tiled=True),
        lax.all_gather(block_up[layer_index], "dp", axis=0, tiled=True),
        lax.all_gather(block_down[layer_index], "dp", axis=0, tiled=True),
    )


def block_forward(current, layer_index, gain_rows, bias_rows, block_params, item_count):
    qkv_weight, out_weight, up_weight, down_weight = block_weights(
        block_params[0], block_params[1], block_params[2], block_params[3], layer_index
    )
    own_rows = current.shape[0]
    group_rows = own_rows * lax.axis_size("mp")
    latents_item = group_rows // item_count
    head_cols = qkv_weight.shape[2]
    heads_local = head_cols // HD
    block_scale = 1.0 / math.sqrt(HD)
    normed = layer_norm(
        current, gain_rows[2 + 2 * layer_index], bias_rows[2 + 2 * layer_index]
    ).astype(jnp.bfloat16)
    normed_group = gather_rows(normed)
    projected = jnp.einsum(
        "rd,dtk->rtk", normed_group, qkv_weight, preferred_element_type=jnp.float32
    ).astype(jnp.bfloat16)
    heads_view = projected.reshape(item_count, latents_item, 3, heads_local, HD)
    raw_scores = (
        jnp.einsum(
            "iqhe,ikhe->ihqk",
            heads_view[:, :, 0],
            heads_view[:, :, 1],
            preferred_element_type=jnp.float32,
        )
        * block_scale
    )
    row_top = jnp.max(raw_scores, axis=-1, keepdims=True)
    lifted = jnp.exp(raw_scores - row_top)
    row_total = jnp.sum(lifted, axis=-1, keepdims=True)
    attention = lifted / row_total
    log_total = row_top + jnp.log(row_total)
    context = jnp.einsum(
        "ihqk,ikhe->iqhe",
        attention.astype(jnp.bfloat16),
        heads_view[:, :, 2],
        preferred_element_type=jnp.float32,
    )
    context = context.astype(jnp.bfloat16).reshape(group_rows, head_cols)
    middle = current + sum_branch(product_term(context, out_weight, "rk,dk->rd"), own_rows)
    hidden_in = layer_norm(
        middle, gain_rows[3 + 2 * layer_index], bias_rows[3 + 2 * layer_index]
    ).astype(jnp.bfloat16)
    hidden_group = gather_rows(hidden_in)
    hidden = matmul(hidden_group, up_weight)
    active = jax.nn.gelu(hidden).astype(jnp.bfloat16)
    result = middle + sum_branch(product_term(active, down_weight, "rf,df->rd"), own_rows)
    stored = (
        qkv_weight,
        out_weight,
        up_weight,
        down_weight,
        normed_group,
        projected,
        log_total,
        context,
        middle,
        hidden_group,
        hidden,
        active,
    )
    return (result, stored)


def block_backward(upstream, current, layer_index, gain_rows, bias_rows, stored, item_count):
    (
        qkv_weight,
        out_weight,
        up_weight,
        down_weight,
        normed_group,
        projected,
        log_total,
        context,
        middle,
        hidden_group,
        hidden,
        active,
    ) = stored
    own_rows = upstream.shape[0]
    group_rows = own_rows * lax.axis_size("mp")
    latents_item = group_rows // item_count
    head_cols = qkv_weight.shape[2]
    heads_local = head_cols // HD
    block_scale = 1.0 / math.sqrt(HD)
    down_group = gather_grads(upstream.astype(jnp.bfloat16))
    down_grad = transposed_times(down_group, active)
    active_cot = matmul(down_group, down_weight)
    hidden_cot = gelu_back(hidden, active_cot).astype(jnp.bfloat16)
    up_grad = transposed_times(hidden_group, hidden_cot)
    hidden_in_cot = sum_inputs(product_term(hidden_cot, up_weight, "rf,df->rd"), own_rows)
    middle_cot, gain_late, bias_late = norm_back(
        middle, gain_rows[3 + 2 * layer_index], bias_rows[3 + 2 * layer_index], hidden_in_cot
    )
    middle_cot = middle_cot + upstream
    out_group = gather_grads(middle_cot.astype(jnp.bfloat16))
    out_grad = transposed_times(out_group, context)
    context_cot = (
        matmul(out_group, out_weight)
        .astype(jnp.bfloat16)
        .reshape(item_count, latents_item, heads_local, HD)
    )
    heads_view = projected.reshape(item_count, latents_item, 3, heads_local, HD)
    queries = heads_view[:, :, 0]
    key_rows = heads_view[:, :, 1]
    value_rows = heads_view[:, :, 2]
    raw_scores = (
        jnp.einsum("iqhe,ikhe->ihqk", queries, key_rows, preferred_element_type=jnp.float32)
        * block_scale
    )
    attention = jnp.exp(raw_scores - log_total)
    value_cot = jnp.einsum(
        "ihqk,iqhe->ikhe",
        attention.astype(jnp.bfloat16),
        context_cot,
        preferred_element_type=jnp.float32,
    )
    prob_cot = jnp.einsum(
        "iqhe,ikhe->ihqk", context_cot, value_rows, preferred_element_type=jnp.float32
    )
    row_terms = jnp.sum(attention * prob_cot, axis=-1, keepdims=True)
    score_cot = (attention * (prob_cot - row_terms) * block_scale).astype(jnp.bfloat16)
    query_cot = jnp.einsum(
        "ihqk,ikhe->iqhe", score_cot, key_rows, preferred_element_type=jnp.float32
    )
    key_cot = jnp.einsum("ihqk,iqhe->ikhe", score_cot, queries, preferred_element_type=jnp.float32)
    projected_cot = jnp.stack(
        [
            query_cot.astype(jnp.bfloat16),
            key_cot.astype(jnp.bfloat16),
            value_cot.astype(jnp.bfloat16),
        ],
        axis=2,
    )
    projected_cot = projected_cot.reshape(group_rows, 3, head_cols)
    qkv_grad = jnp.einsum(
        "rd,rtk->dtk", normed_group, projected_cot, preferred_element_type=jnp.float32
    )
    normed_cot = sum_inputs(product_term(projected_cot, qkv_weight, "rtk,dtk->rd"), own_rows)
    input_cot, gain_early, bias_early = norm_back(
        current, gain_rows[2 + 2 * layer_index], bias_rows[2 + 2 * layer_index], normed_cot
    )
    input_cot = input_cot + middle_cot
    summed = (
        lax.psum_scatter(
            qkv_grad.astype(jnp.bfloat16), "dp", scatter_dimension=0, tiled=True
        ).astype(jnp.float32),
        lax.psum_scatter(
            out_grad.astype(jnp.bfloat16), "dp", scatter_dimension=0, tiled=True
        ).astype(jnp.float32),
        lax.psum_scatter(
            up_grad.astype(jnp.bfloat16), "dp", scatter_dimension=0, tiled=True
        ).astype(jnp.float32),
        lax.psum_scatter(
            down_grad.astype(jnp.bfloat16), "dp", scatter_dimension=0, tiled=True
        ).astype(jnp.float32),
    )
    return (input_cot, summed, (gain_early, bias_early, gain_late, bias_late))


def shards(
    latents,
    pixels,
    pixel_counts,
    cross_query,
    cross_key,
    cross_value,
    cross_out,
    cross_up,
    cross_down,
    block_qkv,
    block_out,
    block_up,
    block_down,
    norm_gains,
    norm_biases,
    pixel_gain,
    pixel_bias,
    cotangent,
):
    layers = block_qkv.shape[0]
    item_count = pixels.shape[0]
    pixel_rows = pixels.shape[1]
    own_rows = latents.shape[0]
    model_width = latents.shape[1]
    group_rows = own_rows * lax.axis_size("mp")
    latents_item = group_rows // item_count
    cross_scale = 1.0 / math.sqrt(model_width)
    block_params = (block_qkv, block_out, block_up, block_down)
    forward_params = cross_params(
        cross_query,
        cross_key,
        cross_value,
        cross_out,
        cross_up,
        cross_down,
        norm_gains,
        norm_biases,
    )
    (
        query_weight,
        key_weight,
        value_weight,
        out_weight,
        up_weight,
        down_weight,
        gain_table,
        bias_table,
    ) = forward_params
    gain_rows = gain_table.astype(jnp.float32)
    bias_rows = bias_table.astype(jnp.float32)
    start_rows = latents.astype(jnp.float32)
    query_in = layer_norm(start_rows, gain_rows[0], bias_rows[0]).astype(jnp.bfloat16)
    query_own = matmul(query_in, query_weight).astype(jnp.bfloat16)
    query_group = gather_rows(query_own).reshape(item_count, latents_item, model_width)
    pixel_floats = pixels.astype(jnp.float32)
    pixel_gain_row = pixel_gain.astype(jnp.float32)
    pixel_bias_row = pixel_bias.astype(jnp.float32)
    pixel_in = layer_norm(pixel_floats, pixel_gain_row, pixel_bias_row).astype(jnp.bfloat16)
    pair_weight = jnp.concatenate([key_weight, value_weight], axis=1)
    pair_rows = jnp.einsum(
        "ipc,cd->ipd", pixel_in, pair_weight, preferred_element_type=jnp.float32
    ).astype(jnp.bfloat16)
    key_rows = pair_rows[:, :, :model_width]
    value_rows = pair_rows[:, :, model_width:]
    positions = lax.axis_index("mp") * pixel_rows + jnp.arange(pixel_rows, dtype=jnp.int32)
    present = positions[None, :] < pixel_counts[:, None]
    present_mask = present.astype(jnp.float32)[:, None, :]

    def cross_scores():
        raw_scores = (
            jnp.einsum("iqd,ipd->iqp", query_group, key_rows, preferred_element_type=jnp.float32)
            * cross_scale
        )
        return jnp.where(present[:, None, :], raw_scores, masked_score)

    scores = cross_scores()
    local_top = jnp.max(scores, axis=-1)
    local_total = jnp.sum(jnp.exp(scores - local_top[:, :, None]) * present_mask, axis=-1)
    group_top, group_total = joined((local_top, local_total), "mp", merge_stats)
    log_total = (group_top + jnp.log(group_total))[:, :, None]
    attention = jnp.exp(scores - log_total) * present_mask
    attended = jnp.einsum(
        "iqp,ipd->iqd",
        attention.astype(jnp.bfloat16),
        value_rows,
        preferred_element_type=jnp.float32,
    )
    attended = attended.reshape(group_rows, model_width)
    context_own = sum_branch(slicer(attended), own_rows).astype(jnp.bfloat16)
    after_cross = start_rows + matmul(context_own, out_weight)
    cross_hidden_in = layer_norm(after_cross, gain_rows[1], bias_rows[1]).astype(jnp.bfloat16)
    cross_hidden = matmul(cross_hidden_in, up_weight)
    cross_active = jax.nn.gelu(cross_hidden).astype(jnp.bfloat16)
    current = after_cross + matmul(cross_active, down_weight)
    inputs_kept = []
    stored_all = []
    for layer_index in range(layers):
        inputs_kept.append(current)
        current, stored = block_forward(
            current, layer_index, gain_rows, bias_rows, block_params, item_count
        )
        stored_all.append(stored)
    latents_out = current.astype(jnp.bfloat16)
    later_params = cross_params(
        cross_query,
        cross_key,
        cross_value,
        cross_out,
        cross_up,
        cross_down,
        norm_gains,
        norm_biases,
    )
    (
        query_weight,
        key_weight,
        value_weight,
        out_weight,
        up_weight,
        down_weight,
        gain_table,
        bias_table,
    ) = later_params
    gain_rows = gain_table.astype(jnp.float32)
    bias_rows = bias_table.astype(jnp.float32)
    gain_parts = [None] * (2 * layers + 2)
    bias_parts = [None] * (2 * layers + 2)
    qkv_grads = [None] * layers
    out_grads = [None] * layers
    up_grads = [None] * layers
    down_grads = [None] * layers
    current_cot = cotangent.astype(jnp.float32)
    for layer_index in reversed(range(layers)):
        _, stored = block_forward(
            inputs_kept[layer_index], layer_index, gain_rows, bias_rows, block_params, item_count
        )
        current_cot, summed, norm_parts = block_backward(
            current_cot,
            inputs_kept[layer_index],
            layer_index,
            gain_rows,
            bias_rows,
            stored,
            item_count,
        )
        qkv_grads[layer_index] = summed[0]
        out_grads[layer_index] = summed[1]
        up_grads[layer_index] = summed[2]
        down_grads[layer_index] = summed[3]
        gain_parts[2 + 2 * layer_index] = norm_parts[0]
        bias_parts[2 + 2 * layer_index] = norm_parts[1]
        gain_parts[3 + 2 * layer_index] = norm_parts[2]
        bias_parts[3 + 2 * layer_index] = norm_parts[3]
    down_in = current_cot.astype(jnp.bfloat16)
    cross_down_grad = transposed_times(cross_active, down_in)
    active_cot = times_transposed(down_in, down_weight)
    hidden_cot = gelu_back(cross_hidden, active_cot).astype(jnp.bfloat16)
    cross_up_grad = transposed_times(cross_hidden_in, hidden_cot)
    hidden_in_cot = times_transposed(hidden_cot, up_weight)
    after_cot, gain_parts[1], bias_parts[1] = norm_back(
        after_cross, gain_rows[1], bias_rows[1], hidden_in_cot
    )
    after_cot = after_cot + current_cot
    out_in = after_cot.astype(jnp.bfloat16)
    cross_out_grad = transposed_times(context_own, out_in)
    context_cot = times_transposed(out_in, out_weight).astype(jnp.bfloat16)
    context_group = gather_grads(context_cot).reshape(item_count, latents_item, model_width)
    scores = cross_scores()
    attention = jnp.exp(scores - log_total) * present_mask
    value_cot = jnp.einsum(
        "iqp,iqd->ipd",
        attention.astype(jnp.bfloat16),
        context_group,
        preferred_element_type=jnp.float32,
    ).astype(jnp.bfloat16)
    prob_cot = jnp.einsum(
        "iqd,ipd->iqp", context_group, value_rows, preferred_element_type=jnp.float32
    )
    row_part = jnp.sum(attention * prob_cot, axis=-1)
    row_terms = lax.psum(row_part, "mp")
    score_cot = (attention * (prob_cot - row_terms[:, :, None]) * cross_scale).astype(jnp.bfloat16)
    query_part = jnp.einsum(
        "iqp,ipd->iqd", score_cot, key_rows, preferred_element_type=jnp.float32
    ).reshape(group_rows, model_width)
    query_cot = sum_inputs(slicer(query_part), own_rows).astype(jnp.bfloat16)
    key_cot = jnp.einsum(
        "iqp,iqd->ipd", score_cot, query_group, preferred_element_type=jnp.float32
    ).astype(jnp.bfloat16)
    cross_query_grad = transposed_times(query_in, query_cot)
    query_in_cot = times_transposed(query_cot, query_weight)
    start_cot, gain_parts[0], bias_parts[0] = norm_back(
        start_rows, gain_rows[0], bias_rows[0], query_in_cot
    )
    latent_grad = (start_cot + after_cot).astype(jnp.bfloat16)
    pair_weight = jnp.concatenate([key_weight, value_weight], axis=1)
    pair_cot = jnp.concatenate([key_cot, value_cot], axis=2)
    pair_grad = jnp.einsum("ipc,ipd->cd", pixel_in, pair_cot, preferred_element_type=jnp.float32)
    cross_key_grad = pair_grad[:, :model_width]
    cross_value_grad = pair_grad[:, model_width:]
    pixel_in_cot = jnp.einsum(
        "ipd,cd->ipc", pair_cot, pair_weight, preferred_element_type=jnp.float32
    )
    pixel_cot, pixel_gain_part, pixel_bias_part = norm_back(
        pixel_floats, pixel_gain_row, pixel_bias_row, pixel_in_cot
    )
    pixel_grad = pixel_cot.astype(jnp.bfloat16)
    gain_stack = jnp.stack(gain_parts, axis=0)
    bias_stack = jnp.stack(bias_parts, axis=0)
    cross_summed = (
        lax.psum_scatter(cross_query_grad, ("dp", "mp"), scatter_dimension=1, tiled=True),
        lax.psum_scatter(cross_key_grad, ("dp", "mp"), scatter_dimension=1, tiled=True),
        lax.psum_scatter(cross_value_grad, ("dp", "mp"), scatter_dimension=1, tiled=True),
        lax.psum_scatter(cross_out_grad, ("dp", "mp"), scatter_dimension=1, tiled=True),
        lax.psum_scatter(cross_up_grad, ("dp", "mp"), scatter_dimension=1, tiled=True),
        lax.psum_scatter(cross_down_grad, ("dp", "mp"), scatter_dimension=1, tiled=True),
        lax.psum_scatter(gain_stack, ("dp", "mp"), scatter_dimension=1, tiled=True),
        lax.psum_scatter(bias_stack, ("dp", "mp"), scatter_dimension=1, tiled=True),
    )
    pixel_gain_grad, pixel_bias_grad = lax.psum((pixel_gain_part, pixel_bias_part), ("dp", "mp"))
    return (
        latents_out,
        latent_grad,
        pixel_grad,
        cross_summed[0],
        cross_summed[1],
        cross_summed[2],
        cross_summed[3],
        cross_summed[4],
        cross_summed[5],
        jnp.stack(qkv_grads, axis=0),
        jnp.stack(out_grads, axis=0),
        jnp.stack(up_grads, axis=0),
        jnp.stack(down_grads, axis=0),
        cross_summed[6],
        cross_summed[7],
        pixel_gain_grad,
        pixel_bias_grad,
    )


MESH_ID = pl.DeviceIdType.MESH
ANY = pl.BlockSpec(memory_space=pl.ANY)
DMA = pltpu.SemaphoreType.DMA


def place():
    dp = lax.axis_index("dp")
    mp = lax.axis_index("mp")
    return dp, mp, dp // 2, dp % 2, mp // 2, mp % 2


def greet(targets):
    barrier = pltpu.get_barrier_semaphore()
    for device, condition in targets:

        def signal(device=device):
            pl.semaphore_signal(barrier, inc=1, device_id=device, device_id_type=MESH_ID)

        if condition is None:
            signal()
        else:
            pl.when(condition)(signal)
    fixed = sum(1 for _, condition in targets if condition is None)
    varying = [condition.astype(jnp.int32) for _, condition in targets if condition is not None]
    pl.semaphore_wait(barrier, sum(varying, fixed))


def remote(source, target, send, recv, device):
    return pltpu.make_async_remote_copy(
        src_ref=source,
        dst_ref=target,
        send_sem=send,
        recv_sem=recv,
        device_id=device,
        device_id_type=MESH_ID,
    )


def when(condition, action):
    if condition is None:
        action()
    else:
        pl.when(condition)(action)


def both(first, second):
    if first is None:
        return second
    if second is None:
        return first
    return jnp.logical_and(first, second)


class Gatherer:
    def __init__(self, line, slabs, outs, by_mp, sems):
        self.line = line
        self.slabs = slabs
        self.outs = outs
        self.by_mp = by_mp
        (
            self.own_sem,
            self.line_send,
            self.line_recv,
            self.plane_send,
            self.plane_recv,
            self.pass_send,
            self.pass_recv,
            self.core_send,
            self.core_recv,
        ) = sems
        self.dp, self.mp, self.z, self.core, self.y, self.x = place()

    @staticmethod
    def sem_shapes(chunks, line):
        return [
            DMA((chunks,)),
            DMA((chunks, line, 2)),
            DMA((chunks, line)),
            DMA((chunks, line, 2)),
            DMA((chunks, line, 2)),
            DMA((chunks, line, 2)),
            DMA((chunks, line, 2)),
            DMA((chunks, line, 4)),
            DMA((chunks, line, 4)),
        ]

    def partners(self):
        z = self.z
        return [
            ((self.dp + 2, self.mp), z < self.line - 1),
            ((self.dp - 2, self.mp), z > 0),
            ((self.dp, self.mp ^ 1), None),
            ((self.dp, self.mp ^ 2), None),
            ((self.dp ^ 1, self.mp), None),
        ]

    def slot(self, chunk, z, core, mp):
        out = self.outs[chunk]
        return out.at[mp, 2 * z + core] if self.by_mp[chunk] else out.at[2 * z + core, mp]

    def halves(self, ref):
        rows = ref.shape[0] // 2
        return ref.at[pl.ds(0, rows)], ref.at[pl.ds(rows, rows)]

    def line_copy(self, chunk, z, way, source=None):
        slot = self.slot(chunk, z, self.core, self.mp)
        step = 2 if way == 0 else -2
        return remote(
            slot if source is None else source,
            slot,
            self.line_send.at[chunk, z, way],
            self.line_recv.at[chunk, z],
            (self.dp + step, self.mp),
        )

    def plane_copy(self, chunk, z, way, source=None):
        slot = self.slot(chunk, z, self.core, self.mp)
        return remote(
            slot if source is None else source,
            slot,
            self.plane_send.at[chunk, z, way],
            self.plane_recv.at[chunk, z, way],
            (self.dp, self.mp ^ (1 if way == 0 else 2)),
        )

    def pass_copy(self, chunk, z, way):
        slot = self.slot(chunk, z, self.core, self.mp ^ (1 if way == 0 else 2))
        half = self.halves(slot)[way]
        return remote(
            half,
            half,
            self.pass_send.at[chunk, z, way],
            self.pass_recv.at[chunk, z, way],
            (self.dp, self.mp ^ (2 if way == 0 else 1)),
        )

    def core_copy(self, chunk, z, mp, turn):
        slot = self.slot(chunk, z, self.core, mp)
        return remote(
            slot,
            slot,
            self.core_send.at[chunk, z, turn],
            self.core_recv.at[chunk, z, turn],
            (self.dp ^ 1, self.mp),
        )

    def arrivals(self):
        z = self.z
        order = [(z, None, None)]
        for distance in range(1, self.line):
            order.append((z - distance, z >= distance, 0))
            order.append((z + distance, z + distance < self.line, 1))
        return order

    def own_copy(self, chunk):
        return pltpu.make_async_copy(
            self.slabs[chunk], self.slot(chunk, self.z, self.core, self.mp), self.own_sem.at[chunk]
        )

    def can_pass(self, way):
        return self.z < self.line - 1 if way == 0 else self.z > 0

    def begin(self, chunk):
        self.own_copy(chunk).start()
        slab = self.slabs[chunk]
        for way in (0, 1):
            when(
                self.can_pass(way),
                lambda way=way: self.line_copy(chunk, self.z, way, slab).start(),
            )
        for way in (0, 1):
            self.plane_copy(chunk, self.z, way, slab).start()

    def stage_line(self, chunk, turn):
        if turn == 0:
            self.begin(chunk)
            return
        z, condition, way = self.arrivals()[turn]

        def act():
            self.line_copy(chunk, z, way).wait_recv()
            when(self.can_pass(way), lambda: self.line_copy(chunk, z, way).start())
            for plane_way in (0, 1):
                self.plane_copy(chunk, z, plane_way).start()

        when(condition, act)

    def stage_plane(self, chunk, turn):
        z, condition, _ = self.arrivals()[turn]

        def act():
            for way in (0, 1):
                self.plane_copy(chunk, z, way).wait_recv()
                self.pass_copy(chunk, z, way).start()
            if turn == 0:
                self.own_copy(chunk).wait()
            self.core_copy(chunk, z, self.mp, 0).start()
            self.core_copy(chunk, z, self.mp ^ 1, 1).start()
            self.core_copy(chunk, z, self.mp ^ 2, 2).start()

        when(condition, act)

    def stage_pass(self, chunk, turn):
        z, condition, _ = self.arrivals()[turn]

        def act():
            for way in (0, 1):
                self.pass_copy(chunk, z, way).wait_recv()
            self.core_copy(chunk, z, self.mp ^ 3, 3).start()

        when(condition, act)

    def stage_core(self, chunk, turn):
        z, condition, _ = self.arrivals()[turn]

        def act():
            for piece in range(4):
                self.core_copy(chunk, z, self.mp, piece).wait_recv()

        when(condition, act)

    def drain(self, chunk):
        for turn, (z, condition, way) in enumerate(self.arrivals()):

            def act(turn=turn, z=z, way=way):
                if turn == 0:
                    for own_way in (0, 1):
                        when(
                            self.can_pass(own_way),
                            lambda own_way=own_way: self.line_copy(
                                chunk, z, own_way, self.slabs[chunk]
                            ).wait_send(),
                        )
                else:
                    when(self.can_pass(way), lambda: self.line_copy(chunk, z, way).wait_send())
                for plane_way in (0, 1):
                    self.plane_copy(chunk, z, plane_way).wait_send()
                    self.pass_copy(chunk, z, plane_way).wait_send()
                for piece in range(4):
                    self.core_copy(chunk, z, self.mp, piece).wait_send()

            when(condition, act)

    def steps(self, chunks, lag=2):
        turns = 2 * self.line - 1
        units = [(chunk, turn) for chunk in chunks for turn in range(turns)]
        todo = []
        for at in range(len(units) + 3 * lag):
            for stage, late in (
                (self.stage_line, 0),
                (self.stage_plane, lag),
                (self.stage_pass, 2 * lag),
                (self.stage_core, 3 * lag),
            ):
                if 0 <= at - late < len(units):
                    todo.append(functools.partial(stage, *units[at - late]))
        for chunk in chunks:
            todo.append(functools.partial(self.drain, chunk))
        return todo


def gather_all(slabs, by_mp, line):
    count = len(slabs)

    def kernel(*refs):
        ins, outs, sems = refs[:count], refs[count : 2 * count], refs[2 * count :]
        gatherer = Gatherer(line, ins, outs, by_mp, sems)
        greet(gatherer.partners())
        for step in gatherer.steps(range(count)):
            step()

    shapes = tuple(
        jax.ShapeDtypeStruct(
            ((4, 2 * line) if over_mp else (2 * line, 4)) + slab.shape, slab.dtype
        )
        for slab, over_mp in zip(slabs, by_mp)
    )
    return pl.pallas_call(
        kernel,
        out_shape=shapes,
        in_specs=[ANY] * count,
        out_specs=[ANY] * count,
        scratch_shapes=Gatherer.sem_shapes(count, line),
        compiler_params=pltpu.CompilerParams(collective_id=0, has_side_effects=True),
        name="weight_gather",
    )(*slabs)


class Reducer:
    def __init__(self, line, parts, outs, by_mp, scratch):
        self.line = line
        self.parts = parts
        self.outs = outs
        self.by_mp = by_mp
        count = len(parts)
        self.core_in = scratch[:count]
        self.own_in = scratch[count : 2 * count]
        self.pass_in = scratch[2 * count : 3 * count]
        self.plane_in = scratch[3 * count : 4 * count]
        self.line_in = scratch[4 * count : 5 * count]
        (
            self.own_sem,
            self.core_send,
            self.core_recv,
            self.pass_send,
            self.pass_recv,
            self.plane_send,
            self.plane_recv,
            self.line_send,
            self.line_recv,
        ) = scratch[5 * count :]
        self.dp, self.mp, self.z, self.core, self.y, self.x = place()

    @staticmethod
    def scratch_shapes(slabs, line):
        def buffers(lead, halve=False):
            return [
                pltpu.VMEM(
                    lead + ((rows // 2 if halve else rows), cols), jnp.bfloat16
                )
                for rows, cols in slabs
            ]

        chunks = len(slabs)
        return (
            buffers((line, 4))
            + buffers((4,))
            + buffers((line, 2), True)
            + buffers((line, 2))
            + buffers((line, 2))
            + [
                DMA((chunks, 4)),
                DMA((chunks, line, 4)),
                DMA((chunks, line, 4)),
                DMA((chunks, line, 2)),
                DMA((chunks, line, 2)),
                DMA((chunks, line, 2)),
                DMA((chunks, line, 2)),
                DMA((chunks, line, 2)),
                DMA((chunks, line, 2)),
            ]
        )

    partners = Gatherer.partners
    halves = Gatherer.halves

    def part(self, chunk, z, core, mp):
        part = self.parts[chunk]
        return part.at[mp, 2 * z + core] if self.by_mp[chunk] else part.at[2 * z + core, mp]

    def core_copy(self, chunk, z, mp):
        return remote(
            self.part(chunk, z, 1 - self.core, mp),
            self.core_in[chunk].at[z, mp],
            self.core_send.at[chunk, z, mp],
            self.core_recv.at[chunk, z, mp],
            (self.dp ^ 1, self.mp),
        )

    def own_copy(self, chunk, z, mp):
        return pltpu.make_async_copy(
            self.part(chunk, z, self.core, mp),
            self.own_in[chunk].at[mp],
            self.own_sem.at[chunk, mp],
        )

    def pass_copy(self, chunk, z, way):
        half = self.halves(self.core_in[chunk].at[z, self.mp ^ 3])[way]
        return remote(
            half,
            self.pass_in[chunk].at[z, way],
            self.pass_send.at[chunk, z, way],
            self.pass_recv.at[chunk, z, way],
            (self.dp, self.mp ^ (2 if way == 0 else 1)),
        )

    def plane_copy(self, chunk, z, way):
        mate = self.mp ^ (1 if way == 0 else 2)
        return remote(
            self.core_in[chunk].at[z, mate],
            self.plane_in[chunk].at[z, way],
            self.plane_send.at[chunk, z, way],
            self.plane_recv.at[chunk, z, way],
            (self.dp, mate),
        )

    def line_copy(self, chunk, z, way):
        return remote(
            self.core_in[chunk].at[z, self.mp],
            self.line_in[chunk].at[z, way],
            self.line_send.at[chunk, z, way],
            self.line_recv.at[chunk, z, way],
            (self.dp + (-2 if way == 0 else 2), self.mp),
        )

    @staticmethod
    def add(target, sources, result=None):
        rows = target.shape[0]
        step = 16

        def body(turn, carry):
            at = pl.ds(pl.multiple_of(turn * step, step), step)
            total = target[at, :].astype(jnp.float32)
            for source in sources:
                total = total + source[at, :].astype(jnp.float32)
            if result is None:
                target[at, :] = total.astype(jnp.bfloat16)
            else:
                result[at, :] = total
            return carry

        lax.fori_loop(0, rows // step, body, 0)

    def order(self):
        low, high, found = 0, self.line - 1, []
        while low <= high:
            found.append(low)
            if high != low:
                found.append(high)
            low, high = low + 1, high - 1
        return found

    def stage_begin(self, chunk, z):
        for mp in range(4):
            self.core_copy(chunk, z, mp).start()

    def stage_core(self, chunk, z):
        for mp in range(4):
            self.own_copy(chunk, z, mp).start()
        for mp in range(4):
            self.core_copy(chunk, z, mp).wait_recv()
            self.own_copy(chunk, z, mp).wait()
            self.add(self.core_in[chunk].at[z, mp], [self.own_in[chunk].at[mp]])
        for way in (0, 1):
            self.pass_copy(chunk, z, way).start()

    def stage_pass(self, chunk, z):
        for way in (0, 1):
            self.pass_copy(chunk, z, way).wait_recv()
            mate = self.mp ^ (1 if way == 0 else 2)
            self.add(
                self.halves(self.core_in[chunk].at[z, mate])[way],
                [self.pass_in[chunk].at[z, way]],
            )
            self.plane_copy(chunk, z, way).start()

    def stage_plane(self, chunk, z):
        for way in (0, 1):
            self.plane_copy(chunk, z, way).wait_recv()
        self.add(
            self.core_in[chunk].at[z, self.mp],
            [self.plane_in[chunk].at[z, 0], self.plane_in[chunk].at[z, 1]],
        )
        last = self.line - 1
        if z < last:
            when(self.z == last, lambda: self.line_copy(chunk, z, 0).start())
        if z > 0:
            when(self.z == 0, lambda: self.line_copy(chunk, z, 1).start())

    def stage_line(self, chunk, z):
        last = self.line - 1
        mine = self.core_in[chunk].at[z, self.mp]

        def join(way):
            self.line_copy(chunk, z, way).wait_recv()
            self.add(mine, [self.line_in[chunk].at[z, way]])
            self.line_copy(chunk, z, way).start()

        when(jnp.logical_and(self.z > z, self.z < last), lambda: join(0))
        when(jnp.logical_and(self.z < z, self.z > 0), lambda: join(1))

        def finish():
            sources = []
            if z < last:
                self.line_copy(chunk, z, 0).wait_recv()
                sources.append(self.line_in[chunk].at[z, 0])
            if z > 0:
                self.line_copy(chunk, z, 1).wait_recv()
                sources.append(self.line_in[chunk].at[z, 1])
            self.add(mine, sources, self.outs[chunk])

        when(self.z == z, finish)

    def drain(self, chunk, z):
        for mp in range(4):
            self.core_copy(chunk, z, mp).wait_send()
        for way in (0, 1):
            self.pass_copy(chunk, z, way).wait_send()
            self.plane_copy(chunk, z, way).wait_send()
        when(self.z > z, lambda: self.line_copy(chunk, z, 0).wait_send())
        when(self.z < z, lambda: self.line_copy(chunk, z, 1).wait_send())

    def steps(self, chunks, lag=1):
        units = [(chunk, z) for chunk in chunks for z in self.order()]
        todo = [functools.partial(self.stage_begin, *unit) for unit in units]
        for at in range(len(units) + 3 * lag):
            for stage, late in (
                (self.stage_core, 0),
                (self.stage_pass, lag),
                (self.stage_plane, 2 * lag),
                (self.stage_line, 3 * lag),
            ):
                if 0 <= at - late < len(units):
                    todo.append(functools.partial(stage, *units[at - late]))
        for unit in units:
            todo.append(functools.partial(self.drain, *unit))
        return todo


def reduce_all(parts, by_mp, line):
    count = len(parts)
    slabs = [part.shape[2:] for part in parts]

    def kernel(*refs):
        ins, outs, scratch = refs[:count], refs[count : 2 * count], refs[2 * count :]
        reducer = Reducer(line, ins, outs, by_mp, scratch)
        greet(reducer.partners())
        for step in reducer.steps(range(count)):
            step()

    return pl.pallas_call(
        kernel,
        out_shape=tuple(jax.ShapeDtypeStruct(slab, jnp.float32) for slab in slabs),
        in_specs=[ANY] * count,
        out_specs=[pl.BlockSpec(memory_space=pltpu.VMEM)] * count,
        scratch_shapes=Reducer.scratch_shapes(slabs, line),
        compiler_params=pltpu.CompilerParams(
            collective_id=1, has_side_effects=True, vmem_limit_bytes=60 * 1024 * 1024
        ),
        name="grad_reduce",
    )(*parts)


def exchange(arrays, kind, collective_id):
    count = len(arrays)
    sources = {"mp": 4, "mp_split": 4, "to_work": 4, "from_work": 4}[kind]

    def kernel(*refs):
        ins, outs = refs[:count], refs[count : 2 * count]
        own_sem, send_sem, recv_sem = refs[2 * count :]
        dp, mp, z, core, y, x = place()
        greet(
            [
                ((dp ^ flip_core, mp ^ flip_mp), None)
                for flip_core in (0, 1)
                for flip_mp in range(4)
                if flip_core or flip_mp
            ]
        )
        todo = []
        for at in range(count):
            for turn in range(4):
                if kind == "mp":
                    peer = mp ^ turn
                    device, slot, piece, frm = (dp, peer), mp, ins[at], peer
                elif kind == "mp_split":
                    peer = mp ^ turn
                    device, slot, piece, frm = (dp, peer), mp, ins[at].at[peer], peer
                elif kind == "to_work":
                    device = (2 * z + turn % 2, 2 * core + turn // 2)
                    slot, piece, frm = mp, ins[at].at[turn], turn
                else:
                    device = (2 * z + mp // 2, turn)
                    slot, piece, frm = 2 * (mp % 2) + core, ins[at], turn
                here = jnp.logical_and(device[0] == dp, device[1] == mp)
                todo.append((at, turn, device, slot, piece, frm, here))
        for at, turn, device, slot, piece, frm, here in todo:
            out = outs[at].at[slot]
            when(
                jnp.logical_not(here),
                lambda: remote(
                    piece, out, send_sem.at[at, turn], recv_sem.at[at, slot], device
                ).start(),
            )
            when(here, lambda: pltpu.make_async_copy(piece, out, own_sem.at[at]).start())
        for at, turn, device, slot, piece, frm, here in todo:
            out = outs[at].at[slot]
            when(
                jnp.logical_not(here),
                lambda: remote(
                    piece, out, send_sem.at[at, turn], recv_sem.at[at, slot], device
                ).wait_send(),
            )
            when(here, lambda: pltpu.make_async_copy(piece, out, own_sem.at[at]).wait())
        for at in range(count):
            for slot in range(4):
                if kind in ("mp", "mp_split"):
                    self_slot = mp == slot
                elif kind == "to_work":
                    self_slot = jnp.logical_and(mp // 2 == core, mp == slot)
                else:
                    self_slot = jnp.logical_and(
                        2 * core + slot // 2 == mp, slot % 2 == core
                    )
                out = outs[at].at[slot]
                piece = ins[at] if kind in ("mp", "from_work") else ins[at].at[0]
                when(
                    jnp.logical_not(self_slot),
                    lambda: remote(
                        piece, out, send_sem.at[at, 0], recv_sem.at[at, slot], (dp, mp)
                    ).wait_recv(),
                )

    shapes = tuple(
        jax.ShapeDtypeStruct(
            (4,) + (a.shape if kind in ("mp", "from_work") else a.shape[1:]), a.dtype
        )
        for a in arrays
    )
    return pl.pallas_call(
        kernel,
        out_shape=shapes,
        in_specs=[ANY] * count,
        out_specs=[ANY] * count,
        scratch_shapes=[DMA((count,)), DMA((count, 4)), DMA((count, 4))],
        compiler_params=pltpu.CompilerParams(collective_id=collective_id, has_side_effects=True),
        name="exchange_" + kind,
    )(*arrays)


def work_moves(line):
    pairs = []
    for dp in range(2 * line):
        for mp in range(4):
            z, core = dp // 2, dp % 2
            pairs.append((dp * 4 + mp, (2 * z + mp % 2) * 4 + 2 * core + mp // 2))
    return pairs


def sibling(value, line):
    pairs = [(dp * 4 + mp, (dp ^ 1) * 4 + mp) for dp in range(2 * line) for mp in range(4)]
    return lax.ppermute(value, ("dp", "mp"), pairs)


def fast_shards(
    latents,
    pixels,
    pixel_counts,
    cross_query,
    cross_key,
    cross_value,
    cross_out,
    cross_up,
    cross_down,
    block_qkv,
    block_out,
    block_up,
    block_down,
    norm_gains,
    norm_biases,
    pixel_gain,
    pixel_bias,
    cotangent,
):
    bf16, f32 = jnp.bfloat16, jnp.float32
    line = lax.axis_size("dp") // 2
    layers, rows_d, _, cols_m = block_qkv.shape
    own_rows, width = latents.shape
    items, slots, channels = pixels.shape
    own_cols = cross_query.shape[1]
    scale = 1.0 / math.sqrt(width)
    moves = work_moves(line)
    back_moves = [(b, a) for a, b in moves]
    both_axes = ("dp", "mp")
    work_latents = lax.ppermute(latents, both_axes, moves)
    work_cotangent = lax.ppermute(cotangent, both_axes, moves)

    pad = (-channels) % 128
    wide = channels + pad

    def lanes(v):
        return jnp.pad(v, ((0, 0), (0, pad)))

    norms = jnp.concatenate([norm_gains, norm_biases], axis=0)
    norm_count = norm_gains.shape[0]
    slab_q = jnp.concatenate(
        [
            cross_query.T,
            lanes(cross_key.T),
            lanes(cross_value.T),
            jnp.pad(norms.T, ((0, 0), (0, 128 - 2 * norm_count))),
        ],
        axis=1,
    )
    slab_c = jnp.concatenate([cross_up.T, cross_down.T, cross_out.T], axis=0)
    slabs_l = [
        jnp.concatenate(
            [
                block_qkv[l].reshape(rows_d, 3 * cols_m),
                block_out[l],
                block_up[l],
                block_down[l],
            ],
            axis=1,
        )
        for l in range(layers)
    ]
    gathered = gather_all(
        [slab_q, slab_c] + slabs_l, [False, False] + [True] * layers, line
    )
    all_q = gathered[0].reshape(width, -1)
    all_c = gathered[1].reshape(-1, 3, own_cols, width)
    query_t = all_q[:, :width]
    key_t = all_q[:, width : width + channels]
    value_t = all_q[:, width + wide : width + wide + channels]
    norm_rows = all_q[:, width + 2 * wide : width + 2 * wide + 2 * norm_count].T.astype(f32)
    gain_rows, bias_rows = norm_rows[:norm_count], norm_rows[norm_count:]
    up_t = all_c[:, 0].reshape(-1, width)
    down_t = all_c[:, 1].reshape(-1, width)
    out_t = all_c[:, 2].reshape(-1, width)
    layer_w = [g.reshape(4, width, 6 * cols_m) for g in gathered[2:]]

    start_rows = latents.astype(f32)
    query_in = layer_norm(start_rows, gain_rows[0], bias_rows[0]).astype(bf16)
    queries = times_transposed(query_in, query_t).astype(bf16)
    qk = (matmul(queries, key_t) * scale).astype(bf16)
    (qk_all,) = exchange([lanes(qk)], "mp", 2)
    half_rows = own_rows
    qk_all = qk_all.reshape(items, 2 * half_rows, wide)[:, :, :channels]
    pixel_floats = pixels.astype(f32)
    pixel_gain_row = pixel_gain.astype(f32)
    pixel_bias_row = pixel_bias.astype(f32)
    pixel_in = layer_norm(pixel_floats, pixel_gain_row, pixel_bias_row).astype(bf16)
    positions = lax.axis_index("mp") * slots + jnp.arange(slots, dtype=jnp.int32)
    present = positions[None, :] < pixel_counts[:, None]

    def cross_scores():
        raw = jnp.einsum("iqc,ipc->iqp", qk_all, pixel_in, preferred_element_type=f32)
        return jnp.where(present[:, None, :], raw, masked_score)

    scores = cross_scores()
    local_top = jnp.max(scores, axis=-1)
    lifted = jnp.exp(scores - local_top[:, :, None]) * present.astype(f32)[:, None, :]
    local_total = jnp.sum(lifted, axis=-1)
    taken = jnp.einsum("iqp,ipc->iqc", lifted.astype(bf16), pixel_in, preferred_element_type=f32)
    taken = jnp.pad(taken.astype(bf16), ((0, 0), (0, 0), (0, pad)))
    stats = jnp.stack([local_top, local_total], axis=1).reshape(items, 2, 2, half_rows)
    stats = jnp.pad(jnp.swapaxes(stats, 1, 2).reshape(4, 2, half_rows), ((0, 0), (0, 6), (0, 0)))
    taken_parts, stat_parts = exchange(
        [taken.reshape(4, half_rows, wide), stats], "to_work", 3
    )
    tops, totals = stat_parts[:, 0], stat_parts[:, 1]
    top = jnp.max(tops, axis=0)
    shares = jnp.exp(tops - top[None])
    total = jnp.sum(shares * totals, axis=0)
    log_total = top + jnp.log(total)
    px = jnp.sum(taken_parts.astype(f32) * shares[:, :, None], axis=0) / total[:, None]
    px = px[:, :channels]
    px_low = px.astype(bf16)
    context_own = times_transposed(px_low, value_t).astype(bf16)
    base_rows = work_latents.astype(f32)
    after_cross = base_rows + times_transposed(context_own, out_t)
    cross_hidden_in = layer_norm(after_cross, gain_rows[1], bias_rows[1]).astype(bf16)
    cross_hidden = times_transposed(cross_hidden_in, up_t)
    cross_active = jax.nn.gelu(cross_hidden).astype(bf16)
    current = after_cross + times_transposed(cross_active, down_t)

    heads = cols_m // HD
    block_scale = 1.0 / math.sqrt(HD)

    def split_heads(v):
        return v.reshape(4, -1, heads, HD)

    saved = []
    for l in range(layers):
        w = layer_w[l]
        w_qkv, w_out, w_up, w_down = (
            w[:, :, : 3 * cols_m],
            w[:, :, 3 * cols_m : 4 * cols_m],
            w[:, :, 4 * cols_m : 5 * cols_m],
            w[:, :, 5 * cols_m :],
        )
        normed = layer_norm(current, gain_rows[2 + 2 * l], bias_rows[2 + 2 * l]).astype(bf16)
        qkv = jnp.einsum("rd,mdk->mrk", normed, w_qkv, preferred_element_type=f32).astype(bf16)
        queries_h = split_heads(qkv[:, :, :cols_m])
        kv = qkv[:, :, cols_m:]
        kv_all = jnp.concatenate([kv, sibling(kv, line)], axis=1)
        keys_h = split_heads(kv_all[:, :, :cols_m])
        values_h = split_heads(kv_all[:, :, cols_m:])
        raw = (
            jnp.einsum("mqhe,mkhe->mhqk", queries_h, keys_h, preferred_element_type=f32)
            * block_scale
        )
        row_top = jnp.max(raw, axis=-1, keepdims=True)
        lifted_h = jnp.exp(raw - row_top)
        row_total = jnp.sum(lifted_h, axis=-1, keepdims=True)
        attention = lifted_h / row_total
        log_h = row_top + jnp.log(row_total)
        context = jnp.einsum(
            "mhqk,mkhe->mqhe", attention.astype(bf16), values_h, preferred_element_type=f32
        )
        context = context.astype(bf16).reshape(4, own_rows, cols_m)
        middle = current + jnp.einsum("mrk,mdk->rd", context, w_out, preferred_element_type=f32)
        hidden_in = layer_norm(middle, gain_rows[3 + 2 * l], bias_rows[3 + 2 * l]).astype(bf16)
        hidden = jnp.einsum("rd,mdf->mrf", hidden_in, w_up, preferred_element_type=f32)
        active = jax.nn.gelu(hidden).astype(bf16)
        result = middle + jnp.einsum("mrf,mdf->rd", active, w_down, preferred_element_type=f32)
        saved.append(
            (
                w_qkv,
                w_out,
                w_up,
                w_down,
                current,
                normed,
                queries_h,
                keys_h,
                values_h,
                log_h,
                context,
                middle,
                hidden_in,
                hidden,
                active,
            )
        )
        current = result
    latents_out = lax.ppermute(current.astype(bf16), both_axes, back_moves)

    gain_parts = [None] * norm_count
    bias_parts = [None] * norm_count
    layer_parts = [None] * layers
    current_cot = work_cotangent.astype(f32)
    for l in reversed(range(layers)):
        (
            w_qkv,
            w_out,
            w_up,
            w_down,
            current,
            normed,
            queries_h,
            keys_h,
            values_h,
            log_h,
            context,
            middle,
            hidden_in,
            hidden,
            active,
        ) = saved[l]
        down_cot = current_cot.astype(bf16)
        down_grad = jnp.einsum("rd,mrf->mdf", down_cot, active, preferred_element_type=f32)
        active_cot = jnp.einsum("rd,mdf->mrf", down_cot, w_down, preferred_element_type=f32)
        hidden_cot = gelu_back(hidden, active_cot).astype(bf16)
        up_grad = jnp.einsum("rd,mrf->mdf", hidden_in, hidden_cot, preferred_element_type=f32)
        hidden_in_cot = jnp.einsum("mrf,mdf->rd", hidden_cot, w_up, preferred_element_type=f32)
        middle_cot, gain_parts[3 + 2 * l], bias_parts[3 + 2 * l] = norm_back(
            middle, gain_rows[3 + 2 * l], bias_rows[3 + 2 * l], hidden_in_cot
        )
        middle_cot = middle_cot + current_cot
        out_cot = middle_cot.astype(bf16)
        out_grad = jnp.einsum("rd,mrk->mdk", out_cot, context, preferred_element_type=f32)
        context_cot = split_heads(
            jnp.einsum("rd,mdk->mrk", out_cot, w_out, preferred_element_type=f32).astype(bf16)
        )
        raw = (
            jnp.einsum("mqhe,mkhe->mhqk", queries_h, keys_h, preferred_element_type=f32)
            * block_scale
        )
        attention = jnp.exp(raw - log_h)
        value_cot = jnp.einsum(
            "mhqk,mqhe->mkhe", attention.astype(bf16), context_cot, preferred_element_type=f32
        )
        prob_cot = jnp.einsum(
            "mqhe,mkhe->mhqk", context_cot, values_h, preferred_element_type=f32
        )
        row_terms = jnp.sum(attention * prob_cot, axis=-1, keepdims=True)
        score_cot = (attention * (prob_cot - row_terms) * block_scale).astype(bf16)
        query_cot = jnp.einsum("mhqk,mkhe->mqhe", score_cot, keys_h, preferred_element_type=f32)
        key_cot = jnp.einsum("mhqk,mqhe->mkhe", score_cot, queries_h, preferred_element_type=f32)
        kv_cot = jnp.concatenate(
            [
                key_cot.reshape(4, 2 * own_rows, cols_m),
                value_cot.reshape(4, 2 * own_rows, cols_m),
            ],
            axis=2,
        )
        theirs = sibling(kv_cot[:, own_rows:].astype(bf16), line)
        kv_cot = (kv_cot[:, :own_rows] + theirs.astype(f32)).astype(bf16)
        qkv_cot = jnp.concatenate(
            [query_cot.astype(bf16).reshape(4, own_rows, cols_m), kv_cot], axis=2
        )
        qkv_grad = jnp.einsum("rd,mrk->mdk", normed, qkv_cot, preferred_element_type=f32)
        normed_cot = jnp.einsum("mrk,mdk->rd", qkv_cot, w_qkv, preferred_element_type=f32)
        input_cot, gain_parts[2 + 2 * l], bias_parts[2 + 2 * l] = norm_back(
            current, gain_rows[2 + 2 * l], bias_rows[2 + 2 * l], normed_cot
        )
        current_cot = input_cot + middle_cot
        layer_parts[l] = jnp.concatenate(
            [g.astype(bf16) for g in (qkv_grad, out_grad, up_grad, down_grad)], axis=2
        ).reshape(4, 2 * line, rows_d, 6 * cols_m)
    down_in = current_cot.astype(bf16)
    down_grad_t = transposed_times(down_in, cross_active)
    active_cot = matmul(down_in, down_t)
    hidden_cot = gelu_back(cross_hidden, active_cot).astype(bf16)
    up_grad_t = transposed_times(hidden_cot, cross_hidden_in)
    hidden_in_cot = matmul(hidden_cot, up_t)
    after_cot, gain_parts[1], bias_parts[1] = norm_back(
        after_cross, gain_rows[1], bias_rows[1], hidden_in_cot
    )
    after_cot = after_cot + current_cot
    out_in = after_cot.astype(bf16)
    cross_part = jnp.concatenate(
        [
            up_grad_t.astype(bf16).reshape(-1, own_cols, width),
            down_grad_t.astype(bf16).reshape(-1, own_cols, width),
        ],
        axis=1,
    ).reshape(2 * line, 4, 2 * own_cols, width)
    reduced = reduce_all(
        [layer_parts[l] for l in reversed(range(layers))] + [cross_part],
        [True] * layers + [False],
        line,
    )

    k_part = transposed_times(out_in, px_low).astype(bf16)
    k_all = lax.psum(k_part, both_axes)
    context_cot = matmul(out_in, out_t).astype(bf16)
    cv = matmul(context_cot, value_t).astype(bf16)
    delta = jnp.sum(cv.astype(f32) * px, axis=1)
    rows_sent = jnp.pad(jnp.stack([log_total, delta], axis=0), ((0, 6), (0, 0)))
    cv_all, rows_all = exchange([lanes(cv), rows_sent], "from_work", 4)
    after_home = lax.ppermute(out_in, both_axes, back_moves)
    cv_all = cv_all.reshape(items, 2 * half_rows, wide)[:, :, :channels]
    log_all = rows_all[:, 0].reshape(items, 2 * half_rows)[:, :, None]
    delta_all = rows_all[:, 1].reshape(items, 2 * half_rows)[:, :, None]
    attention = jnp.exp(cross_scores() - log_all) * present.astype(f32)[:, None, :]
    prob_cot = jnp.einsum("iqc,ipc->iqp", cv_all, pixel_in, preferred_element_type=f32)
    score_cot = (attention * (prob_cot - delta_all)).astype(bf16)
    dsx = jnp.einsum("iqp,ipc->iqc", score_cot, pixel_in, preferred_element_type=f32)
    dsx = jnp.pad((dsx * scale).astype(bf16), ((0, 0), (0, 0), (0, pad)))
    (dsx_parts,) = exchange([dsx.reshape(4, half_rows, wide)], "mp_split", 5)
    dsx_own = jnp.sum(dsx_parts.astype(f32), axis=0)[:, :channels].astype(bf16)
    pixel_in_cot = jnp.einsum(
        "iqp,iqc->ipc", score_cot, qk_all, preferred_element_type=f32
    ) + jnp.einsum("iqp,iqc->ipc", attention.astype(bf16), cv_all, preferred_element_type=f32)
    pixel_cot, pixel_gain_part, pixel_bias_part = norm_back(
        pixel_floats, pixel_gain_row, pixel_bias_row, pixel_in_cot
    )
    pixel_grad = pixel_cot.astype(bf16)
    query_cot = times_transposed(dsx_own, key_t).astype(bf16)
    query_in_cot = matmul(query_cot, query_t)
    start_cot, gain_parts[0], bias_parts[0] = norm_back(
        start_rows, gain_rows[0], bias_rows[0], query_in_cot
    )
    latent_grad = (start_cot + after_home.astype(f32)).astype(bf16)
    g_part = transposed_times(query_in, dsx_own).astype(bf16)
    g_all, small = lax.psum(
        (
            g_part,
            (
                jnp.stack(gain_parts, axis=0),
                jnp.stack(bias_parts, axis=0),
                pixel_gain_part,
                pixel_bias_part,
            ),
        ),
        both_axes,
    )
    cross_query_grad = matmul(g_all, cross_key)
    cross_key_grad = transposed_times(g_all, cross_query)
    at = (lax.axis_index("dp") * 4 + lax.axis_index("mp")) * own_cols
    k_own = lax.dynamic_slice_in_dim(k_all, at, own_cols, 0)
    cross_out_grad = lax.dot_general(
        value_t, k_own, (((1,), (1,)), ((), ())), preferred_element_type=f32
    )
    out_own = lax.dynamic_slice_in_dim(out_t, at, own_cols, 1)
    cross_value_grad = transposed_times(k_all, out_own)
    gain_grad = lax.dynamic_slice_in_dim(small[0], at, own_cols, 1)
    bias_grad = lax.dynamic_slice_in_dim(small[1], at, own_cols, 1)
    layer_grads = [reduced[layers - 1 - l] for l in range(layers)]
    qkv_out = jnp.stack(
        [g[:, : 3 * cols_m].reshape(rows_d, 3, cols_m) for g in layer_grads], axis=0
    )
    out_out, up_out, down_out = [
        jnp.stack([g[:, k * cols_m : (k + 1) * cols_m] for g in layer_grads], axis=0)
        for k in (3, 4, 5)
    ]
    cross_sum = reduced[layers]
    return (
        latents_out,
        latent_grad,
        pixel_grad,
        cross_query_grad,
        cross_key_grad,
        cross_value_grad,
        cross_out_grad,
        cross_sum[:own_cols].T,
        cross_sum[own_cols:].T,
        qkv_out,
        out_out,
        up_out,
        down_out,
        gain_grad,
        bias_grad,
        small[2],
        small[3],
    )


def fits(mesh):
    return mesh.shape["mp"] == 4 and mesh.shape["dp"] % 2 == 0


def solution(mesh):
    return jax.shard_map(
        fast_shards if fits(mesh) else shards,
        mesh=mesh,
        in_specs=(
            P(("dp", "mp"), None),
            P("dp", "mp", None),
            P("dp"),
            P(None, ("dp", "mp")),
            P(None, ("dp", "mp")),
            P(None, ("dp", "mp")),
            P(None, ("dp", "mp")),
            P(None, ("dp", "mp")),
            P(None, ("dp", "mp")),
            P(None, "dp", None, "mp"),
            P(None, "dp", "mp"),
            P(None, "dp", "mp"),
            P(None, "dp", "mp"),
            P(None, ("dp", "mp")),
            P(None, ("dp", "mp")),
            P(),
            P(),
            P(("dp", "mp"), None),
        ),
        out_specs=(
            P(("dp", "mp"), None),
            P(("dp", "mp"), None),
            P("dp", "mp", None),
            P(None, ("dp", "mp")),
            P(None, ("dp", "mp")),
            P(None, ("dp", "mp")),
            P(None, ("dp", "mp")),
            P(None, ("dp", "mp")),
            P(None, ("dp", "mp")),
            P(None, "dp", None, "mp"),
            P(None, "dp", "mp"),
            P(None, "dp", "mp"),
            P(None, "dp", "mp"),
            P(None, ("dp", "mp")),
            P(None, ("dp", "mp")),
            P(),
            P(),
        ),
        check_vma=False,
    )
```

```python
import functools
import math
import types

import ml_dtypes

import jax
import jax.numpy as jnp
from jax import lax
from jax.experimental import pallas as pl
from jax.experimental.pallas import tpu as pltpu
from jax.sharding import PartitionSpec as P

HD = 128


norm_eps = 1e-05
masked_score = -1e30


def joined(value, axis, join):
    pieces = jax.tree.map(lambda part: lax.all_gather(part, axis), value)
    head = jax.tree.map(lambda part: part[0], pieces)
    tail = jax.tree.map(lambda part: part[1:], pieces)
    running, _ = lax.scan(lambda running, share: (join(running, share), None), head, tail)
    return running


def layer_norm(features, gain_row, offset):
    average = jnp.mean(features, axis=-1, keepdims=True)
    centered = features - average
    variance = jnp.mean(centered * centered, axis=-1, keepdims=True)
    return centered * lax.rsqrt(variance + norm_eps) * gain_row + offset


def norm_back(features, gain_row, offset, upstream):
    _, pullback = jax.vjp(layer_norm, features, gain_row, offset)
    return pullback(upstream)


def gelu_back(hidden, upstream):
    _, pullback = jax.vjp(jax.nn.gelu, hidden)
    return pullback(upstream)[0]


def matmul(left_side, right_side):
    return jnp.dot(left_side, right_side, preferred_element_type=jnp.float32)


def times_transposed(left_side, right_side):
    return lax.dot_general(
        left_side, right_side, (((1,), (1,)), ((), ())), preferred_element_type=jnp.float32
    )


def transposed_times(left_side, right_side):
    return lax.dot_general(
        left_side, right_side, (((0,), (0,)), ((), ())), preferred_element_type=jnp.float32
    )


def gather_rows(payload):
    return lax.all_gather(payload, "mp", axis=0, tiled=True)


def gather_grads(payload):
    return lax.all_gather(payload, "mp", axis=0, tiled=True)


def sum_branch(row_term, own_rows):
    return lax.psum_scatter(
        row_term(jnp.int32(0), own_rows * lax.axis_size("mp")).astype(jnp.bfloat16),
        "mp",
        scatter_dimension=0,
        tiled=True,
    ).astype(jnp.float32)


def sum_inputs(row_term, own_rows):
    return lax.psum_scatter(
        row_term(jnp.int32(0), own_rows * lax.axis_size("mp")).astype(jnp.bfloat16),
        "mp",
        scatter_dimension=0,
        tiled=True,
    ).astype(jnp.float32)


def slicer(source):

    def row_term(first_row, row_count):
        return source

    return row_term


def product_term(source, weight, formula):

    def row_term(first_row, row_count):
        return jnp.einsum(formula, source, weight, preferred_element_type=jnp.float32)

    return row_term


def merge_stats(earlier, latter):
    row_top = jnp.maximum(earlier[0], latter[0])
    return (
        row_top,
        earlier[1] * jnp.exp(earlier[0] - row_top) + latter[1] * jnp.exp(latter[0] - row_top),
    )


def cross_params(
    cross_query, cross_key, cross_value, cross_out, cross_up, cross_down, norm_gains, norm_biases
):
    return (
        lax.all_gather(cross_query, ("dp", "mp"), axis=1, tiled=True),
        lax.all_gather(cross_key, ("dp", "mp"), axis=1, tiled=True),
        lax.all_gather(cross_value, ("dp", "mp"), axis=1, tiled=True),
        lax.all_gather(cross_out, ("dp", "mp"), axis=1, tiled=True),
        lax.all_gather(cross_up, ("dp", "mp"), axis=1, tiled=True),
        lax.all_gather(cross_down, ("dp", "mp"), axis=1, tiled=True),
        lax.all_gather(norm_gains, ("dp", "mp"), axis=1, tiled=True),
        lax.all_gather(norm_biases, ("dp", "mp"), axis=1, tiled=True),
    )


def block_weights(block_qkv, block_out, block_up, block_down, layer_index):
    return (
        lax.all_gather(block_qkv[layer_index], "dp", axis=0, tiled=True),
        lax.all_gather(block_out[layer_index], "dp", axis=0, tiled=True),
        lax.all_gather(block_up[layer_index], "dp", axis=0, tiled=True),
        lax.all_gather(block_down[layer_index], "dp", axis=0, tiled=True),
    )


def block_forward(current, layer_index, gain_rows, bias_rows, block_params, item_count):
    qkv_weight, out_weight, up_weight, down_weight = block_weights(
        block_params[0], block_params[1], block_params[2], block_params[3], layer_index
    )
    own_rows = current.shape[0]
    group_rows = own_rows * lax.axis_size("mp")
    latents_item = group_rows // item_count
    head_cols = qkv_weight.shape[2]
    heads_local = head_cols // HD
    block_scale = 1.0 / math.sqrt(HD)
    normed = layer_norm(
        current, gain_rows[2 + 2 * layer_index], bias_rows[2 + 2 * layer_index]
    ).astype(jnp.bfloat16)
    normed_group = gather_rows(normed)
    projected = jnp.einsum(
        "rd,dtk->rtk", normed_group, qkv_weight, preferred_element_type=jnp.float32
    ).astype(jnp.bfloat16)
    heads_view = projected.reshape(item_count, latents_item, 3, heads_local, HD)
    raw_scores = (
        jnp.einsum(
            "iqhe,ikhe->ihqk",
            heads_view[:, :, 0],
            heads_view[:, :, 1],
            preferred_element_type=jnp.float32,
        )
        * block_scale
    )
    row_top = jnp.max(raw_scores, axis=-1, keepdims=True)
    lifted = jnp.exp(raw_scores - row_top)
    row_total = jnp.sum(lifted, axis=-1, keepdims=True)
    attention = lifted / row_total
    log_total = row_top + jnp.log(row_total)
    context = jnp.einsum(
        "ihqk,ikhe->iqhe",
        attention.astype(jnp.bfloat16),
        heads_view[:, :, 2],
        preferred_element_type=jnp.float32,
    )
    context = context.astype(jnp.bfloat16).reshape(group_rows, head_cols)
    middle = current + sum_branch(product_term(context, out_weight, "rk,dk->rd"), own_rows)
    hidden_in = layer_norm(
        middle, gain_rows[3 + 2 * layer_index], bias_rows[3 + 2 * layer_index]
    ).astype(jnp.bfloat16)
    hidden_group = gather_rows(hidden_in)
    hidden = matmul(hidden_group, up_weight)
    active = jax.nn.gelu(hidden).astype(jnp.bfloat16)
    result = middle + sum_branch(product_term(active, down_weight, "rf,df->rd"), own_rows)
    stored = (
        qkv_weight,
        out_weight,
        up_weight,
        down_weight,
        normed_group,
        projected,
        log_total,
        context,
        middle,
        hidden_group,
        hidden,
        active,
    )
    return (result, stored)


def block_backward(upstream, current, layer_index, gain_rows, bias_rows, stored, item_count):
    (
        qkv_weight,
        out_weight,
        up_weight,
        down_weight,
        normed_group,
        projected,
        log_total,
        context,
        middle,
        hidden_group,
        hidden,
        active,
    ) = stored
    own_rows = upstream.shape[0]
    group_rows = own_rows * lax.axis_size("mp")
    latents_item = group_rows // item_count
    head_cols = qkv_weight.shape[2]
    heads_local = head_cols // HD
    block_scale = 1.0 / math.sqrt(HD)
    down_group = gather_grads(upstream.astype(jnp.bfloat16))
    down_grad = transposed_times(down_group, active)
    active_cot = matmul(down_group, down_weight)
    hidden_cot = gelu_back(hidden, active_cot).astype(jnp.bfloat16)
    up_grad = transposed_times(hidden_group, hidden_cot)
    hidden_in_cot = sum_inputs(product_term(hidden_cot, up_weight, "rf,df->rd"), own_rows)
    middle_cot, gain_late, bias_late = norm_back(
        middle, gain_rows[3 + 2 * layer_index], bias_rows[3 + 2 * layer_index], hidden_in_cot
    )
    middle_cot = middle_cot + upstream
    out_group = gather_grads(middle_cot.astype(jnp.bfloat16))
    out_grad = transposed_times(out_group, context)
    context_cot = (
        matmul(out_group, out_weight)
        .astype(jnp.bfloat16)
        .reshape(item_count, latents_item, heads_local, HD)
    )
    heads_view = projected.reshape(item_count, latents_item, 3, heads_local, HD)
    queries = heads_view[:, :, 0]
    key_rows = heads_view[:, :, 1]
    value_rows = heads_view[:, :, 2]
    raw_scores = (
        jnp.einsum("iqhe,ikhe->ihqk", queries, key_rows, preferred_element_type=jnp.float32)
        * block_scale
    )
    attention = jnp.exp(raw_scores - log_total)
    value_cot = jnp.einsum(
        "ihqk,iqhe->ikhe",
        attention.astype(jnp.bfloat16),
        context_cot,
        preferred_element_type=jnp.float32,
    )
    prob_cot = jnp.einsum(
        "iqhe,ikhe->ihqk", context_cot, value_rows, preferred_element_type=jnp.float32
    )
    row_terms = jnp.sum(attention * prob_cot, axis=-1, keepdims=True)
    score_cot = (attention * (prob_cot - row_terms) * block_scale).astype(jnp.bfloat16)
    query_cot = jnp.einsum(
        "ihqk,ikhe->iqhe", score_cot, key_rows, preferred_element_type=jnp.float32
    )
    key_cot = jnp.einsum("ihqk,iqhe->ikhe", score_cot, queries, preferred_element_type=jnp.float32)
    projected_cot = jnp.stack(
        [
            query_cot.astype(jnp.bfloat16),
            key_cot.astype(jnp.bfloat16),
            value_cot.astype(jnp.bfloat16),
        ],
        axis=2,
    )
    projected_cot = projected_cot.reshape(group_rows, 3, head_cols)
    qkv_grad = jnp.einsum(
        "rd,rtk->dtk", normed_group, projected_cot, preferred_element_type=jnp.float32
    )
    normed_cot = sum_inputs(product_term(projected_cot, qkv_weight, "rtk,dtk->rd"), own_rows)
    input_cot, gain_early, bias_early = norm_back(
        current, gain_rows[2 + 2 * layer_index], bias_rows[2 + 2 * layer_index], normed_cot
    )
    input_cot = input_cot + middle_cot
    summed = (
        lax.psum_scatter(
            qkv_grad.astype(jnp.bfloat16), "dp", scatter_dimension=0, tiled=True
        ).astype(jnp.float32),
        lax.psum_scatter(
            out_grad.astype(jnp.bfloat16), "dp", scatter_dimension=0, tiled=True
        ).astype(jnp.float32),
        lax.psum_scatter(
            up_grad.astype(jnp.bfloat16), "dp", scatter_dimension=0, tiled=True
        ).astype(jnp.float32),
        lax.psum_scatter(
            down_grad.astype(jnp.bfloat16), "dp", scatter_dimension=0, tiled=True
        ).astype(jnp.float32),
    )
    return (input_cot, summed, (gain_early, bias_early, gain_late, bias_late))


def shards(
    latents,
    pixels,
    pixel_counts,
    cross_query,
    cross_key,
    cross_value,
    cross_out,
    cross_up,
    cross_down,
    block_qkv,
    block_out,
    block_up,
    block_down,
    norm_gains,
    norm_biases,
    pixel_gain,
    pixel_bias,
    cotangent,
):
    layers = block_qkv.shape[0]
    item_count = pixels.shape[0]
    pixel_rows = pixels.shape[1]
    own_rows = latents.shape[0]
    model_width = latents.shape[1]
    group_rows = own_rows * lax.axis_size("mp")
    latents_item = group_rows // item_count
    cross_scale = 1.0 / math.sqrt(model_width)
    block_params = (block_qkv, block_out, block_up, block_down)
    forward_params = cross_params(
        cross_query,
        cross_key,
        cross_value,
        cross_out,
        cross_up,
        cross_down,
        norm_gains,
        norm_biases,
    )
    (
        query_weight,
        key_weight,
        value_weight,
        out_weight,
        up_weight,
        down_weight,
        gain_table,
        bias_table,
    ) = forward_params
    gain_rows = gain_table.astype(jnp.float32)
    bias_rows = bias_table.astype(jnp.float32)
    start_rows = latents.astype(jnp.float32)
    query_in = layer_norm(start_rows, gain_rows[0], bias_rows[0]).astype(jnp.bfloat16)
    query_own = matmul(query_in, query_weight).astype(jnp.bfloat16)
    query_group = gather_rows(query_own).reshape(item_count, latents_item, model_width)
    pixel_floats = pixels.astype(jnp.float32)
    pixel_gain_row = pixel_gain.astype(jnp.float32)
    pixel_bias_row = pixel_bias.astype(jnp.float32)
    pixel_in = layer_norm(pixel_floats, pixel_gain_row, pixel_bias_row).astype(jnp.bfloat16)
    pair_weight = jnp.concatenate([key_weight, value_weight], axis=1)
    pair_rows = jnp.einsum(
        "ipc,cd->ipd", pixel_in, pair_weight, preferred_element_type=jnp.float32
    ).astype(jnp.bfloat16)
    key_rows = pair_rows[:, :, :model_width]
    value_rows = pair_rows[:, :, model_width:]
    positions = lax.axis_index("mp") * pixel_rows + jnp.arange(pixel_rows, dtype=jnp.int32)
    present = positions[None, :] < pixel_counts[:, None]
    present_mask = present.astype(jnp.float32)[:, None, :]

    def cross_scores():
        raw_scores = (
            jnp.einsum("iqd,ipd->iqp", query_group, key_rows, preferred_element_type=jnp.float32)
            * cross_scale
        )
        return jnp.where(present[:, None, :], raw_scores, masked_score)

    scores = cross_scores()
    local_top = jnp.max(scores, axis=-1)
    local_total = jnp.sum(jnp.exp(scores - local_top[:, :, None]) * present_mask, axis=-1)
    group_top, group_total = joined((local_top, local_total), "mp", merge_stats)
    log_total = (group_top + jnp.log(group_total))[:, :, None]
    attention = jnp.exp(scores - log_total) * present_mask
    attended = jnp.einsum(
        "iqp,ipd->iqd",
        attention.astype(jnp.bfloat16),
        value_rows,
        preferred_element_type=jnp.float32,
    )
    attended = attended.reshape(group_rows, model_width)
    context_own = sum_branch(slicer(attended), own_rows).astype(jnp.bfloat16)
    after_cross = start_rows + matmul(context_own, out_weight)
    cross_hidden_in = layer_norm(after_cross, gain_rows[1], bias_rows[1]).astype(jnp.bfloat16)
    cross_hidden = matmul(cross_hidden_in, up_weight)
    cross_active = jax.nn.gelu(cross_hidden).astype(jnp.bfloat16)
    current = after_cross + matmul(cross_active, down_weight)
    inputs_kept = []
    stored_all = []
    for layer_index in range(layers):
        inputs_kept.append(current)
        current, stored = block_forward(
            current, layer_index, gain_rows, bias_rows, block_params, item_count
        )
        stored_all.append(stored)
    latents_out = current.astype(jnp.bfloat16)
    later_params = cross_params(
        cross_query,
        cross_key,
        cross_value,
        cross_out,
        cross_up,
        cross_down,
        norm_gains,
        norm_biases,
    )
    (
        query_weight,
        key_weight,
        value_weight,
        out_weight,
        up_weight,
        down_weight,
        gain_table,
        bias_table,
    ) = later_params
    gain_rows = gain_table.astype(jnp.float32)
    bias_rows = bias_table.astype(jnp.float32)
    gain_parts = [None] * (2 * layers + 2)
    bias_parts = [None] * (2 * layers + 2)
    qkv_grads = [None] * layers
    out_grads = [None] * layers
    up_grads = [None] * layers
    down_grads = [None] * layers
    current_cot = cotangent.astype(jnp.float32)
    for layer_index in reversed(range(layers)):
        _, stored = block_forward(
            inputs_kept[layer_index], layer_index, gain_rows, bias_rows, block_params, item_count
        )
        current_cot, summed, norm_parts = block_backward(
            current_cot,
            inputs_kept[layer_index],
            layer_index,
            gain_rows,
            bias_rows,
            stored,
            item_count,
        )
        qkv_grads[layer_index] = summed[0]
        out_grads[layer_index] = summed[1]
        up_grads[layer_index] = summed[2]
        down_grads[layer_index] = summed[3]
        gain_parts[2 + 2 * layer_index] = norm_parts[0]
        bias_parts[2 + 2 * layer_index] = norm_parts[1]
        gain_parts[3 + 2 * layer_index] = norm_parts[2]
        bias_parts[3 + 2 * layer_index] = norm_parts[3]
    down_in = current_cot.astype(jnp.bfloat16)
    cross_down_grad = transposed_times(cross_active, down_in)
    active_cot = times_transposed(down_in, down_weight)
    hidden_cot = gelu_back(cross_hidden, active_cot).astype(jnp.bfloat16)
    cross_up_grad = transposed_times(cross_hidden_in, hidden_cot)
    hidden_in_cot = times_transposed(hidden_cot, up_weight)
    after_cot, gain_parts[1], bias_parts[1] = norm_back(
        after_cross, gain_rows[1], bias_rows[1], hidden_in_cot
    )
    after_cot = after_cot + current_cot
    out_in = after_cot.astype(jnp.bfloat16)
    cross_out_grad = transposed_times(context_own, out_in)
    context_cot = times_transposed(out_in, out_weight).astype(jnp.bfloat16)
    context_group = gather_grads(context_cot).reshape(item_count, latents_item, model_width)
    scores = cross_scores()
    attention = jnp.exp(scores - log_total) * present_mask
    value_cot = jnp.einsum(
        "iqp,iqd->ipd",
        attention.astype(jnp.bfloat16),
        context_group,
        preferred_element_type=jnp.float32,
    ).astype(jnp.bfloat16)
    prob_cot = jnp.einsum(
        "iqd,ipd->iqp", context_group, value_rows, preferred_element_type=jnp.float32
    )
    row_part = jnp.sum(attention * prob_cot, axis=-1)
    row_terms = lax.psum(row_part, "mp")
    score_cot = (attention * (prob_cot - row_terms[:, :, None]) * cross_scale).astype(jnp.bfloat16)
    query_part = jnp.einsum(
        "iqp,ipd->iqd", score_cot, key_rows, preferred_element_type=jnp.float32
    ).reshape(group_rows, model_width)
    query_cot = sum_inputs(slicer(query_part), own_rows).astype(jnp.bfloat16)
    key_cot = jnp.einsum(
        "iqp,iqd->ipd", score_cot, query_group, preferred_element_type=jnp.float32
    ).astype(jnp.bfloat16)
    cross_query_grad = transposed_times(query_in, query_cot)
    query_in_cot = times_transposed(query_cot, query_weight)
    start_cot, gain_parts[0], bias_parts[0] = norm_back(
        start_rows, gain_rows[0], bias_rows[0], query_in_cot
    )
    latent_grad = (start_cot + after_cot).astype(jnp.bfloat16)
    pair_weight = jnp.concatenate([key_weight, value_weight], axis=1)
    pair_cot = jnp.concatenate([key_cot, value_cot], axis=2)
    pair_grad = jnp.einsum("ipc,ipd->cd", pixel_in, pair_cot, preferred_element_type=jnp.float32)
    cross_key_grad = pair_grad[:, :model_width]
    cross_value_grad = pair_grad[:, model_width:]
    pixel_in_cot = jnp.einsum(
        "ipd,cd->ipc", pair_cot, pair_weight, preferred_element_type=jnp.float32
    )
    pixel_cot, pixel_gain_part, pixel_bias_part = norm_back(
        pixel_floats, pixel_gain_row, pixel_bias_row, pixel_in_cot
    )
    pixel_grad = pixel_cot.astype(jnp.bfloat16)
    gain_stack = jnp.stack(gain_parts, axis=0)
    bias_stack = jnp.stack(bias_parts, axis=0)
    cross_summed = (
        lax.psum_scatter(cross_query_grad, ("dp", "mp"), scatter_dimension=1, tiled=True),
        lax.psum_scatter(cross_key_grad, ("dp", "mp"), scatter_dimension=1, tiled=True),
        lax.psum_scatter(cross_value_grad, ("dp", "mp"), scatter_dimension=1, tiled=True),
        lax.psum_scatter(cross_out_grad, ("dp", "mp"), scatter_dimension=1, tiled=True),
        lax.psum_scatter(cross_up_grad, ("dp", "mp"), scatter_dimension=1, tiled=True),
        lax.psum_scatter(cross_down_grad, ("dp", "mp"), scatter_dimension=1, tiled=True),
        lax.psum_scatter(gain_stack, ("dp", "mp"), scatter_dimension=1, tiled=True),
        lax.psum_scatter(bias_stack, ("dp", "mp"), scatter_dimension=1, tiled=True),
    )
    pixel_gain_grad, pixel_bias_grad = lax.psum((pixel_gain_part, pixel_bias_part), ("dp", "mp"))
    return (
        latents_out,
        latent_grad,
        pixel_grad,
        cross_summed[0],
        cross_summed[1],
        cross_summed[2],
        cross_summed[3],
        cross_summed[4],
        cross_summed[5],
        jnp.stack(qkv_grads, axis=0),
        jnp.stack(out_grads, axis=0),
        jnp.stack(up_grads, axis=0),
        jnp.stack(down_grads, axis=0),
        cross_summed[6],
        cross_summed[7],
        pixel_gain_grad,
        pixel_bias_grad,
    )


MESH_ID = pl.DeviceIdType.MESH
ANY = pl.BlockSpec(memory_space=pl.ANY)
DMA = pltpu.SemaphoreType.DMA


def place():
    dp = lax.axis_index("dp")
    mp = lax.axis_index("mp")
    return dp, mp, dp // 2, dp % 2, mp // 2, mp % 2


def greet(targets):
    barrier = pltpu.get_barrier_semaphore()
    for device, condition in targets:

        def signal(device=device):
            pl.semaphore_signal(barrier, inc=1, device_id=device, device_id_type=MESH_ID)

        if condition is None:
            signal()
        else:
            pl.when(condition)(signal)
    fixed = sum(1 for _, condition in targets if condition is None)
    varying = [condition.astype(jnp.int32) for _, condition in targets if condition is not None]
    pl.semaphore_wait(barrier, sum(varying, fixed))


def remote(source, target, send, recv, device):
    return pltpu.make_async_remote_copy(
        src_ref=source,
        dst_ref=target,
        send_sem=send,
        recv_sem=recv,
        device_id=device,
        device_id_type=MESH_ID,
    )


def when(condition, action):
    if condition is None:
        action()
    else:
        pl.when(condition)(action)


def both(first, second):
    if first is None:
        return second
    if second is None:
        return first
    return jnp.logical_and(first, second)


def slab_of(ref, slab, dp, mp):
    rows, columns = slab[-2:]
    if columns == ref.shape[-1]:
        at = pl.ds(pl.multiple_of((dp * 4 + mp) * rows, rows), rows)
        return ref.at[at] if len(ref.shape) == 2 else ref.at[:, at]
    return ref.at[
        :,
        pl.ds(pl.multiple_of(dp * rows, rows), rows),
        pl.ds(pl.multiple_of(mp * columns, columns), columns),
    ]


class Gatherer:
    def __init__(self, line, slabs, outs, sems):
        self.line = line
        self.slabs = slabs
        self.outs = outs
        self.on_unit = None
        (
            self.own_sem,
            self.line_send,
            self.line_recv,
            self.plane_send,
            self.plane_recv,
            self.pass_send,
            self.pass_recv,
            self.core_send,
            self.core_recv,
        ) = sems
        self.dp, self.mp, self.z, self.core, self.y, self.x = place()

    @staticmethod
    def sem_shapes(chunks, line):
        return [
            DMA((chunks,)),
            DMA((chunks, line, 2)),
            DMA((chunks, line)),
            DMA((chunks, line, 2)),
            DMA((chunks, line, 2)),
            DMA((chunks, line, 2)),
            DMA((chunks, line, 2)),
            DMA((chunks, line, 4)),
            DMA((chunks, line, 4)),
        ]

    def partners(self):
        z = self.z
        return [
            ((self.dp + 2, self.mp), z < self.line - 1),
            ((self.dp - 2, self.mp), z > 0),
            ((self.dp, self.mp ^ 1), None),
            ((self.dp, self.mp ^ 2), None),
            ((self.dp ^ 1, self.mp), None),
        ]

    def slot(self, chunk, z, core, mp):
        return slab_of(self.outs[chunk], self.slabs[chunk].shape, 2 * z + core, mp)

    @staticmethod
    def halves(ref):
        rows = ref.shape[-2] // 2
        if len(ref.shape) == 3:
            return ref.at[:, pl.ds(0, rows)], ref.at[:, pl.ds(rows, rows)]
        return ref.at[pl.ds(0, rows)], ref.at[pl.ds(rows, rows)]

    def line_copy(self, chunk, z, way, source=None):
        slot = self.slot(chunk, z, self.core, self.mp)
        step = 2 if way == 0 else -2
        return remote(
            slot if source is None else source,
            slot,
            self.line_send.at[chunk, z, way],
            self.line_recv.at[chunk, z],
            (self.dp + step, self.mp),
        )

    def plane_copy(self, chunk, z, way, source=None):
        slot = self.slot(chunk, z, self.core, self.mp)
        return remote(
            slot if source is None else source,
            slot,
            self.plane_send.at[chunk, z, way],
            self.plane_recv.at[chunk, z, way],
            (self.dp, self.mp ^ (1 if way == 0 else 2)),
        )

    def pass_copy(self, chunk, z, way):
        slot = self.slot(chunk, z, self.core, self.mp ^ (1 if way == 0 else 2))
        half = self.halves(slot)[way]
        return remote(
            half,
            half,
            self.pass_send.at[chunk, z, way],
            self.pass_recv.at[chunk, z, way],
            (self.dp, self.mp ^ (2 if way == 0 else 1)),
        )

    def core_copy(self, chunk, z, mp, turn):
        slot = self.slot(chunk, z, self.core, mp)
        return remote(
            slot,
            slot,
            self.core_send.at[chunk, z, turn],
            self.core_recv.at[chunk, z, turn],
            (self.dp ^ 1, self.mp),
        )

    def arrivals(self):
        z = self.z
        order = [(z, None, None)]
        for distance in range(1, self.line):
            order.append((z - distance, z >= distance, 0))
            order.append((z + distance, z + distance < self.line, 1))
        return order

    def own_copy(self, chunk):
        return pltpu.make_async_copy(
            self.slabs[chunk], self.slot(chunk, self.z, self.core, self.mp), self.own_sem.at[chunk]
        )

    def can_pass(self, way):
        return self.z < self.line - 1 if way == 0 else self.z > 0

    def begin(self, chunk):
        self.own_copy(chunk).start()
        slab = self.slabs[chunk]
        for way in (0, 1):
            when(
                self.can_pass(way),
                lambda way=way: self.line_copy(chunk, self.z, way, slab).start(),
            )
        for way in (0, 1):
            self.plane_copy(chunk, self.z, way, slab).start()

    def stage_line(self, chunk, turn):
        if turn == 0:
            self.begin(chunk)
            return
        z, condition, way = self.arrivals()[turn]

        def act():
            self.line_copy(chunk, z, way).wait_recv()
            when(self.can_pass(way), lambda: self.line_copy(chunk, z, way).start())
            for plane_way in (0, 1):
                self.plane_copy(chunk, z, plane_way).start()

        when(condition, act)

    def stage_plane(self, chunk, turn):
        z, condition, _ = self.arrivals()[turn]

        def act():
            for way in (0, 1):
                self.plane_copy(chunk, z, way).wait_recv()
                self.pass_copy(chunk, z, way).start()
            if turn == 0:
                self.own_copy(chunk).wait()
            self.core_copy(chunk, z, self.mp, 0).start()
            self.core_copy(chunk, z, self.mp ^ 1, 1).start()
            self.core_copy(chunk, z, self.mp ^ 2, 2).start()

        when(condition, act)

    def stage_pass(self, chunk, turn):
        z, condition, _ = self.arrivals()[turn]

        def act():
            for way in (0, 1):
                self.pass_copy(chunk, z, way).wait_recv()
            self.core_copy(chunk, z, self.mp ^ 3, 3).start()

        when(condition, act)

    def stage_core(self, chunk, turn):
        z, condition, _ = self.arrivals()[turn]

        def act():
            for piece in range(4):
                self.core_copy(chunk, z, self.mp, piece).wait_recv()
            if self.on_unit is not None:
                self.on_unit(chunk, z)

        when(condition, act)

    def drain(self, chunk):
        for turn, (z, condition, way) in enumerate(self.arrivals()):

            def act(turn=turn, z=z, way=way):
                if turn == 0:
                    for own_way in (0, 1):
                        when(
                            self.can_pass(own_way),
                            lambda own_way=own_way: self.line_copy(
                                chunk, z, own_way, self.slabs[chunk]
                            ).wait_send(),
                        )
                else:
                    when(self.can_pass(way), lambda: self.line_copy(chunk, z, way).wait_send())
                for plane_way in (0, 1):
                    self.plane_copy(chunk, z, plane_way).wait_send()
                    self.pass_copy(chunk, z, plane_way).wait_send()
                for piece in range(4):
                    self.core_copy(chunk, z, self.mp, piece).wait_send()

            when(condition, act)

    def schedule(self, chunks, lag=2):
        turns = 2 * self.line - 1
        units = [(chunk, turn) for chunk in chunks for turn in range(turns)]
        todo, marks = [], {}
        for at in range(len(units) + 3 * lag):
            for stage, late in (
                (self.stage_line, 0),
                (self.stage_plane, lag),
                (self.stage_pass, 2 * lag),
                (self.stage_core, 3 * lag),
            ):
                if 0 <= at - late < len(units):
                    todo.append(functools.partial(stage, *units[at - late]))
                    if late == 3 * lag:
                        marks[units[at - late][0]] = len(todo)
        for chunk in chunks:
            todo.append(functools.partial(self.drain, chunk))
        return todo, marks


class Reducer:
    def __init__(self, line, parts, slabs, outs, sets, buffers, sems):
        self.line = line
        self.parts = parts
        self.slabs = slabs
        self.outs = outs
        self.sets = sets
        count = len(set(sets))
        self.core_in, self.own_in, self.pass_in, self.plane_in, self.line_in = (
            buffers[kind * count : (kind + 1) * count] for kind in range(5)
        )
        (
            self.own_sem,
            self.core_send,
            self.core_recv,
            self.pass_send,
            self.pass_recv,
            self.plane_send,
            self.plane_recv,
            self.line_send,
            self.line_recv,
            self.free,
        ) = sems
        self.dp, self.mp, self.z, self.core, self.y, self.x = place()

    @staticmethod
    def buffer_shapes(slabs, sets, line):
        firsts = [sets.index(s) for s in sorted(set(sets))]

        def buffers(lead, halve=False):
            found = []
            for at in firsts:
                slab = list(slabs[at])
                if halve:
                    slab[-2] //= 2
                found.append(pltpu.VMEM(lead + tuple(slab), jnp.bfloat16))
            return found

        return (
            buffers((line, 4))
            + buffers((2,))
            + buffers((line, 2), True)
            + buffers((line, 2))
            + buffers((line + 1,))
        )

    @staticmethod
    def sem_shapes(chunks, line):
        return (
            [DMA((chunks, 4)), DMA((chunks, line, 4)), DMA((chunks, line, 4))]
            + [DMA((chunks, line, 2))] * 6
            + [pltpu.SemaphoreType.REGULAR((5,))]
        )

    halves = staticmethod(Gatherer.halves)

    def part(self, chunk, z, core, mp):
        return slab_of(self.parts[chunk], self.slabs[chunk], 2 * z + core, mp)

    def core_copy(self, chunk, z, mp):
        return remote(
            self.part(chunk, z, 1 - self.core, mp),
            self.core_in[self.sets[chunk]].at[z, mp],
            self.core_send.at[chunk, z, mp],
            self.core_recv.at[chunk, z, mp],
            (self.dp ^ 1, self.mp),
        )

    def own_copy(self, chunk, z, mp):
        return pltpu.make_async_copy(
            self.part(chunk, z, self.core, mp),
            self.own_in[self.sets[chunk]].at[mp % 2],
            self.own_sem.at[chunk, mp],
        )

    def pass_copy(self, chunk, z, way):
        half = self.halves(self.core_in[self.sets[chunk]].at[z, self.mp ^ 3])[way]
        return remote(
            half,
            self.pass_in[self.sets[chunk]].at[z, way],
            self.pass_send.at[chunk, z, way],
            self.pass_recv.at[chunk, z, way],
            (self.dp, self.mp ^ (2 if way == 0 else 1)),
        )

    def plane_copy(self, chunk, z, way):
        mate = self.mp ^ (1 if way == 0 else 2)
        return remote(
            self.core_in[self.sets[chunk]].at[z, mate],
            self.plane_in[self.sets[chunk]].at[z, way],
            self.plane_send.at[chunk, z, way],
            self.plane_recv.at[chunk, z, way],
            (self.dp, mate),
        )

    def line_copy(self, chunk, z, way, slot):
        return remote(
            self.core_in[self.sets[chunk]].at[z, self.mp],
            self.line_in[self.sets[chunk]].at[slot],
            self.line_send.at[chunk, z, way],
            self.line_recv.at[chunk, z, way],
            (self.dp + (-2 if way == 0 else 2), self.mp),
        )

    @classmethod
    def add(cls, target, sources, result=None):
        if len(target.shape) == 3:
            for at in range(target.shape[0]):
                cls.add(
                    target.at[at],
                    [source.at[at] for source in sources],
                    None if result is None else result.at[at],
                )
            return

        def body(rows):
            total = target[rows, :].astype(jnp.float32)
            for source in sources:
                total = total + source[rows, :].astype(jnp.float32)
            if result is None:
                target[rows, :] = total.astype(jnp.bfloat16)
            else:
                result[rows, :] = total

        loop(target.shape[0], 16, body)

    def order(self):
        low, high, found = 0, self.line - 1, []
        while low <= high:
            found.append(low)
            if high != low:
                found.append(high)
            low, high = low + 1, high - 1
        return found

    def neighbours(self):
        return [
            ((self.dp ^ 1, self.mp), None, 0, 0),
            ((self.dp, self.mp ^ 1), None, 1, 1),
            ((self.dp, self.mp ^ 2), None, 2, 2),
            ((self.dp + 2, self.mp), self.z < self.line - 1, 4, 3),
            ((self.dp - 2, self.mp), self.z > 0, 3, 4),
        ]

    def stage_begin(self, chunk, z, wait):
        if wait:
            for device, condition, theirs, mine in self.neighbours():
                when(condition, lambda mine=mine: pl.semaphore_wait(self.free.at[mine], 1))
        for mp in range(4):
            self.core_copy(chunk, z, mp).start()

    def stage_core(self, chunk, z):
        for mp in range(2):
            self.own_copy(chunk, z, mp).start()
        for mp in range(4):
            self.core_copy(chunk, z, mp).wait_recv()
            self.own_copy(chunk, z, mp).wait()
            self.add(
                self.core_in[self.sets[chunk]].at[z, mp],
                [self.own_in[self.sets[chunk]].at[mp % 2]],
            )
            if mp < 2:
                self.own_copy(chunk, z, mp + 2).start()
        for way in (0, 1):
            self.pass_copy(chunk, z, way).start()

    def stage_pass(self, chunk, z):
        for way in (0, 1):
            self.pass_copy(chunk, z, way).wait_recv()
            mate = self.mp ^ (1 if way == 0 else 2)
            self.add(
                self.halves(self.core_in[self.sets[chunk]].at[z, mate])[way],
                [self.pass_in[self.sets[chunk]].at[z, way]],
            )
            self.plane_copy(chunk, z, way).start()

    def stage_plane(self, chunk, z):
        for way in (0, 1):
            self.plane_copy(chunk, z, way).wait_recv()
        plane_in = self.plane_in[self.sets[chunk]]
        self.add(
            self.core_in[self.sets[chunk]].at[z, self.mp],
            [plane_in.at[z, 0], plane_in.at[z, 1]],
        )
        last = self.line - 1
        if z < last:
            when(self.z == last, lambda: self.line_copy(chunk, z, 0, z).start())
        if z > 0:
            when(self.z == 0, lambda: self.send_up(chunk, z))

    def send_up(self, chunk, z):
        slot = jnp.where(self.z + 1 == z, self.line, z)
        self.line_copy(chunk, z, 1, slot).start()

    def stage_line(self, chunk, z, hop):
        last = self.line - 1
        line_in = self.line_in[self.sets[chunk]]
        mine = self.core_in[self.sets[chunk]].at[z, self.mp]

        def join(way):
            self.line_copy(chunk, z, way, z).wait_recv()
            self.add(mine, [line_in.at[z]])
            if way == 0:
                self.line_copy(chunk, z, 0, z).start()
            else:
                self.send_up(chunk, z)

        if z < last - hop:
            when(self.z == last - hop, lambda: join(0))
        if z > hop:
            when(self.z == hop, lambda: join(1))

        def finish():
            sources = []
            if z < last:
                self.line_copy(chunk, z, 0, z).wait_recv()
                sources.append(line_in.at[z])
            if z > 0:
                self.line_copy(chunk, z, 1, self.line).wait_recv()
                sources.append(line_in.at[self.line])
            self.add(mine, sources, self.outs[chunk])

        if hop == max(z, last - z):
            when(self.z == z, finish)

    def release(self, chunk, z, tell):
        for mp in range(4):
            self.core_copy(chunk, z, mp).wait_send()
        for way in (0, 1):
            self.pass_copy(chunk, z, way).wait_send()
            self.plane_copy(chunk, z, way).wait_send()
        when(self.z > z, lambda: self.line_copy(chunk, z, 0, z).wait_send())
        when(self.z < z, lambda: self.line_copy(chunk, z, 1, z).wait_send())
        if tell:
            for device, condition, theirs, mine in self.neighbours():
                when(
                    condition,
                    lambda device=device, theirs=theirs: pl.semaphore_signal(
                        self.free.at[theirs], inc=1, device_id=device, device_id_type=MESH_ID
                    ),
                )

    def schedule(self, chunks):
        units = [(chunk, z) for chunk in chunks for z in self.order()]
        todo = []
        follows = {}
        for chunk in chunks:
            later = [c for c in chunks if c > chunk and self.sets[c] == self.sets[chunk]]
            follows[chunk] = bool(later)
        preceded = {c: any(self.sets[d] == self.sets[c] and d < c for d in chunks) for c in chunks}
        begun = set()

        def begin(at):
            if at < len(units) and at not in begun:
                begun.add(at)
                unit = units[at]
                todo.append(
                    (unit[0], functools.partial(self.stage_begin, *unit, preceded[unit[0]]))
                )

        last_hop = self.line - 1
        settled = last_hop + 3
        for at in range(len(units) + settled):
            if 0 <= at - settled < len(units):
                unit = units[at - settled]
                todo.append((None, functools.partial(self.release, *unit, follows[unit[0]])))
            begin(at)
            if at < len(units) and not preceded[units[at][0]]:
                for other in range(len(units)):
                    if units[other][0] == units[at][0]:
                        begin(other)
            stages = [(self.stage_core, 0, ()), (self.stage_pass, 1, ()), (self.stage_plane, 2, ())]
            stages += [(self.stage_line, 2 + hop, (hop,)) for hop in range(1, self.line)]
            for stage, late, more in stages:
                if 0 <= at - late < len(units):
                    unit = units[at - late]
                    todo.append((unit[0], functools.partial(stage, *unit, *more)))
            if at + 1 < len(units) and units[at + 1][0] == units[at][0]:
                begin(at + 1)
        return todo


NEG = float(ml_dtypes.bfloat16(-1e30))
ONES, MASK, LOW = 0, 1, 2


def nn(a, b):
    return jnp.dot(a, b, preferred_element_type=jnp.float32)


def nt(a, b):
    return lax.dot_general(a, b, (((1,), (1,)), ((), ())), preferred_element_type=jnp.float32)


def tn(a, b):
    return lax.dot_general(a, b, (((0,), (0,)), ((), ())), preferred_element_type=jnp.float32)


def loop(total, step, body):
    def turn(at, carry):
        body(pl.ds(pl.multiple_of(at * step, step), step))
        return carry

    lax.fori_loop(0, total // step, turn, 0)


def standard(v):
    average = jnp.mean(v, axis=-1, keepdims=True)
    centered = v - average
    variance = jnp.mean(centered * centered, axis=-1, keepdims=True)
    inverse = lax.rsqrt(variance + norm_eps)
    return centered * inverse, inverse


GELU_A = math.sqrt(2.0 / math.pi)
GELU_B = 0.044715


def gelu(v):
    return 0.5 * v * (1.0 + jnp.tanh(GELU_A * (v + GELU_B * v * v * v)))


def gelu_slope(v):
    t = jnp.tanh(GELU_A * (v + GELU_B * v * v * v))
    return 0.5 * (1.0 + t) + 0.5 * v * (1.0 - t * t) * GELU_A * (1.0 + 3.0 * GELU_B * v * v)


def lane_index(shape):
    return lax.broadcasted_iota(jnp.int32, shape, len(shape) - 1)


class Plane:
    def __init__(self, dp, mp, z, core):
        self.dp, self.mp, self.z, self.core = dp, mp, z, core

    def partners(self):
        return [
            ((self.dp ^ flip_core, self.mp ^ flip_mp), None)
            for flip_core in (0, 1)
            for flip_mp in range(4)
            if flip_core or flip_mp
        ]

    def routes(self, kind, source, target):
        dp, mp, z, core = self.dp, self.mp, self.z, self.core
        sends, fills = [], []
        for turn in range(4):
            if kind == "mp":
                if turn:
                    peer = mp ^ turn
                    sends.append((source, target.at[mp], (dp, peer), mp, turn, None))
                    fills.append((target.at[peer], peer, None))
            elif kind == "mp_split":
                if turn:
                    peer = mp ^ turn
                    sends.append((source.at[peer], target.at[mp], (dp, peer), mp, turn, None))
                    fills.append((target.at[peer], peer, None))
            elif kind == "to_work":
                device = (2 * z + turn % 2, 2 * (turn // 2) + core)
                here = jnp.logical_and(device[0] == dp, device[1] == mp)
                sends.append((source.at[turn], target.at[mp], device, mp, turn, here))
                own = jnp.logical_and(mp % 2 == core, mp == turn)
                fills.append((target.at[turn], turn, own))
            elif kind == "from_work":
                device = (2 * z + mp % 2, turn)
                slot = 2 * (mp // 2) + core
                here = jnp.logical_and(device[0] == dp, device[1] == mp)
                sends.append((source, target.at[slot], device, slot, turn, here))
                own = jnp.logical_and(2 * (turn // 2) + core == mp, turn % 2 == core)
                fills.append((target.at[turn], turn, own))
        return sends, fills

    def start(self, kind, source, target, sems):
        own_sem, send_sem, recv_sem = sems
        sends, _ = self.routes(kind, source, target)
        for piece, there, device, slot, turn, here in sends:
            copy = remote(piece, there, send_sem.at[turn], recv_sem.at[slot], device)
            if here is None:
                copy.start()
            else:
                pl.when(jnp.logical_not(here))(copy.start)
                pl.when(here)(pltpu.make_async_copy(piece, there, own_sem).start)

    def arrive(self, kind, source, target, sems):
        own_sem, send_sem, recv_sem = sems
        sends, fills = self.routes(kind, source, target)
        for there, slot, own in fills:
            piece = source if kind in ("mp", "from_work") else source.at[0]
            copy = remote(piece, there, send_sem.at[0], recv_sem.at[slot], (self.dp ^ 1, self.mp))
            if own is None:
                copy.wait_recv()
            else:
                pl.when(jnp.logical_not(own))(copy.wait_recv)
        for piece, there, device, slot, turn, here in sends:
            if here is not None:
                pl.when(here)(pltpu.make_async_copy(piece, there, own_sem).wait)

    def sent(self, kind, source, target, sems):
        own_sem, send_sem, recv_sem = sems
        sends, _ = self.routes(kind, source, target)
        for piece, there, device, slot, turn, here in sends:
            copy = remote(piece, there, send_sem.at[turn], recv_sem.at[slot], device)
            if here is None:
                copy.wait_send()
            else:
                pl.when(jnp.logical_not(here))(copy.wait_send)

    def move(self, back, source, target, sems):
        send_sem, recv_sem = sems
        dp, mp, z, core = self.dp, self.mp, self.z, self.core
        if back:
            device = (2 * z + mp % 2, 2 * (mp // 2) + core)
        else:
            device = (2 * z + mp % 2, 2 * (mp // 2) + core)
        here = jnp.logical_and(device[0] == dp, device[1] == mp)
        away = jnp.logical_not(here)
        far = remote(source, target, send_sem, recv_sem, device)
        near = pltpu.make_async_copy(source, target, recv_sem)

        def start():
            pl.when(away)(far.start)
            pl.when(here)(near.start)

        def arrive():
            pl.when(away)(far.wait_recv)
            pl.when(here)(near.wait)

        def sent():
            pl.when(away)(far.wait_send)

        return start, arrive, sent


class Keeper:
    def __init__(self, sems):
        self.sems = sems
        self.count = 0
        self.open = {}

    def put(self, name, source, target):
        copy = pltpu.make_async_copy(source, target, self.sems.at[self.count])
        self.count += 1
        copy.start()
        self.open[name] = copy

    def settle(self, *names):
        for name in names or tuple(self.open):
            if name in self.open:
                self.open.pop(name).wait()


def pixel_rows(block, gain, offset, out, tail, positions_from, count, channels):
    n, inverse = standard(block.astype(jnp.float32))
    result = n * gain + offset
    rows, whole = block.shape[0], channels // 128 * 128
    rest = channels - whole
    out[:, 0:whole] = result[:, 0:whole].astype(jnp.bfloat16)
    tail[:, 0:rest] = result[:, whole:channels]
    lane = lax.broadcasted_iota(jnp.int32, (rows, 128), 1) - rest
    slot = positions_from + lax.broadcasted_iota(jnp.int32, (rows, 128), 0)
    mask = jnp.where(slot < count, 0.0, NEG)
    ones = jnp.where(jnp.logical_or(lane == ONES, lane == LOW), 1.0, 0.0)
    extra = jnp.where(lane == MASK, mask, ones)
    out[:, whole : whole + 128] = jnp.where(lane < 0, tail[...], extra).astype(jnp.bfloat16)
    return n, inverse


def interleave(comm, compute, rate):
    at, due = 0, 0.0
    for after, thunk, microseconds in compute:
        while at < after:
            comm[at]()
            at += 1
        thunk()
        due = max(due, at) + rate * microseconds
        while at < min(due, len(comm)):
            comm[at]()
            at += 1
    while at < len(comm):
        comm[at]()
        at += 1


PIXEL_BLOCK = 512
FORWARD_RATE = 1.0


def forward_kernel(slabs, latents, cotangent, pixels, counts, pixel_gain, pixel_bias, line, layers):
    bf16, f32 = jnp.bfloat16, jnp.float32
    own_rows, width = latents.shape
    items, slots, channels = pixels.shape
    wide = channels + (-channels) % 128
    chunks = len(slabs)
    q_cols = slabs[0].shape[1]
    heads = width // HD
    all_rows = 2 * own_rows
    scale = 1.0 / math.sqrt(width)
    block_scale = 1.0 / math.sqrt(HD)
    kept = dict(
        query_in=((own_rows, width), bf16),
        px=((own_rows, wide), f32),
        after_cross=((own_rows, width), f32),
        cross_hidden_in=((own_rows, width), bf16),
        cross_hidden=((own_rows, width), f32),
        cross_active=((own_rows, width), bf16),
        result=((own_rows, width), bf16),
        qk=((4, own_rows, wide), bf16),
    )
    layer_kept = dict(
        current=((own_rows, width), f32),
        normed=((own_rows, width), bf16),
        qkv=((3, own_rows, width), bf16),
        kv_in=((2, own_rows, width), bf16),
        probs=((heads, own_rows, all_rows), bf16),
        context=((own_rows, width), bf16),
        middle=((own_rows, width), f32),
        hidden_in=((own_rows, width), bf16),
        hidden=((own_rows, width), f32),
        active=((own_rows, width), bf16),
    )
    scratch_types = dict(kept)
    scratch_types.update(layer_kept)
    names = list(scratch_types)
    out_names = list(kept) + [(name, l) for l in range(layers) for name in layer_kept]
    out_types = dict(kept)
    for l in range(layers):
        out_types.update({(name, l): layer_kept[name] for name in layer_kept})
    gathered_types = [
        jax.ShapeDtypeStruct((width, q_cols), bf16),
        jax.ShapeDtypeStruct((3, width, width), bf16),
    ] + [jax.ShapeDtypeStruct((6, width, width), bf16)] * layers

    def kernel(*refs):
        refs = list(refs)

        def take(n):
            found = refs[:n]
            del refs[:n]
            return found

        slab_refs = take(chunks)
        latents_ref, cot_ref, pixels_ref, counts_ref, gain_ref, bias_ref = take(6)
        gathered = take(chunks)
        (cot_work,) = take(1)
        outs = dict(zip(out_names, take(len(out_names))))
        v = types.SimpleNamespace(**dict(zip(names, take(len(names)))))
        called = types.SimpleNamespace(**{name: name for name in names})
        weights = take(chunks)
        latents_home, latents_work, pixels_v, xs, xs_tail, scores_v, acc, top, norms, px_send, px_in = take(11)
        gather_sems = take(9)
        load_sems, io_sems, keep_sems = take(3)
        qk_sems, px_sems, move_sems, kv_sems = take(3), take(3), take(2), take(2)
        vq, vc = weights[0], weights[1]
        gatherer = Gatherer(line, slab_refs, gathered, sems=gather_sems)
        dp, mp, z, core = gatherer.dp, gatherer.mp, gatherer.z, gatherer.core
        plane = Plane(dp, mp, z, core)
        keep = Keeper(keep_sems)
        partners = plane.partners() + [
            ((dp + 2, mp), z < line - 1),
            ((dp - 2, mp), z > 0),
        ]
        greet(partners)
        def store(name):
            keep.put(name, getattr(v, name), outs[name])

        home_copy = pltpu.make_async_copy(latents_ref, latents_home, io_sems.at[0])
        pixel_copy = pltpu.make_async_copy(pixels_ref, pixels_v, io_sems.at[1])
        home_copy.start()
        pixel_copy.start()
        move_start, move_arrive, move_sent = plane.move(
            False, latents_ref, latents_work, [s.at[0] for s in move_sems]
        )
        cot_start, cot_arrive, cot_sent = plane.move(
            False, cot_ref, cot_work, [s.at[1] for s in move_sems]
        )

        def load_copy(chunk, at):
            source, target = gathered[chunk], weights[chunk]
            if chunk == 0:
                rows = pl.ds(pl.multiple_of(at * 8 * 32, 256), 256)
                return pltpu.make_async_copy(
                    source.at[rows], target.at[rows], load_sems.at[chunk, at]
                )
            span = 256
            rows = pl.ds(pl.multiple_of(at * span, span), span)
            return pltpu.make_async_copy(
                source.at[:, rows], target.at[:, rows], load_sems.at[chunk, at]
            )

        gatherer.on_unit = lambda chunk, at: load_copy(chunk, at).start()

        def loaded(chunk):
            for at in range(line):
                load_copy(chunk, at).wait()

        def norm_rows(source, j, target):
            n, _ = standard(source[...].astype(f32))
            target[...] = (n * norms[j : j + 1, :] + norms[j + 6 : j + 7, :]).astype(bf16)

        def start_queries():
            loaded(0)
            raw = vq[:, width + 2 * wide :].astype(f32)
            norms[...] = raw.T[0:16, :]
            home_copy.wait()
            norm_rows(latents_home, 0, v.query_in)
            store(called.query_in)

            v.cross_hidden_in[...] = nt(v.query_in[...], vq[:, 0:width]).astype(bf16)
            qk = nn(v.cross_hidden_in[...], vq[:, width : width + wide]) * scale
            lane = lane_index(qk.shape)
            v.qk[mp] = jnp.where(lane == channels + MASK, 1.0, qk).astype(bf16)
            plane.start("mp", v.qk.at[mp], v.qk, qk_sems)
            move_start()

        def queries_here():
            plane.arrive("mp", v.qk.at[mp], v.qk, qk_sems)
            store(called.qk)

        def cross_blocks(item, first, last):
            if first == 0:
                acc[...] = jnp.zeros_like(acc)
                top[...] = jnp.full_like(top, NEG)
            queries = v.qk[2 * item : 2 * item + 2].reshape(all_rows, wide)

            def body(at, carry):
                begin = pl.multiple_of(at * PIXEL_BLOCK, PIXEL_BLOCK)
                block = pixels_v[item, pl.ds(begin, PIXEL_BLOCK), :]
                pixel_rows(
                    block,
                    gain_ref[...],
                    bias_ref[...],
                    xs,
                    xs_tail,
                    mp * slots + begin,
                    counts_ref[item],
                    channels,
                )
                scores = nt(queries, xs[...])
                old = top[:, 0:1]
                new = jnp.maximum(old, jnp.max(scores, axis=1, keepdims=True))
                lifted = jnp.exp(scores - new).astype(bf16)
                acc[...] = acc[...] * jnp.exp(old - new) + nn(lifted, xs[...])
                top[...] = jnp.broadcast_to(new, top.shape)
                return carry

            lax.fori_loop(first, last, body, 0)

        def cross_finish(item):
            def body(rows):
                high = top[rows, 0:1]
                rounded = high.astype(bf16).astype(f32)
                value = acc[rows, :] * jnp.exp(high - rounded)
                total = value[:, channels + ONES : channels + ONES + 1]
                total_high = total.astype(bf16).astype(f32)
                lane = lane_index(value.shape)
                value = jnp.where(lane == channels + MASK, rounded, value)
                value = jnp.where(lane == channels + LOW, total - total_high, value)
                scores_v[rows, :] = value.astype(bf16)

            loop(all_rows, 64, body)
            px_send[2 * item] = scores_v[0:own_rows, :]
            px_send[2 * item + 1] = scores_v[own_rows:all_rows, :]

        def send_px():
            plane.start("to_work", px_send, px_in, px_sems)

        def merge():
            plane.arrive("to_work", px_send, px_in, px_sems)
            move_arrive()

            def body(rows):
                parts = [px_in[j, rows, :].astype(f32) for j in range(4)]
                tops = [p[:, channels + MASK : channels + MASK + 1] for p in parts]
                totals = [
                    p[:, channels + ONES : channels + ONES + 1]
                    + p[:, channels + LOW : channels + LOW + 1]
                    for p in parts
                ]
                high = jnp.maximum(jnp.maximum(tops[0], tops[1]), jnp.maximum(tops[2], tops[3]))
                shares = [jnp.exp(t - high) for t in tops]
                total = sum(s * t for s, t in zip(shares, totals))
                px = sum(s * p for s, p in zip(shares, parts)) / total
                lane = lane_index(px.shape)
                px = jnp.where(lane < channels, px, 0.0)
                v.px[rows, :] = jnp.where(
                    lane == channels, high + jnp.log(total), px
                )
                px_in[0, rows, :] = px.astype(bf16)

            loop(own_rows, 64, body)
            store(called.px)

        def cross_context():
            loaded(1)

            v.cross_active[...] = nt(
                px_in[0], vq[:, width + wide : width + 2 * wide]
            ).astype(bf16)
            v.after_cross[...] = latents_work[...].astype(f32) + nt(v.cross_active[...], vc[2])
            store(called.after_cross)

        def cross_branch():
            norm_rows(v.after_cross, 1, v.cross_hidden_in)
            store(called.cross_hidden_in)
            hidden = nt(v.cross_hidden_in[...], vc[0])
            v.cross_hidden[...] = hidden
            v.cross_active[...] = gelu(hidden).astype(bf16)
            store(called.cross_hidden)
            store(called.cross_active)

        def cross_result():
            cot_start()
            v.current[...] = v.after_cross[...] + nt(v.cross_active[...], vc[1])

        def kv_copy(t, l):
            return remote(
                v.qkv.at[1 + t],
                v.kv_in.at[t],
                kv_sems[0].at[l, t],
                kv_sems[1].at[l, t],
                (dp ^ 1, mp),
            )

        def save(name, l):
            keep.put((name, l), getattr(v, name), outs[name, l])

        def done(name, l):
            if l:
                keep.settle((name, l - 1))

        def block_qkv(l):
            w = weights[2 + l]
            loaded(2 + l)
            save(called.current, l)
            done(called.normed, l)
            norm_rows(v.current, 2 + 2 * l, v.normed)
            save(called.normed, l)
            done(called.qkv, l)
            if l:
                done(called.kv_in, l)
                for t in range(2):
                    kv_copy(t, l - 1).wait_send()
                pl.semaphore_signal(
                    kv_free, inc=1, device_id=(dp ^ 1, mp), device_id_type=MESH_ID
                )
                pl.semaphore_wait(kv_free, 1)
            for t in range(2):
                v.qkv[1 + t] = nn(v.normed[...], w[1 + t]).astype(bf16)
                kv_copy(t, l).start()

        def block_q(l):
            v.qkv[0] = nn(v.normed[...], weights[2 + l][0]).astype(bf16)
            save(called.qkv, l)
            done(called.probs, l)
            done(called.context, l)
            for t in range(2):
                kv_copy(t, l).wait_recv()

        def block_attention(first, last):
            def body(h, carry):
                one_head(2 * h)
                one_head(2 * h + 1)
                return carry

            lax.fori_loop(first // 2, last // 2, body, 0)

        def one_head(h):
            at = pl.ds(pl.multiple_of(h * HD, HD), HD)
            queries = v.qkv[0, :, at]
            keys, values = v.qkv[1, :, at], v.qkv[2, :, at]
            keys_in, values_in = v.kv_in[0, :, at], v.kv_in[1, :, at]
            near = nt(queries, keys) * block_scale
            far = nt(queries, keys_in) * block_scale
            high = jnp.maximum(
                jnp.max(near, axis=1, keepdims=True), jnp.max(far, axis=1, keepdims=True)
            )
            near, far = jnp.exp(near - high), jnp.exp(far - high)
            inverse = 1.0 / (
                jnp.sum(near, axis=1, keepdims=True) + jnp.sum(far, axis=1, keepdims=True)
            )
            near, far = (near * inverse).astype(bf16), (far * inverse).astype(bf16)
            v.probs[h, :, 0:own_rows] = near
            v.probs[h, :, own_rows:all_rows] = far
            v.context[:, at] = (nn(near, values) + nn(far, values_in)).astype(bf16)

        def block_out(l):
            w = weights[2 + l]
            save(called.kv_in, l)
            save(called.probs, l)
            save(called.context, l)
            done(called.middle, l)
            v.middle[...] = v.current[...] + nt(v.context[...], w[3])
            save(called.middle, l)
            done(called.hidden_in, l)
            norm_rows(v.middle, 3 + 2 * l, v.hidden_in)
            save(called.hidden_in, l)

        def block_up(l):
            w = weights[2 + l]
            done(called.hidden, l)
            done(called.active, l)
            hidden = nn(v.hidden_in[...], w[4])
            v.hidden[...] = hidden
            v.active[...] = gelu(hidden).astype(bf16)
            save(called.hidden, l)
            save(called.active, l)
            keep.settle((called.current, l))
            v.current[...] = v.middle[...] + nt(v.active[...], w[5])
            if l == layers - 1:
                v.result[...] = v.current[...].astype(bf16)
                store(called.result)

        (kv_free,) = take(1)
        comm, marks = gatherer.schedule(range(chunks))
        pixel_blocks = slots // PIXEL_BLOCK
        work = [
            (marks[0], start_queries, 4),
            (0, lambda: (pixel_copy.wait(), queries_here()), 1),
        ]
        for item in range(items):
            for at in range(0, pixel_blocks, 2):
                work.append((0, functools.partial(cross_blocks, item, at, at + 2), 3.5))
            work.append((0, functools.partial(cross_finish, item), 1))
        work += [
            (0, send_px, 1),
            (marks[1], merge, 2),
            (marks[1], cross_context, 2),
            (0, cross_branch, 2),
            (0, cross_result, 2),
        ]
        for l in range(layers):
            work += [
                (marks[2 + l], functools.partial(block_qkv, l), 3),
                (0, functools.partial(block_q, l), 1),
                (0, functools.partial(block_attention, 0, heads // 2), 1.5),
                (0, functools.partial(block_attention, heads // 2, heads), 1.5),
                (0, functools.partial(block_out, l), 2),
                (0, functools.partial(block_up, l), 2),
            ]
        interleave(comm, work, FORWARD_RATE)
        plane.sent("mp", v.qk.at[mp], v.qk, qk_sems)
        plane.sent("to_work", px_send, px_in, px_sems)
        move_sent()
        cot_arrive()
        cot_sent()
        for t in range(2):
            kv_copy(t, layers - 1).wait_send()
        keep.settle()

    results = pl.pallas_call(
        kernel,
        out_shape=tuple(
            gathered_types
            + [jax.ShapeDtypeStruct(cotangent.shape, bf16)]
            + [jax.ShapeDtypeStruct(*out_types[name]) for name in out_names]
        ),
        in_specs=[ANY] * chunks
        + [ANY, ANY, ANY, pl.BlockSpec(memory_space=pltpu.SMEM)]
        + [pl.BlockSpec(memory_space=pltpu.VMEM)] * 2,
        out_specs=[ANY] * (chunks + 1 + len(out_names)),
        scratch_shapes=[pltpu.VMEM(*scratch_types[name]) for name in names]
        + [pltpu.VMEM(t.shape, t.dtype) for t in gathered_types]
        + [
            pltpu.VMEM((own_rows, width), bf16),
            pltpu.VMEM((own_rows, width), bf16),
            pltpu.VMEM(pixels.shape, bf16),
            pltpu.VMEM((PIXEL_BLOCK, wide), bf16),
            pltpu.VMEM((PIXEL_BLOCK, 128), f32),
            pltpu.VMEM((all_rows, wide), bf16),
            pltpu.VMEM((all_rows, wide), f32),
            pltpu.VMEM((all_rows, 128), f32),
            pltpu.VMEM((16, width), f32),
            pltpu.VMEM((4, own_rows, wide), bf16),
            pltpu.VMEM((4, own_rows, wide), bf16),
        ]
        + Gatherer.sem_shapes(chunks, line)
        + [DMA((chunks, line)), DMA((2,)), DMA((len(out_names),))]
        + [DMA(()), DMA((4,)), DMA((4,))] * 2
        + [DMA((2,)), DMA((2,))]
        + [DMA((layers, 2)), DMA((layers, 2))]
        + [pltpu.SemaphoreType.REGULAR],
        compiler_params=pltpu.CompilerParams(
            collective_id=0, has_side_effects=True, vmem_limit_bytes=63 * 1024 * 1024
        ),
        name="forward",
    )(*slabs, latents, cotangent, pixels, counts, pixel_gain, pixel_bias)
    return results[:chunks], results[chunks], dict(zip(out_names, results[chunks + 1 :]))


BACK_BLOCK = 512


def backward_kernel(
    gathered, kept, cotangent, result, latents, pixels, counts, pixel_gain, pixel_bias, line, layers
):
    bf16, f32 = jnp.bfloat16, jnp.float32
    own_rows, width = latents.shape
    items, slots, channels = pixels.shape
    wide = channels + (-channels) % 128
    q_cols = gathered[0].shape[1]
    cols_m = width // 4
    heads = width // HD
    all_rows = 2 * own_rows
    scale = 1.0 / math.sqrt(width)
    block_scale = 1.0 / math.sqrt(HD)
    own_cols = width // (8 * line)
    rows_d = width // (2 * line)
    gk_cols = 2 * wide + 128
    kept_names = list(kept)
    layer_names = [name[0] for name in kept_names if isinstance(name, tuple) and name[1] == 0]
    qk_name = next(name for name in kept_names if name == "qk")
    slabs = [(3, rows_d, cols_m)] * (2 * layers) + [(2, own_cols, width), (own_cols, gk_cols)]
    sets = [0, 1] * layers + [2, 3]
    chunks = len(slabs)
    c_chunk, gk_chunk = 2 * layers, 2 * layers + 1
    part_types = [jax.ShapeDtypeStruct((3, width, width), bf16)] * (2 * layers) + [
        jax.ShapeDtypeStruct((2, width, width), bf16),
        jax.ShapeDtypeStruct((width, gk_cols), bf16),
    ]
    reduced_types = [jax.ShapeDtypeStruct(s, f32) for s in slabs[:-1]]
    other_types = [
        jax.ShapeDtypeStruct((width, gk_cols), bf16),
        jax.ShapeDtypeStruct((own_rows, width), bf16),
        jax.ShapeDtypeStruct(pixels.shape, bf16),
        jax.ShapeDtypeStruct((own_rows, width), bf16),
    ]
    v_types = {name: (kept[name, 0].shape, kept[name, 0].dtype) for name in layer_names}
    v_types.update(
        dict(
            qk=(kept[qk_name].shape, bf16),
            weights=((6, width, width), bf16),
            stage=((4, width, 256), bf16),
            cot=((own_rows, width), f32),
            tmp=((own_rows, width), f32),
            low=((own_rows, width), bf16),
            turned=((width, own_rows), bf16),
            qkv_cot=((3, own_rows, width), bf16),
            kv_out=((2, own_rows, width), bf16),
            kv_in_cot=((layers, 2, own_rows, width), bf16),
            norms=((16, width), f32),
            grads=((16, width), f32),
            after_home=((own_rows, width), bf16),
            cv_all=((4, own_rows, wide), bf16),
            dsx_in=((4, own_rows, wide), bf16),
            block=((2, BACK_BLOCK, channels), bf16),
            out_block=((2, BACK_BLOCK, channels), bf16),
            xs=((BACK_BLOCK, wide), bf16),
            xs_tail=((BACK_BLOCK, 128), f32),
            pixel_sums=((16, channels), f32),
            gk_own=((own_cols, gk_cols), f32),
            gk_low=((own_cols, gk_cols), bf16),
        )
    )
    v_names = list(v_types)
    ins = list(gathered) + [kept[n] for n in kept_names]

    def kernel(*refs):
        refs = list(refs)

        def take(n):
            found = refs[:n]
            del refs[:n]
            return found

        g_refs = take(len(gathered))
        layer_refs = dict(zip(kept_names, take(len(kept_names))))
        kept_refs = types.SimpleNamespace(
            **{name: ref for name, ref in layer_refs.items() if not isinstance(name, tuple)}
        )
        cot_ref, result_ref, latents_ref, pixels_ref, counts_ref, gain_ref, bias_ref = take(7)
        parts = take(chunks)
        reduced = take(chunks - 1)
        gk_all, latent_grad_ref, pixel_grad_ref, out_ref = take(4)
        v = types.SimpleNamespace(**dict(zip(v_names, take(len(v_names)))))
        called = types.SimpleNamespace(**{name: name for name in v_names})
        v.low2 = v.active
        v.px = v.middle.at[:, pl.ds(0, wide)]
        v.cv = v.context.at[:, pl.ds(0, wide)]

        class Pieces:
            def __getitem__(self, piece):
                column = pl.multiple_of(piece % 2 * all_rows, all_rows)
                return v.kv_out.at[piece // 2, :, pl.ds(column, wide)]

        pieces = types.SimpleNamespace(at=Pieces())
        acc_parts = (
            (v.tmp.at[:, pl.ds(0, all_rows)], slice(0, own_rows)),
            (v.tmp.at[pl.ds(0, wide - own_rows), pl.ds(all_rows, all_rows)], slice(own_rows, wide)),
        )
        buffers = take(len(Reducer.buffer_shapes(slabs, sets, line)))
        reduce_sems = take(10)
        gather_sems = take(9)
        fetch_sems, stage_sems, block_sems, out_sems = take(4)
        kv_sems, cv_sems, dsx_sems, move_sems = take(2), take(3), take(3), take(2)
        reducer = Reducer(line, parts, slabs, reduced + [v.gk_own], sets, buffers, reduce_sems)
        gatherer = Gatherer(line, [v.gk_low], [gk_all], gather_sems)
        dp, mp, z, core = reducer.dp, reducer.mp, reducer.z, reducer.core
        plane = Plane(dp, mp, z, core)
        greet(
            plane.partners()
            + [((dp + 2, mp), z < line - 1), ((dp - 2, mp), z > 0)]
        )
        w = v.weights
        open_copies = {}
        numbered = []

        def fetch(tag, source, target):
            copy = pltpu.make_async_copy(source, target, fetch_sems.at[len(numbered)])
            numbered.append(tag)
            copy.start()
            open_copies[tag] = copy

        def here(*tags):
            for tag in tags:
                if tag in open_copies:
                    open_copies.pop(tag).wait()

        w_qkv, w_out, w_up, w_down = (0, 3), (3, 1), (4, 1), (5, 1)

        def fetch_weight(span, l):
            if l >= 0:
                part = pl.ds(*span)
                fetch((span, l), g_refs[2 + l].at[part], w.at[part])

        def fetch_kept(name, l):
            if l >= 0:
                fetch((name, l), layer_refs[name, l], getattr(v, name))

        stage_open = []

        def stage_out(at, value, target):
            n = value.shape[1]
            slot = v.stage.at[at, :, pl.ds(0, n)] if n < 256 else v.stage.at[at]
            slot[...] = value
            return pltpu.make_async_copy(slot, target, stage_sems.at[at])

        def settle_stage():
            while stage_open:
                stage_open.pop()()

        def grad_out(right, target):
            settle_stage()

            def body(m, carry):
                stage_out(m, nn(v.turned[...], right(m)).astype(bf16), target(m)).start()
                return carry

            lax.fori_loop(0, 4, body, 0)

            def settle():
                def wait(m, carry):
                    pltpu.make_async_copy(v.stage.at[m], target(m), stage_sems.at[m]).wait()
                    return carry

                lax.fori_loop(0, 4, wait, 0)

            stage_open.append(settle)

        def layer_part(l, which):
            part = parts[2 * (layers - 1 - l) + (0 if which >= 3 else 1)]
            return lambda m: part.at[which % 3, :, lane_block(m)]

        def lane_block(m):
            return pl.ds(pl.multiple_of(m * 256, 256), 256)

        def turn(value):
            v.turned[...] = value[...].T

        def norm_back_into(source, j, add, write):
            gains = biases = jnp.zeros((1, width), f32)
            for first_row in range(0, own_rows, own_rows // 2):
                rows = slice(first_row, first_row + own_rows // 2)
                n, inverse = standard(source[rows, :].astype(f32))
                u = v.tmp[rows, :]
                scaled = u * v.norms[j : j + 1, :]
                first = jnp.mean(scaled, axis=1, keepdims=True)
                second = jnp.mean(scaled * n, axis=1, keepdims=True)
                write(rows, add(rows) + (scaled - first - n * second) * inverse)
                gains = gains + jnp.sum(u * n, axis=0, keepdims=True)
                biases = biases + jnp.sum(u, axis=0, keepdims=True)
            v.grads[j : j + 1, :] = gains
            v.grads[j + 6 : j + 7, :] = biases

        def into_cot(rows, value):
            v.cot[rows, :] = value

        def add_cot(rows):
            return v.cot[rows, :]

        def each(body):
            def step(m, carry):
                body(m)
                return carry

            lax.fori_loop(0, 4, step, 0)

        def begin():
            fetch(0, g_refs[0].at[:, pl.ds(width + 2 * wide, 128)], v.stage.at[0, :, pl.ds(0, 128)])
            fetch(1, cot_ref, v.low)
            out_start()
            last = layers - 1
            fetch_kept(called.active, last)
            fetch_weight(w_down, last)
            fetch_kept(called.hidden, last)
            fetch_kept(called.hidden_in, last)
            fetch_weight(w_up, last)
            fetch_kept(called.middle, last)
            fetch_weight(w_out, last)
            for name in (called.context, called.probs, called.qkv, called.kv_in, called.normed):
                fetch_kept(name, last)
            fetch_weight(w_qkv, last)
            fetch_kept(called.current, last)
            fetch(3, kept_refs.qk, v.qk)
            v.grads[...] = jnp.zeros_like(v.grads)
            here(0, 1)
            raw = v.stage[0, :, 0:128].astype(f32)
            v.norms[...] = raw.T[0:16, :]
            v.cot[...] = v.low[...].astype(f32)

        def branch_a(l):
            v.low[...] = v.cot[...].astype(bf16)
            turn(v.low)
            here((called.active, l))
            grad_out(lambda m: v.active[:, lane_block(m)], layer_part(l, 5))

        def branch_a2(l):
            here((w_down, l), (called.hidden, l))
            active_cot = nn(v.low[...], w[5])
            v.active[...] = (active_cot * gelu_slope(v.hidden[...])).astype(bf16)
            fetch_weight(w_down, l - 1)
            fetch_kept(called.hidden, l - 1)

        def branch_b(l):
            here((called.hidden_in, l))
            turn(v.hidden_in)
            fetch_kept(called.hidden_in, l - 1)
            grad_out(lambda m: v.active[:, lane_block(m)], layer_part(l, 4))

        def branch_b2(l):
            here((w_up, l), (called.middle, l))
            v.tmp[...] = nt(v.active[...], w[4])
            norm_back_into(v.middle, 3 + 2 * l, add_cot, into_cot)
            fetch_weight(w_up, l - 1)
            fetch_kept(called.active, l - 1)
            fetch_kept(called.middle, l - 1)

        def branch_c(l):
            v.low[...] = v.cot[...].astype(bf16)
            turn(v.low)
            here((called.context, l), (w_out, l))
            grad_out(lambda m: v.context[:, lane_block(m)], layer_part(l, 3))
            v.context[...] = nn(v.low[...], w[3]).astype(bf16)
            fetch_weight(w_out, l - 1)
            settle_stage()

        def kv_copy(t, l):
            return remote(
                v.kv_out.at[t],
                v.kv_in_cot.at[l, t],
                kv_sems[0].at[l, t],
                kv_sems[1].at[l, t],
                (dp ^ 1, mp),
            )

        def attention(l, first, last):
            if first == 0:
                here((called.probs, l), (called.qkv, l), (called.kv_in, l))
                if l < layers - 1:
                    for t in range(2):
                        kv_copy(t, l + 1).wait_send()

            def body(h, carry):
                one_head(2 * h)
                one_head(2 * h + 1)
                return carry

            lax.fori_loop(first // 2, last // 2, body, 0)
            if last == heads:
                for t in range(2):
                    kv_copy(t, l).start()
                for name in (called.context, called.probs, called.qkv, called.kv_in):
                    fetch_kept(name, l - 1)

        def one_head(h):
            at = pl.ds(pl.multiple_of(h * HD, HD), HD)
            queries = v.qkv[0, :, at]
            keys, values = v.qkv[1, :, at], v.qkv[2, :, at]
            keys_in, values_in = v.kv_in[0, :, at], v.kv_in[1, :, at]
            up = v.context[:, at]
            near_low = v.probs[h, :, 0:own_rows]
            far_low = v.probs[h, :, own_rows:all_rows]
            v.qkv_cot[2, :, at] = tn(near_low, up).astype(bf16)
            v.kv_out[1, :, at] = tn(far_low, up).astype(bf16)
            near, far = near_low.astype(f32), far_low.astype(f32)
            near_cot = near * nt(up, values)
            far_cot = far * nt(up, values_in)
            row = jnp.sum(near_cot, axis=1, keepdims=True) + jnp.sum(
                far_cot, axis=1, keepdims=True
            )
            near_cot = ((near_cot - near * row) * block_scale).astype(bf16)
            far_cot = ((far_cot - far * row) * block_scale).astype(bf16)
            v.qkv_cot[0, :, at] = (nn(near_cot, keys) + nn(far_cot, keys_in)).astype(bf16)
            v.qkv_cot[1, :, at] = tn(near_cot, queries).astype(bf16)
            v.kv_out[0, :, at] = tn(far_cot, queries).astype(bf16)

        def branch_d(l):
            here((called.normed, l))
            turn(v.normed)
            fetch_kept(called.normed, l - 1)
            grad_out(lambda m: v.qkv_cot[0, :, lane_block(m)], layer_part(l, 0))
            for t in range(2):
                kv_copy(t, l).wait_recv()
                v.qkv_cot[1 + t] = (
                    v.qkv_cot[1 + t].astype(f32) + v.kv_in_cot[l, t].astype(f32)
                ).astype(bf16)

        def branch_d2(l):
            for t in (1, 2):
                grad_out(lambda m, t=t: v.qkv_cot[t, :, lane_block(m)], layer_part(l, t))

        def branch_e(l):
            here((w_qkv, l), (called.current, l))
            v.tmp[...] = nt(v.qkv_cot[0], w[0]) + nt(v.qkv_cot[1], w[1]) + nt(v.qkv_cot[2], w[2])
            norm_back_into(v.current, 2 + 2 * l, add_cot, into_cot)
            fetch_weight(w_qkv, l - 1)
            fetch_kept(called.current, l - 1)
            settle_stage()

        def cross_begin():
            for k in range(3):
                fetch(4 + k, g_refs[1].at[k], w.at[k])
            fetch(7, g_refs[0].at[:, pl.ds(0, width)], w.at[3])
            fetch(8, g_refs[0].at[:, pl.ds(width, wide)], w.at[4, :, pl.ds(0, wide)])
            fetch(9, g_refs[0].at[:, pl.ds(width + wide, wide)], w.at[5, :, pl.ds(0, wide)])
            fetch(10, kept_refs.after_cross, v.current)
            fetch(11, kept_refs.cross_hidden_in, v.hidden_in)
            fetch(12, kept_refs.cross_active, v.normed)
            fetch(13, kept_refs.cross_hidden, v.middle)
            v.low[...] = v.cot[...].astype(bf16)
            turn(v.low)

        def cross_a():
            here(12)
            grad_out(
                lambda m: v.normed[:, lane_block(m)],
                lambda m: parts[c_chunk].at[1, :, lane_block(m)],
            )
            here(5, 13)

            active_cot = nn(v.low[...], w[1])
            v.low2[...] = (active_cot * gelu_slope(v.middle[...])).astype(bf16)

        def cross_b():
            turn(v.low2)
            here(11, 4)
            grad_out(
                lambda m: v.hidden_in[:, lane_block(m)],
                lambda m: parts[c_chunk].at[0, :, lane_block(m)],
            )

        def cross_b2():
            fetch(2, kept_refs.px, v.px)
            v.tmp[...] = nn(v.low2[...], w[0])
            here(10)
            norm_back_into(v.current, 1, add_cot, into_cot)
            v.low[...] = v.cot[...].astype(bf16)
            settle_stage()
            fetch(14, kept_refs.query_in, v.normed)
            fetch(15, latents_ref, v.hidden_in)

        home_start, home_arrive, home_sent = plane.move(
            True, v.low, v.after_home, [s.at[0] for s in move_sems]
        )
        out_start, out_arrive, out_sent = plane.move(
            True, result_ref, out_ref, [s.at[1] for s in move_sems]
        )

        def gk_columns(value, column):
            settle_stage()
            copies = [
                stage_out(0, value[:, 0:256], parts[gk_chunk].at[:, pl.ds(column, 256)]),
                stage_out(1, value[:, 256:wide], parts[gk_chunk].at[:, pl.ds(column + 256, wide - 256)]),
            ]
            for copy in copies:
                copy.start()
                stage_open.append(copy.wait)

        def cross_c():
            home_start()
            turn(v.low)
            here(2, 6, 9)
            lane = lane_index((own_rows, wide))
            px = v.px[...]
            px = jnp.where(lane < channels, px, 0.0)
            gk_columns(nn(v.turned[...], px.astype(bf16)).astype(bf16), wide)

            v.low2[...] = nn(v.low[...], w[2]).astype(bf16)
            cv = nn(v.low2[...], w[5, :, 0:wide]).astype(bf16).astype(f32)
            delta = jnp.sum(cv * px, axis=1, keepdims=True)
            logs = v.px[:, channels : channels + 1]

            def two(value):
                high = value.astype(bf16).astype(f32)
                return high, value - high

            delta_high, delta_low = two(-delta)
            log_high, log_low = two(logs)
            for at, value in (
                (ONES, delta_high),
                (LOW, delta_low),
                (3, log_high),
                (4, log_low),
            ):
                cv = jnp.where(lane == channels + at, value, cv)
            v.cv[...] = cv.astype(bf16)
            plane.start("from_work", v.cv, v.cv_all, cv_sems)

        def cross_d():
            plane.arrive("from_work", v.cv, v.cv_all, cv_sems)
            here(3)

            def body(m):
                cv = v.cv_all[m].astype(f32)
                qk = v.qk[m].astype(f32)
                lane = lane_index(qk.shape)
                qk = jnp.where(lane == channels + ONES, -cv[:, channels + 3 : channels + 4], qk)
                qk = jnp.where(lane == channels + LOW, -cv[:, channels + 4 : channels + 5], qk)
                v.qk[m] = qk.astype(bf16)

            each(body)
            v.pixel_sums[...] = jnp.zeros_like(v.pixel_sums)

        blocks = slots // BACK_BLOCK

        def block_in(item, at):
            rows = pl.ds(pl.multiple_of(at * BACK_BLOCK, BACK_BLOCK), BACK_BLOCK)
            return pltpu.make_async_copy(
                pixels_ref.at[item, rows], v.block.at[lax.rem(at, 2)], block_sems.at[lax.rem(at, 2)]
            )

        def block_out(item, at):
            rows = pl.ds(pl.multiple_of(at * BACK_BLOCK, BACK_BLOCK), BACK_BLOCK)
            return pltpu.make_async_copy(
                v.out_block.at[lax.rem(at, 2)],
                pixel_grad_ref.at[item, rows],
                out_sems.at[lax.rem(at, 2)],
            )

        def cross_blocks(item, first, last):
            block_in(item, first).start()
            if first == 0:
                v.tmp[...] = jnp.zeros_like(v.tmp)
            queries = v.qk[2 * item : 2 * item + 2].reshape(all_rows, wide)
            cvs = v.cv_all[2 * item : 2 * item + 2].reshape(all_rows, wide)

            def body(at, carry):
                slot = lax.rem(at, 2)
                block_in(item, at).wait()
                pl.when(at + 1 < last)(lambda: block_in(item, at + 1).start())
                gain = gain_ref[...]
                n, inverse = pixel_rows(
                    v.block[slot],
                    gain,
                    bias_ref[...],
                    v.xs,
                    v.xs_tail,
                    mp * slots + at * BACK_BLOCK,
                    counts_ref[item],
                    channels,
                )
                xs = v.xs[...]
                probs = jnp.exp(nt(xs, queries))
                score_cot = (probs * nt(xs, cvs)).astype(bf16)
                u = nn(score_cot, queries) + nn(probs.astype(bf16), cvs)
                sums = tn(xs, score_cot)
                for part, rows in acc_parts:
                    part[...] += sums[rows]
                u = u[:, 0:channels]
                scaled = u * gain
                mean = jnp.mean(scaled, axis=1, keepdims=True)
                second = jnp.mean(scaled * n, axis=1, keepdims=True)
                v.pixel_sums[0:1, :] += jnp.sum(u * n, axis=0, keepdims=True)
                v.pixel_sums[1:2, :] += jnp.sum(u, axis=0, keepdims=True)
                pl.when(at >= first + 2)(lambda: block_out(item, at - 2).wait())
                v.out_block[slot] = ((scaled - mean - n * second) * inverse).astype(bf16)
                block_out(item, at).start()
                return carry

            lax.fori_loop(first, last, body, 0)
            block_out(item, last - 2).wait()
            block_out(item, last - 1).wait()

        def cross_finish(item):
            whole = jnp.concatenate([part[...] for part, _ in acc_parts], axis=0)
            whole = (whole * scale).T
            lane = lane_index(whole.shape)
            whole = jnp.where(lane < channels, whole, 0.0).astype(bf16)
            if item == 0:
                for t in range(2):
                    kv_copy(t, 0).wait_send()
            for half in range(2):
                piece = pieces.at[2 * item + half]
                piece[...] = whole[half * own_rows : (half + 1) * own_rows]

        def send_dsx():
            plane.start("mp_split", pieces, v.dsx_in, dsx_sems)
            here(14)
            turn(v.normed)

        def home():
            plane.arrive("mp_split", pieces, v.dsx_in, dsx_sems)
            total = pieces.at[mp][...].astype(f32)
            for flip in range(1, 4):
                total = total + v.dsx_in[mp ^ flip].astype(f32)
            dsx = total.astype(bf16)
            gk_columns(nn(v.turned[...], dsx).astype(bf16), 0)
            here(7, 8, 15)
            home_sent()

            v.low2[...] = nt(dsx, w[4, :, 0:wide]).astype(bf16)
            v.tmp[...] = nn(v.low2[...], w[3])
            home_arrive()

            def write(rows, value):
                v.low[rows, :] = value.astype(bf16)

            norm_back_into(
                v.hidden_in, 0, lambda rows: v.after_home[rows, :].astype(f32), write
            )
            fetch(16, v.low, latent_grad_ref)
            v.grads[12:14, 0:channels] = v.pixel_sums[0:2, :]
            settle_stage()
            v.tmp[0:128, :] = jnp.zeros((128, width), f32)
            v.tmp[0:16, :] = v.grads[...]
            copy = stage_out(
                2, v.tmp[0:128, :].T.astype(bf16), parts[gk_chunk].at[:, pl.ds(2 * wide, 128)]
            )
            copy.start()
            copy.wait()

        work = [(begin, None, 3)]
        for l in reversed(range(layers)):
            rest = 2 * (layers - 1 - l)
            half = heads // 2
            work += [
                (functools.partial(branch_a, l), None, 1.6),
                (functools.partial(branch_a2, l), None, 1.2),
                (functools.partial(branch_b, l), None, 1.6),
                (functools.partial(branch_b2, l), None, 1.5),
                (functools.partial(branch_c, l), rest, 2.5),
                (functools.partial(attention, l, 0, half), None, 2),
                (functools.partial(attention, l, half, heads), None, 2),
                (functools.partial(branch_d, l), None, 2),
                (functools.partial(branch_d2, l), None, 2.6),
                (functools.partial(branch_e, l), rest + 1, 3.2),
            ]
        work += [
            (cross_begin, None, 0.5),
            (cross_a, None, 2.3),
            (cross_b, None, 1.6),
            (cross_b2, c_chunk, 1.3),
            (cross_c, None, 3),
            (cross_d, None, 0.5),
        ]
        for item in range(items):
            for at in range(0, blocks, 2):
                work.append((functools.partial(cross_blocks, item, at, at + 2), None, 4.6))
            work.append((functools.partial(cross_finish, item), None, 1))
        work += [(send_dsx, None, 0.5), (home, gk_chunk, 4)]
        comm = reducer.schedule(range(chunks))
        ready, at, due = {None}, 0, 0.0
        for thunk, makes, microseconds in work:
            thunk()
            if makes is not None:
                ready.add(makes)
            if len(ready) > 1:
                due = max(due, at) + BACK_RATE * microseconds
            while at < min(due, len(comm)) and comm[at][0] in ready:
                comm[at][1]()
                at += 1
        while at < len(comm):
            comm[at][1]()
            at += 1
        v.gk_low[...] = v.gk_own[...].astype(bf16)
        for thunk in gatherer.schedule([0])[0]:
            thunk()
        out_arrive()
        out_sent()
        plane.sent("from_work", v.cv, v.cv_all, cv_sems)
        plane.sent("mp_split", pieces, v.dsx_in, dsx_sems)
        here(*list(open_copies))

    vmem = pl.BlockSpec(memory_space=pltpu.VMEM)
    fetches = (layers * (len(layer_names) + 4)) + 20
    results = pl.pallas_call(
        kernel,
        out_shape=tuple(part_types + reduced_types + other_types),
        in_specs=[ANY] * (len(ins) + 4)
        + [pl.BlockSpec(memory_space=pltpu.SMEM), vmem, vmem],
        out_specs=[ANY] * chunks + [vmem] * (chunks - 1) + [ANY] * 4,
        scratch_shapes=[pltpu.VMEM(*v_types[name]) for name in v_names]
        + Reducer.buffer_shapes(slabs, sets, line)
        + Reducer.sem_shapes(chunks, line)
        + Gatherer.sem_shapes(1, line)
        + [DMA((fetches,)), DMA((4,)), DMA((2,)), DMA((2,))]
        + [DMA((layers, 2)), DMA((layers, 2))]
        + [DMA(()), DMA((4,)), DMA((4,))] * 2
        + [DMA((2,)), DMA((2,))],
        compiler_params=pltpu.CompilerParams(
            collective_id=1, has_side_effects=True, vmem_limit_bytes=63 * 1024 * 1024
        ),
        name="backward",
    )(*ins, cotangent, result, latents, pixels, counts, pixel_gain, pixel_bias)
    return results[chunks : 2 * chunks - 1], results[2 * chunks - 1 :]


BACK_RATE = 1.2


def fast_shards(
    latents,
    pixels,
    pixel_counts,
    cross_query,
    cross_key,
    cross_value,
    cross_out,
    cross_up,
    cross_down,
    block_qkv,
    block_out,
    block_up,
    block_down,
    norm_gains,
    norm_biases,
    pixel_gain,
    pixel_bias,
    cotangent,
):
    bf16, f32 = jnp.bfloat16, jnp.float32
    line = lax.axis_size("dp") // 2
    layers, rows_d, _, cols_m = block_qkv.shape
    own_rows, width = latents.shape
    channels = pixels.shape[2]
    own_cols = cross_query.shape[1]
    pad = (-channels) % 128
    wide = channels + pad

    def lanes(v):
        return jnp.pad(v, ((0, 0), (0, pad)))

    norms = jnp.concatenate([norm_gains, norm_biases], axis=0)
    norm_count = norm_gains.shape[0]
    slab_q = jnp.concatenate(
        [
            cross_query.T,
            lanes(cross_key.T),
            lanes(cross_value.T),
            jnp.pad(norms.T, ((0, 0), (0, 128 - 2 * norm_count))),
        ],
        axis=1,
    )
    slab_c = jnp.stack([cross_up.T, cross_down.T, cross_out.T], axis=0)
    slabs_l = [
        jnp.concatenate(
            [
                jnp.swapaxes(block_qkv[l], 0, 1),
                jnp.stack([block_out[l], block_up[l], block_down[l]], axis=0),
            ],
            axis=0,
        )
        for l in range(layers)
    ]
    gain_row, bias_row = pixel_gain.astype(f32)[None], pixel_bias.astype(f32)[None]
    gathered, cotangent_work, kept = forward_kernel(
        [slab_q, slab_c] + slabs_l,
        latents,
        cotangent,
        pixels,
        pixel_counts,
        gain_row,
        bias_row,
        line,
        layers,
    )
    result_name = next(name for name in kept if name == "result")
    result = kept.pop(result_name)
    reduced, (gk_all, latent_grad, pixel_grad, latents_out) = backward_kernel(
        gathered,
        kept,
        cotangent_work,
        result,
        latents,
        pixels,
        pixel_counts,
        gain_row,
        bias_row,
        line,
        layers,
    )
    value_t = gathered[0][:, width + wide : width + wide + channels]
    g_all = gk_all[:, :channels]
    k_all = gk_all[:, wide : wide + channels]
    small = gk_all[:, 2 * wide :].astype(f32)
    at = (lax.axis_index("dp") * 4 + lax.axis_index("mp")) * own_cols
    small_own = lax.dynamic_slice_in_dim(small, at, own_cols, 0)
    k_own = lax.dynamic_slice_in_dim(k_all, at, own_cols, 0)
    out_own = lax.dynamic_slice_in_dim(gathered[1][2], at, own_cols, 1)
    rest_grads = [reduced[2 * (layers - 1 - l)] for l in range(layers)]
    qkv_grads = [reduced[2 * (layers - 1 - l) + 1] for l in range(layers)]
    qkv_out = jnp.swapaxes(jnp.stack(qkv_grads, axis=0), 1, 2)
    out_out, up_out, down_out = [jnp.stack([g[k] for g in rest_grads], axis=0) for k in range(3)]
    return (
        latents_out,
        latent_grad,
        pixel_grad,
        matmul(g_all, cross_key),
        transposed_times(g_all, cross_query),
        transposed_times(k_all, out_own),
        times_transposed(value_t, k_own),
        reduced[2 * layers][0].T,
        reduced[2 * layers][1].T,
        qkv_out,
        out_out,
        up_out,
        down_out,
        small_own[:, :norm_count].T,
        small_own[:, norm_count : 2 * norm_count].T,
        small[:channels, 2 * norm_count],
        small[:channels, 2 * norm_count + 1],
    )


def fits(mesh):
    return mesh.shape["mp"] == 4 and mesh.shape["dp"] % 2 == 0


def solution(mesh):
    return jax.shard_map(
        fast_shards if fits(mesh) else shards,
        mesh=mesh,
        in_specs=(
            P(("dp", "mp"), None),
            P("dp", "mp", None),
            P("dp"),
            P(None, ("dp", "mp")),
            P(None, ("dp", "mp")),
            P(None, ("dp", "mp")),
            P(None, ("dp", "mp")),
            P(None, ("dp", "mp")),
            P(None, ("dp", "mp")),
            P(None, "dp", None, "mp"),
            P(None, "dp", "mp"),
            P(None, "dp", "mp"),
            P(None, "dp", "mp"),
            P(None, ("dp", "mp")),
            P(None, ("dp", "mp")),
            P(),
            P(),
            P(("dp", "mp"), None),
        ),
        out_specs=(
            P(("dp", "mp"), None),
            P(("dp", "mp"), None),
            P("dp", "mp", None),
            P(None, ("dp", "mp")),
            P(None, ("dp", "mp")),
            P(None, ("dp", "mp")),
            P(None, ("dp", "mp")),
            P(None, ("dp", "mp")),
            P(None, ("dp", "mp")),
            P(None, "dp", None, "mp"),
            P(None, "dp", "mp"),
            P(None, "dp", "mp"),
            P(None, "dp", "mp"),
            P(None, ("dp", "mp")),
            P(None, ("dp", "mp")),
            P(),
            P(),
        ),
        check_vma=False,
    )
```

```python
import functools
import math
import types

import ml_dtypes

import jax
import jax.numpy as jnp
from jax import lax
from jax.experimental import pallas as pl
from jax.experimental.pallas import tpu as pltpu
from jax.sharding import PartitionSpec as P

HD = 128


norm_eps = 1e-05
masked_score = -1e30


def joined(value, axis, join):
    pieces = jax.tree.map(lambda part: lax.all_gather(part, axis), value)
    head = jax.tree.map(lambda part: part[0], pieces)
    tail = jax.tree.map(lambda part: part[1:], pieces)
    running, _ = lax.scan(lambda running, share: (join(running, share), None), head, tail)
    return running


def layer_norm(features, gain_row, offset):
    average = jnp.mean(features, axis=-1, keepdims=True)
    centered = features - average
    variance = jnp.mean(centered * centered, axis=-1, keepdims=True)
    return centered * lax.rsqrt(variance + norm_eps) * gain_row + offset


def norm_back(features, gain_row, offset, upstream):
    _, pullback = jax.vjp(layer_norm, features, gain_row, offset)
    return pullback(upstream)


def gelu_back(hidden, upstream):
    _, pullback = jax.vjp(jax.nn.gelu, hidden)
    return pullback(upstream)[0]


def matmul(left_side, right_side):
    return jnp.dot(left_side, right_side, preferred_element_type=jnp.float32)


def times_transposed(left_side, right_side):
    return lax.dot_general(
        left_side, right_side, (((1,), (1,)), ((), ())), preferred_element_type=jnp.float32
    )


def transposed_times(left_side, right_side):
    return lax.dot_general(
        left_side, right_side, (((0,), (0,)), ((), ())), preferred_element_type=jnp.float32
    )


def gather_rows(payload):
    return lax.all_gather(payload, "mp", axis=0, tiled=True)


def gather_grads(payload):
    return lax.all_gather(payload, "mp", axis=0, tiled=True)


def sum_branch(row_term, own_rows):
    return lax.psum_scatter(
        row_term(jnp.int32(0), own_rows * lax.axis_size("mp")).astype(jnp.bfloat16),
        "mp",
        scatter_dimension=0,
        tiled=True,
    ).astype(jnp.float32)


def sum_inputs(row_term, own_rows):
    return lax.psum_scatter(
        row_term(jnp.int32(0), own_rows * lax.axis_size("mp")).astype(jnp.bfloat16),
        "mp",
        scatter_dimension=0,
        tiled=True,
    ).astype(jnp.float32)


def slicer(source):

    def row_term(first_row, row_count):
        return source

    return row_term


def product_term(source, weight, formula):

    def row_term(first_row, row_count):
        return jnp.einsum(formula, source, weight, preferred_element_type=jnp.float32)

    return row_term


def merge_stats(earlier, latter):
    row_top = jnp.maximum(earlier[0], latter[0])
    return (
        row_top,
        earlier[1] * jnp.exp(earlier[0] - row_top) + latter[1] * jnp.exp(latter[0] - row_top),
    )


def cross_params(
    cross_query, cross_key, cross_value, cross_out, cross_up, cross_down, norm_gains, norm_biases
):
    return (
        lax.all_gather(cross_query, ("dp", "mp"), axis=1, tiled=True),
        lax.all_gather(cross_key, ("dp", "mp"), axis=1, tiled=True),
        lax.all_gather(cross_value, ("dp", "mp"), axis=1, tiled=True),
        lax.all_gather(cross_out, ("dp", "mp"), axis=1, tiled=True),
        lax.all_gather(cross_up, ("dp", "mp"), axis=1, tiled=True),
        lax.all_gather(cross_down, ("dp", "mp"), axis=1, tiled=True),
        lax.all_gather(norm_gains, ("dp", "mp"), axis=1, tiled=True),
        lax.all_gather(norm_biases, ("dp", "mp"), axis=1, tiled=True),
    )


def block_weights(block_qkv, block_out, block_up, block_down, layer_index):
    return (
        lax.all_gather(block_qkv[layer_index], "dp", axis=0, tiled=True),
        lax.all_gather(block_out[layer_index], "dp", axis=0, tiled=True),
        lax.all_gather(block_up[layer_index], "dp", axis=0, tiled=True),
        lax.all_gather(block_down[layer_index], "dp", axis=0, tiled=True),
    )


def block_forward(current, layer_index, gain_rows, bias_rows, block_params, item_count):
    qkv_weight, out_weight, up_weight, down_weight = block_weights(
        block_params[0], block_params[1], block_params[2], block_params[3], layer_index
    )
    own_rows = current.shape[0]
    group_rows = own_rows * lax.axis_size("mp")
    latents_item = group_rows // item_count
    head_cols = qkv_weight.shape[2]
    heads_local = head_cols // HD
    block_scale = 1.0 / math.sqrt(HD)
    normed = layer_norm(
        current, gain_rows[2 + 2 * layer_index], bias_rows[2 + 2 * layer_index]
    ).astype(jnp.bfloat16)
    normed_group = gather_rows(normed)
    projected = jnp.einsum(
        "rd,dtk->rtk", normed_group, qkv_weight, preferred_element_type=jnp.float32
    ).astype(jnp.bfloat16)
    heads_view = projected.reshape(item_count, latents_item, 3, heads_local, HD)
    raw_scores = (
        jnp.einsum(
            "iqhe,ikhe->ihqk",
            heads_view[:, :, 0],
            heads_view[:, :, 1],
            preferred_element_type=jnp.float32,
        )
        * block_scale
    )
    row_top = jnp.max(raw_scores, axis=-1, keepdims=True)
    lifted = jnp.exp(raw_scores - row_top)
    row_total = jnp.sum(lifted, axis=-1, keepdims=True)
    attention = lifted / row_total
    log_total = row_top + jnp.log(row_total)
    context = jnp.einsum(
        "ihqk,ikhe->iqhe",
        attention.astype(jnp.bfloat16),
        heads_view[:, :, 2],
        preferred_element_type=jnp.float32,
    )
    context = context.astype(jnp.bfloat16).reshape(group_rows, head_cols)
    middle = current + sum_branch(product_term(context, out_weight, "rk,dk->rd"), own_rows)
    hidden_in = layer_norm(
        middle, gain_rows[3 + 2 * layer_index], bias_rows[3 + 2 * layer_index]
    ).astype(jnp.bfloat16)
    hidden_group = gather_rows(hidden_in)
    hidden = matmul(hidden_group, up_weight)
    active = jax.nn.gelu(hidden).astype(jnp.bfloat16)
    result = middle + sum_branch(product_term(active, down_weight, "rf,df->rd"), own_rows)
    stored = (
        qkv_weight,
        out_weight,
        up_weight,
        down_weight,
        normed_group,
        projected,
        log_total,
        context,
        middle,
        hidden_group,
        hidden,
        active,
    )
    return (result, stored)


def block_backward(upstream, current, layer_index, gain_rows, bias_rows, stored, item_count):
    (
        qkv_weight,
        out_weight,
        up_weight,
        down_weight,
        normed_group,
        projected,
        log_total,
        context,
        middle,
        hidden_group,
        hidden,
        active,
    ) = stored
    own_rows = upstream.shape[0]
    group_rows = own_rows * lax.axis_size("mp")
    latents_item = group_rows // item_count
    head_cols = qkv_weight.shape[2]
    heads_local = head_cols // HD
    block_scale = 1.0 / math.sqrt(HD)
    down_group = gather_grads(upstream.astype(jnp.bfloat16))
    down_grad = transposed_times(down_group, active)
    active_cot = matmul(down_group, down_weight)
    hidden_cot = gelu_back(hidden, active_cot).astype(jnp.bfloat16)
    up_grad = transposed_times(hidden_group, hidden_cot)
    hidden_in_cot = sum_inputs(product_term(hidden_cot, up_weight, "rf,df->rd"), own_rows)
    middle_cot, gain_late, bias_late = norm_back(
        middle, gain_rows[3 + 2 * layer_index], bias_rows[3 + 2 * layer_index], hidden_in_cot
    )
    middle_cot = middle_cot + upstream
    out_group = gather_grads(middle_cot.astype(jnp.bfloat16))
    out_grad = transposed_times(out_group, context)
    context_cot = (
        matmul(out_group, out_weight)
        .astype(jnp.bfloat16)
        .reshape(item_count, latents_item, heads_local, HD)
    )
    heads_view = projected.reshape(item_count, latents_item, 3, heads_local, HD)
    queries = heads_view[:, :, 0]
    key_rows = heads_view[:, :, 1]
    value_rows = heads_view[:, :, 2]
    raw_scores = (
        jnp.einsum("iqhe,ikhe->ihqk", queries, key_rows, preferred_element_type=jnp.float32)
        * block_scale
    )
    attention = jnp.exp(raw_scores - log_total)
    value_cot = jnp.einsum(
        "ihqk,iqhe->ikhe",
        attention.astype(jnp.bfloat16),
        context_cot,
        preferred_element_type=jnp.float32,
    )
    prob_cot = jnp.einsum(
        "iqhe,ikhe->ihqk", context_cot, value_rows, preferred_element_type=jnp.float32
    )
    row_terms = jnp.sum(attention * prob_cot, axis=-1, keepdims=True)
    score_cot = (attention * (prob_cot - row_terms) * block_scale).astype(jnp.bfloat16)
    query_cot = jnp.einsum(
        "ihqk,ikhe->iqhe", score_cot, key_rows, preferred_element_type=jnp.float32
    )
    key_cot = jnp.einsum("ihqk,iqhe->ikhe", score_cot, queries, preferred_element_type=jnp.float32)
    projected_cot = jnp.stack(
        [
            query_cot.astype(jnp.bfloat16),
            key_cot.astype(jnp.bfloat16),
            value_cot.astype(jnp.bfloat16),
        ],
        axis=2,
    )
    projected_cot = projected_cot.reshape(group_rows, 3, head_cols)
    qkv_grad = jnp.einsum(
        "rd,rtk->dtk", normed_group, projected_cot, preferred_element_type=jnp.float32
    )
    normed_cot = sum_inputs(product_term(projected_cot, qkv_weight, "rtk,dtk->rd"), own_rows)
    input_cot, gain_early, bias_early = norm_back(
        current, gain_rows[2 + 2 * layer_index], bias_rows[2 + 2 * layer_index], normed_cot
    )
    input_cot = input_cot + middle_cot
    summed = (
        lax.psum_scatter(
            qkv_grad.astype(jnp.bfloat16), "dp", scatter_dimension=0, tiled=True
        ).astype(jnp.float32),
        lax.psum_scatter(
            out_grad.astype(jnp.bfloat16), "dp", scatter_dimension=0, tiled=True
        ).astype(jnp.float32),
        lax.psum_scatter(
            up_grad.astype(jnp.bfloat16), "dp", scatter_dimension=0, tiled=True
        ).astype(jnp.float32),
        lax.psum_scatter(
            down_grad.astype(jnp.bfloat16), "dp", scatter_dimension=0, tiled=True
        ).astype(jnp.float32),
    )
    return (input_cot, summed, (gain_early, bias_early, gain_late, bias_late))


def shards(
    latents,
    pixels,
    pixel_counts,
    cross_query,
    cross_key,
    cross_value,
    cross_out,
    cross_up,
    cross_down,
    block_qkv,
    block_out,
    block_up,
    block_down,
    norm_gains,
    norm_biases,
    pixel_gain,
    pixel_bias,
    cotangent,
):
    layers = block_qkv.shape[0]
    item_count = pixels.shape[0]
    pixel_rows = pixels.shape[1]
    own_rows = latents.shape[0]
    model_width = latents.shape[1]
    group_rows = own_rows * lax.axis_size("mp")
    latents_item = group_rows // item_count
    cross_scale = 1.0 / math.sqrt(model_width)
    block_params = (block_qkv, block_out, block_up, block_down)
    forward_params = cross_params(
        cross_query,
        cross_key,
        cross_value,
        cross_out,
        cross_up,
        cross_down,
        norm_gains,
        norm_biases,
    )
    (
        query_weight,
        key_weight,
        value_weight,
        out_weight,
        up_weight,
        down_weight,
        gain_table,
        bias_table,
    ) = forward_params
    gain_rows = gain_table.astype(jnp.float32)
    bias_rows = bias_table.astype(jnp.float32)
    start_rows = latents.astype(jnp.float32)
    query_in = layer_norm(start_rows, gain_rows[0], bias_rows[0]).astype(jnp.bfloat16)
    query_own = matmul(query_in, query_weight).astype(jnp.bfloat16)
    query_group = gather_rows(query_own).reshape(item_count, latents_item, model_width)
    pixel_floats = pixels.astype(jnp.float32)
    pixel_gain_row = pixel_gain.astype(jnp.float32)
    pixel_bias_row = pixel_bias.astype(jnp.float32)
    pixel_in = layer_norm(pixel_floats, pixel_gain_row, pixel_bias_row).astype(jnp.bfloat16)
    pair_weight = jnp.concatenate([key_weight, value_weight], axis=1)
    pair_rows = jnp.einsum(
        "ipc,cd->ipd", pixel_in, pair_weight, preferred_element_type=jnp.float32
    ).astype(jnp.bfloat16)
    key_rows = pair_rows[:, :, :model_width]
    value_rows = pair_rows[:, :, model_width:]
    positions = lax.axis_index("mp") * pixel_rows + jnp.arange(pixel_rows, dtype=jnp.int32)
    present = positions[None, :] < pixel_counts[:, None]
    present_mask = present.astype(jnp.float32)[:, None, :]

    def cross_scores():
        raw_scores = (
            jnp.einsum("iqd,ipd->iqp", query_group, key_rows, preferred_element_type=jnp.float32)
            * cross_scale
        )
        return jnp.where(present[:, None, :], raw_scores, masked_score)

    scores = cross_scores()
    local_top = jnp.max(scores, axis=-1)
    local_total = jnp.sum(jnp.exp(scores - local_top[:, :, None]) * present_mask, axis=-1)
    group_top, group_total = joined((local_top, local_total), "mp", merge_stats)
    log_total = (group_top + jnp.log(group_total))[:, :, None]
    attention = jnp.exp(scores - log_total) * present_mask
    attended = jnp.einsum(
        "iqp,ipd->iqd",
        attention.astype(jnp.bfloat16),
        value_rows,
        preferred_element_type=jnp.float32,
    )
    attended = attended.reshape(group_rows, model_width)
    context_own = sum_branch(slicer(attended), own_rows).astype(jnp.bfloat16)
    after_cross = start_rows + matmul(context_own, out_weight)
    cross_hidden_in = layer_norm(after_cross, gain_rows[1], bias_rows[1]).astype(jnp.bfloat16)
    cross_hidden = matmul(cross_hidden_in, up_weight)
    cross_active = jax.nn.gelu(cross_hidden).astype(jnp.bfloat16)
    current = after_cross + matmul(cross_active, down_weight)
    inputs_kept = []
    stored_all = []
    for layer_index in range(layers):
        inputs_kept.append(current)
        current, stored = block_forward(
            current, layer_index, gain_rows, bias_rows, block_params, item_count
        )
        stored_all.append(stored)
    latents_out = current.astype(jnp.bfloat16)
    later_params = cross_params(
        cross_query,
        cross_key,
        cross_value,
        cross_out,
        cross_up,
        cross_down,
        norm_gains,
        norm_biases,
    )
    (
        query_weight,
        key_weight,
        value_weight,
        out_weight,
        up_weight,
        down_weight,
        gain_table,
        bias_table,
    ) = later_params
    gain_rows = gain_table.astype(jnp.float32)
    bias_rows = bias_table.astype(jnp.float32)
    gain_parts = [None] * (2 * layers + 2)
    bias_parts = [None] * (2 * layers + 2)
    qkv_grads = [None] * layers
    out_grads = [None] * layers
    up_grads = [None] * layers
    down_grads = [None] * layers
    current_cot = cotangent.astype(jnp.float32)
    for layer_index in reversed(range(layers)):
        _, stored = block_forward(
            inputs_kept[layer_index], layer_index, gain_rows, bias_rows, block_params, item_count
        )
        current_cot, summed, norm_parts = block_backward(
            current_cot,
            inputs_kept[layer_index],
            layer_index,
            gain_rows,
            bias_rows,
            stored,
            item_count,
        )
        qkv_grads[layer_index] = summed[0]
        out_grads[layer_index] = summed[1]
        up_grads[layer_index] = summed[2]
        down_grads[layer_index] = summed[3]
        gain_parts[2 + 2 * layer_index] = norm_parts[0]
        bias_parts[2 + 2 * layer_index] = norm_parts[1]
        gain_parts[3 + 2 * layer_index] = norm_parts[2]
        bias_parts[3 + 2 * layer_index] = norm_parts[3]
    down_in = current_cot.astype(jnp.bfloat16)
    cross_down_grad = transposed_times(cross_active, down_in)
    active_cot = times_transposed(down_in, down_weight)
    hidden_cot = gelu_back(cross_hidden, active_cot).astype(jnp.bfloat16)
    cross_up_grad = transposed_times(cross_hidden_in, hidden_cot)
    hidden_in_cot = times_transposed(hidden_cot, up_weight)
    after_cot, gain_parts[1], bias_parts[1] = norm_back(
        after_cross, gain_rows[1], bias_rows[1], hidden_in_cot
    )
    after_cot = after_cot + current_cot
    out_in = after_cot.astype(jnp.bfloat16)
    cross_out_grad = transposed_times(context_own, out_in)
    context_cot = times_transposed(out_in, out_weight).astype(jnp.bfloat16)
    context_group = gather_grads(context_cot).reshape(item_count, latents_item, model_width)
    scores = cross_scores()
    attention = jnp.exp(scores - log_total) * present_mask
    value_cot = jnp.einsum(
        "iqp,iqd->ipd",
        attention.astype(jnp.bfloat16),
        context_group,
        preferred_element_type=jnp.float32,
    ).astype(jnp.bfloat16)
    prob_cot = jnp.einsum(
        "iqd,ipd->iqp", context_group, value_rows, preferred_element_type=jnp.float32
    )
    row_part = jnp.sum(attention * prob_cot, axis=-1)
    row_terms = lax.psum(row_part, "mp")
    score_cot = (attention * (prob_cot - row_terms[:, :, None]) * cross_scale).astype(jnp.bfloat16)
    query_part = jnp.einsum(
        "iqp,ipd->iqd", score_cot, key_rows, preferred_element_type=jnp.float32
    ).reshape(group_rows, model_width)
    query_cot = sum_inputs(slicer(query_part), own_rows).astype(jnp.bfloat16)
    key_cot = jnp.einsum(
        "iqp,iqd->ipd", score_cot, query_group, preferred_element_type=jnp.float32
    ).astype(jnp.bfloat16)
    cross_query_grad = transposed_times(query_in, query_cot)
    query_in_cot = times_transposed(query_cot, query_weight)
    start_cot, gain_parts[0], bias_parts[0] = norm_back(
        start_rows, gain_rows[0], bias_rows[0], query_in_cot
    )
    latent_grad = (start_cot + after_cot).astype(jnp.bfloat16)
    pair_weight = jnp.concatenate([key_weight, value_weight], axis=1)
    pair_cot = jnp.concatenate([key_cot, value_cot], axis=2)
    pair_grad = jnp.einsum("ipc,ipd->cd", pixel_in, pair_cot, preferred_element_type=jnp.float32)
    cross_key_grad = pair_grad[:, :model_width]
    cross_value_grad = pair_grad[:, model_width:]
    pixel_in_cot = jnp.einsum(
        "ipd,cd->ipc", pair_cot, pair_weight, preferred_element_type=jnp.float32
    )
    pixel_cot, pixel_gain_part, pixel_bias_part = norm_back(
        pixel_floats, pixel_gain_row, pixel_bias_row, pixel_in_cot
    )
    pixel_grad = pixel_cot.astype(jnp.bfloat16)
    gain_stack = jnp.stack(gain_parts, axis=0)
    bias_stack = jnp.stack(bias_parts, axis=0)
    cross_summed = (
        lax.psum_scatter(cross_query_grad, ("dp", "mp"), scatter_dimension=1, tiled=True),
        lax.psum_scatter(cross_key_grad, ("dp", "mp"), scatter_dimension=1, tiled=True),
        lax.psum_scatter(cross_value_grad, ("dp", "mp"), scatter_dimension=1, tiled=True),
        lax.psum_scatter(cross_out_grad, ("dp", "mp"), scatter_dimension=1, tiled=True),
        lax.psum_scatter(cross_up_grad, ("dp", "mp"), scatter_dimension=1, tiled=True),
        lax.psum_scatter(cross_down_grad, ("dp", "mp"), scatter_dimension=1, tiled=True),
        lax.psum_scatter(gain_stack, ("dp", "mp"), scatter_dimension=1, tiled=True),
        lax.psum_scatter(bias_stack, ("dp", "mp"), scatter_dimension=1, tiled=True),
    )
    pixel_gain_grad, pixel_bias_grad = lax.psum((pixel_gain_part, pixel_bias_part), ("dp", "mp"))
    return (
        latents_out,
        latent_grad,
        pixel_grad,
        cross_summed[0],
        cross_summed[1],
        cross_summed[2],
        cross_summed[3],
        cross_summed[4],
        cross_summed[5],
        jnp.stack(qkv_grads, axis=0),
        jnp.stack(out_grads, axis=0),
        jnp.stack(up_grads, axis=0),
        jnp.stack(down_grads, axis=0),
        cross_summed[6],
        cross_summed[7],
        pixel_gain_grad,
        pixel_bias_grad,
    )


MESH_ID = pl.DeviceIdType.MESH
ANY = pl.BlockSpec(memory_space=pl.ANY)
DMA = pltpu.SemaphoreType.DMA


def place():
    dp = lax.axis_index("dp")
    mp = lax.axis_index("mp")
    return dp, mp, dp // 2, dp % 2, mp // 2, mp % 2


def greet(targets):
    barrier = pltpu.get_barrier_semaphore()
    for device, condition in targets:

        def signal(device=device):
            pl.semaphore_signal(barrier, inc=1, device_id=device, device_id_type=MESH_ID)

        if condition is None:
            signal()
        else:
            pl.when(condition)(signal)
    fixed = sum(1 for _, condition in targets if condition is None)
    varying = [condition.astype(jnp.int32) for _, condition in targets if condition is not None]
    pl.semaphore_wait(barrier, sum(varying, fixed))


def remote(source, target, send, recv, device):
    return pltpu.make_async_remote_copy(
        src_ref=source,
        dst_ref=target,
        send_sem=send,
        recv_sem=recv,
        device_id=device,
        device_id_type=MESH_ID,
    )


def when(condition, action):
    if condition is None:
        action()
    else:
        pl.when(condition)(action)


def both(first, second):
    if first is None:
        return second
    if second is None:
        return first
    return jnp.logical_and(first, second)


def slab_of(ref, slab, dp, mp):
    rows, columns = slab[-2:]
    if columns == ref.shape[-1]:
        at = pl.ds(pl.multiple_of((dp * 4 + mp) * rows, rows), rows)
        return ref.at[at] if len(ref.shape) == 2 else ref.at[:, at]
    return ref.at[
        :,
        pl.ds(pl.multiple_of(dp * rows, rows), rows),
        pl.ds(pl.multiple_of(mp * columns, columns), columns),
    ]


class Gatherer:
    def __init__(self, line, slabs, outs, sems):
        self.line = line
        self.slabs = slabs
        self.outs = outs
        self.on_unit = None
        (
            self.own_sem,
            self.line_send,
            self.line_recv,
            self.plane_send,
            self.plane_recv,
            self.pass_send,
            self.pass_recv,
            self.core_send,
            self.core_recv,
        ) = sems
        self.dp, self.mp, self.z, self.core, self.y, self.x = place()

    @staticmethod
    def sem_shapes(chunks, line):
        return [
            DMA((chunks,)),
            DMA((chunks, line, 2)),
            DMA((chunks, line)),
            DMA((chunks, line, 2)),
            DMA((chunks, line, 2)),
            DMA((chunks, line, 2)),
            DMA((chunks, line, 2)),
            DMA((chunks, line, 4)),
            DMA((chunks, line, 4)),
        ]

    def partners(self):
        z = self.z
        return [
            ((self.dp + 2, self.mp), z < self.line - 1),
            ((self.dp - 2, self.mp), z > 0),
            ((self.dp, self.mp ^ 1), None),
            ((self.dp, self.mp ^ 2), None),
            ((self.dp ^ 1, self.mp), None),
        ]

    def slot(self, chunk, z, core, mp):
        return slab_of(self.outs[chunk], self.slabs[chunk].shape, 2 * z + core, mp)

    @staticmethod
    def halves(ref):
        rows = ref.shape[-2] // 2
        if len(ref.shape) == 3:
            return ref.at[:, pl.ds(0, rows)], ref.at[:, pl.ds(rows, rows)]
        return ref.at[pl.ds(0, rows)], ref.at[pl.ds(rows, rows)]

    def line_copy(self, chunk, z, way, source=None):
        slot = self.slot(chunk, z, self.core, self.mp)
        step = 2 if way == 0 else -2
        return remote(
            slot if source is None else source,
            slot,
            self.line_send.at[chunk, z, way],
            self.line_recv.at[chunk, z],
            (self.dp + step, self.mp),
        )

    def plane_copy(self, chunk, z, way, source=None):
        slot = self.slot(chunk, z, self.core, self.mp)
        return remote(
            slot if source is None else source,
            slot,
            self.plane_send.at[chunk, z, way],
            self.plane_recv.at[chunk, z, way],
            (self.dp, self.mp ^ (1 if way == 0 else 2)),
        )

    def pass_copy(self, chunk, z, way):
        slot = self.slot(chunk, z, self.core, self.mp ^ (1 if way == 0 else 2))
        half = self.halves(slot)[way]
        return remote(
            half,
            half,
            self.pass_send.at[chunk, z, way],
            self.pass_recv.at[chunk, z, way],
            (self.dp, self.mp ^ (2 if way == 0 else 1)),
        )

    def core_copy(self, chunk, z, mp, turn):
        slot = self.slot(chunk, z, self.core, mp)
        return remote(
            slot,
            slot,
            self.core_send.at[chunk, z, turn],
            self.core_recv.at[chunk, z, turn],
            (self.dp ^ 1, self.mp),
        )

    def arrivals(self):
        z = self.z
        order = [(z, None, None)]
        for distance in range(1, self.line):
            order.append((z - distance, z >= distance, 0))
            order.append((z + distance, z + distance < self.line, 1))
        return order

    def own_copy(self, chunk):
        return pltpu.make_async_copy(
            self.slabs[chunk], self.slot(chunk, self.z, self.core, self.mp), self.own_sem.at[chunk]
        )

    def can_pass(self, way):
        return self.z < self.line - 1 if way == 0 else self.z > 0

    def begin(self, chunk):
        self.own_copy(chunk).start()
        slab = self.slabs[chunk]
        for way in (0, 1):
            when(
                self.can_pass(way),
                lambda way=way: self.line_copy(chunk, self.z, way, slab).start(),
            )
        for way in (0, 1):
            self.plane_copy(chunk, self.z, way, slab).start()

    def stage_line(self, chunk, turn):
        if turn == 0:
            self.begin(chunk)
            return
        z, condition, way = self.arrivals()[turn]

        def act():
            self.line_copy(chunk, z, way).wait_recv()
            when(self.can_pass(way), lambda: self.line_copy(chunk, z, way).start())
            for plane_way in (0, 1):
                self.plane_copy(chunk, z, plane_way).start()

        when(condition, act)

    def stage_plane(self, chunk, turn):
        z, condition, _ = self.arrivals()[turn]

        def act():
            for way in (0, 1):
                self.plane_copy(chunk, z, way).wait_recv()
                self.pass_copy(chunk, z, way).start()
            if turn == 0:
                self.own_copy(chunk).wait()
            self.core_copy(chunk, z, self.mp, 0).start()
            self.core_copy(chunk, z, self.mp ^ 1, 1).start()
            self.core_copy(chunk, z, self.mp ^ 2, 2).start()

        when(condition, act)

    def stage_pass(self, chunk, turn):
        z, condition, _ = self.arrivals()[turn]

        def act():
            for way in (0, 1):
                self.pass_copy(chunk, z, way).wait_recv()
            self.core_copy(chunk, z, self.mp ^ 3, 3).start()

        when(condition, act)

    def stage_core(self, chunk, turn):
        z, condition, _ = self.arrivals()[turn]

        def act():
            for piece in range(4):
                self.core_copy(chunk, z, self.mp, piece).wait_recv()
            if self.on_unit is not None:
                self.on_unit(chunk, z)

        when(condition, act)

    def drain(self, chunk):
        for turn, (z, condition, way) in enumerate(self.arrivals()):

            def act(turn=turn, z=z, way=way):
                if turn == 0:
                    for own_way in (0, 1):
                        when(
                            self.can_pass(own_way),
                            lambda own_way=own_way: self.line_copy(
                                chunk, z, own_way, self.slabs[chunk]
                            ).wait_send(),
                        )
                else:
                    when(self.can_pass(way), lambda: self.line_copy(chunk, z, way).wait_send())
                for plane_way in (0, 1):
                    self.plane_copy(chunk, z, plane_way).wait_send()
                    self.pass_copy(chunk, z, plane_way).wait_send()
                for piece in range(4):
                    self.core_copy(chunk, z, self.mp, piece).wait_send()

            when(condition, act)

    def schedule(self, chunks, lag=2):
        turns = 2 * self.line - 1
        units = [(chunk, turn) for chunk in chunks for turn in range(turns)]
        todo, marks = [], {}
        for at in range(len(units) + 3 * lag):
            for stage, late in (
                (self.stage_line, 0),
                (self.stage_plane, lag),
                (self.stage_pass, 2 * lag),
                (self.stage_core, 3 * lag),
            ):
                if 0 <= at - late < len(units):
                    todo.append(functools.partial(stage, *units[at - late]))
                    if late == 3 * lag:
                        marks[units[at - late][0]] = len(todo)
        for chunk in chunks:
            todo.append(functools.partial(self.drain, chunk))
        return todo, marks


class Reducer:
    def __init__(self, line, parts, slabs, outs, sets, buffers, sems):
        self.line = line
        self.parts = parts
        self.slabs = slabs
        self.outs = outs
        self.sets = sets
        count, shapes = len(set(sets)), sorted(set(slabs))
        self.core_in, buffers = buffers[:count], buffers[count:]
        self.own_in, buffers = buffers[: len(shapes)], buffers[len(shapes) :]
        self.own_at = [shapes.index(slab) for slab in slabs]
        self.pass_in, self.plane_in, self.line_in = (
            buffers[kind * count : (kind + 1) * count] for kind in range(3)
        )
        (
            self.own_sem,
            self.core_send,
            self.core_recv,
            self.pass_send,
            self.pass_recv,
            self.plane_send,
            self.plane_recv,
            self.line_send,
            self.line_recv,
            self.free,
        ) = sems
        self.dp, self.mp, self.z, self.core, self.y, self.x = place()

    @staticmethod
    def buffer_shapes(slabs, sets, line):
        firsts = [sets.index(s) for s in sorted(set(sets))]

        def buffers(lead, halve=False):
            found = []
            for at in firsts:
                slab = list(slabs[at])
                if halve:
                    slab[-2] //= 2
                found.append(pltpu.VMEM(lead + tuple(slab), jnp.bfloat16))
            return found

        def own_buffers():
            return [pltpu.VMEM((4,) + tuple(s), jnp.bfloat16) for s in sorted(set(slabs))]

        return (
            buffers((line, 4))
            + own_buffers()
            + buffers((line, 2), True)
            + buffers((line, 2))
            + buffers((line + 1,))
        )

    @staticmethod
    def sem_shapes(chunks, line):
        return (
            [DMA((chunks, 4)), DMA((chunks, line, 4)), DMA((chunks, line, 4))]
            + [DMA((chunks, line, 2))] * 6
            + [pltpu.SemaphoreType.REGULAR((5,))]
        )

    halves = staticmethod(Gatherer.halves)

    def part(self, chunk, z, core, mp):
        return slab_of(self.parts[chunk], self.slabs[chunk], 2 * z + core, mp)

    def core_copy(self, chunk, z, mp):
        return remote(
            self.part(chunk, z, 1 - self.core, mp),
            self.core_in[self.sets[chunk]].at[z, mp],
            self.core_send.at[chunk, z, mp],
            self.core_recv.at[chunk, z, mp],
            (self.dp ^ 1, self.mp),
        )

    def own_copy(self, chunk, z, mp):
        return pltpu.make_async_copy(
            self.part(chunk, z, self.core, mp),
            self.own_in[self.own_at[chunk]].at[mp],
            self.own_sem.at[chunk, mp],
        )

    def pass_copy(self, chunk, z, way):
        half = self.halves(self.core_in[self.sets[chunk]].at[z, self.mp ^ 3])[way]
        return remote(
            half,
            self.pass_in[self.sets[chunk]].at[z, way],
            self.pass_send.at[chunk, z, way],
            self.pass_recv.at[chunk, z, way],
            (self.dp, self.mp ^ (2 if way == 0 else 1)),
        )

    def plane_copy(self, chunk, z, way):
        mate = self.mp ^ (1 if way == 0 else 2)
        return remote(
            self.core_in[self.sets[chunk]].at[z, mate],
            self.plane_in[self.sets[chunk]].at[z, way],
            self.plane_send.at[chunk, z, way],
            self.plane_recv.at[chunk, z, way],
            (self.dp, mate),
        )

    def line_copy(self, chunk, z, way, slot):
        return remote(
            self.core_in[self.sets[chunk]].at[z, self.mp],
            self.line_in[self.sets[chunk]].at[slot],
            self.line_send.at[chunk, z, way],
            self.line_recv.at[chunk, z, way],
            (self.dp + (-2 if way == 0 else 2), self.mp),
        )

    @classmethod
    def add(cls, target, sources, result=None):
        if len(target.shape) == 3:
            for at in range(target.shape[0]):
                cls.add(
                    target.at[at],
                    [source.at[at] for source in sources],
                    None if result is None else result.at[at],
                )
            return

        def body(rows):
            if result is None and len(sources) == 1:
                target[rows, :] = target[rows, :] + sources[0][rows, :]
                return
            total = target[rows, :].astype(jnp.float32)
            for source in sources:
                total = total + source[rows, :].astype(jnp.float32)
            if result is None:
                target[rows, :] = total.astype(jnp.bfloat16)
            else:
                result[rows, :] = total

        rows = target.shape[0]
        loop(rows, min(rows, 64 * 256 // target.shape[1] // 16 * 16), body)

    def order(self):
        low, high, found = 0, self.line - 1, []
        while low <= high:
            found.append(low)
            if high != low:
                found.append(high)
            low, high = low + 1, high - 1
        return found

    def neighbours(self):
        return [
            ((self.dp ^ 1, self.mp), None, 0, 0),
            ((self.dp, self.mp ^ 1), None, 1, 1),
            ((self.dp, self.mp ^ 2), None, 2, 2),
            ((self.dp + 2, self.mp), self.z < self.line - 1, 4, 3),
            ((self.dp - 2, self.mp), self.z > 0, 3, 4),
        ]

    def stage_begin(self, chunk, z, wait):
        if wait:
            for device, condition, theirs, mine in self.neighbours():
                when(condition, lambda mine=mine: pl.semaphore_wait(self.free.at[mine], 1))
        for mp in range(4):
            self.core_copy(chunk, z, mp).start()

    def stage_own(self, chunk, z):
        for mp in range(4):
            self.own_copy(chunk, z, mp).start()

    def stage_core(self, chunk, z):
        for mp in range(4):
            self.core_copy(chunk, z, mp).wait_recv()
            self.own_copy(chunk, z, mp).wait()
            self.add(
                self.core_in[self.sets[chunk]].at[z, mp], [self.own_in[self.own_at[chunk]].at[mp]]
            )
        for way in (0, 1):
            self.pass_copy(chunk, z, way).start()

    def stage_pass(self, chunk, z):
        for way in (0, 1):
            self.pass_copy(chunk, z, way).wait_recv()
            mate = self.mp ^ (1 if way == 0 else 2)
            self.add(
                self.halves(self.core_in[self.sets[chunk]].at[z, mate])[way],
                [self.pass_in[self.sets[chunk]].at[z, way]],
            )
            self.plane_copy(chunk, z, way).start()

    def stage_plane(self, chunk, z):
        for way in (0, 1):
            self.plane_copy(chunk, z, way).wait_recv()
        plane_in = self.plane_in[self.sets[chunk]]
        self.add(
            self.core_in[self.sets[chunk]].at[z, self.mp],
            [plane_in.at[z, 0], plane_in.at[z, 1]],
        )
        last = self.line - 1
        if z < last:
            when(self.z == last, lambda: self.line_copy(chunk, z, 0, z).start())
        if z > 0:
            when(self.z == 0, lambda: self.send_up(chunk, z))

    def send_up(self, chunk, z):
        slot = jnp.where(self.z + 1 == z, self.line, z)
        self.line_copy(chunk, z, 1, slot).start()

    def stage_line(self, chunk, z, hop):
        last = self.line - 1
        line_in = self.line_in[self.sets[chunk]]
        mine = self.core_in[self.sets[chunk]].at[z, self.mp]

        def join(way):
            self.line_copy(chunk, z, way, z).wait_recv()
            self.add(mine, [line_in.at[z]])
            if way == 0:
                self.line_copy(chunk, z, 0, z).start()
            else:
                self.send_up(chunk, z)

        if z < last - hop:
            when(self.z == last - hop, lambda: join(0))
        if z > hop:
            when(self.z == hop, lambda: join(1))

        def finish():
            sources = []
            if z < last:
                self.line_copy(chunk, z, 0, z).wait_recv()
                sources.append(line_in.at[z])
            if z > 0:
                self.line_copy(chunk, z, 1, self.line).wait_recv()
                sources.append(line_in.at[self.line])
            self.add(mine, sources, self.outs[chunk])

        if hop == max(z, last - z):
            when(self.z == z, finish)

    def release(self, chunk, z, tell):
        for mp in range(4):
            self.core_copy(chunk, z, mp).wait_send()
        for way in (0, 1):
            self.pass_copy(chunk, z, way).wait_send()
            self.plane_copy(chunk, z, way).wait_send()
        when(self.z > z, lambda: self.line_copy(chunk, z, 0, z).wait_send())
        when(self.z < z, lambda: self.line_copy(chunk, z, 1, z).wait_send())
        if tell:
            for device, condition, theirs, mine in self.neighbours():
                when(
                    condition,
                    lambda device=device, theirs=theirs: pl.semaphore_signal(
                        self.free.at[theirs], inc=1, device_id=device, device_id_type=MESH_ID
                    ),
                )

    def schedule(self, chunks):
        units = [(chunk, z) for chunk in chunks for z in self.order()]
        todo = []
        follows = {}
        for chunk in chunks:
            later = [c for c in chunks if c > chunk and self.sets[c] == self.sets[chunk]]
            follows[chunk] = bool(later)
        preceded = {c: any(self.sets[d] == self.sets[c] and d < c for d in chunks) for c in chunks}
        begun = set()

        def begin(at):
            if at < len(units) and at not in begun:
                begun.add(at)
                unit = units[at]
                todo.append(
                    (unit[0], functools.partial(self.stage_begin, *unit, preceded[unit[0]]))
                )

        fetched = set()

        def fetch(at):
            if at < len(units) and at not in fetched:
                fetched.add(at)
                todo.append((units[at][0], functools.partial(self.stage_own, *units[at])))

        last_hop = self.line - 1
        settled = last_hop + 3
        for at in range(len(units) + settled):
            if 0 <= at - settled < len(units):
                unit = units[at - settled]
                todo.append((None, functools.partial(self.release, *unit, follows[unit[0]])))
            begin(at)
            if at < len(units) and not preceded[units[at][0]]:
                for other in range(len(units)):
                    if units[other][0] == units[at][0]:
                        begin(other)
            fetch(at)
            stages = [(self.stage_core, 0, ()), (self.stage_pass, 1, ()), (self.stage_plane, 2, ())]
            stages += [(self.stage_line, 2 + hop, (hop,)) for hop in range(1, self.line)]
            for stage, late, more in stages:
                if 0 <= at - late < len(units):
                    unit = units[at - late]
                    todo.append((unit[0], functools.partial(stage, *unit, *more)))
            if at + 1 < len(units) and units[at + 1][0] == units[at][0]:
                begin(at + 1)
                fetch(at + 1)
        return todo


NEG = float(ml_dtypes.bfloat16(-1e30))
ONES, MASK, LOW = 0, 1, 2


def nn(a, b):
    return jnp.dot(a, b, preferred_element_type=jnp.float32)


def nt(a, b):
    return lax.dot_general(a, b, (((1,), (1,)), ((), ())), preferred_element_type=jnp.float32)


def tn(a, b):
    return lax.dot_general(a, b, (((0,), (0,)), ((), ())), preferred_element_type=jnp.float32)


def loop(total, step, body):
    def turn(at, carry):
        body(pl.ds(pl.multiple_of(at * step, step), step))
        return carry

    lax.fori_loop(0, total // step, turn, 0)


def standard(v):
    average = jnp.mean(v, axis=-1, keepdims=True)
    centered = v - average
    variance = jnp.mean(centered * centered, axis=-1, keepdims=True)
    inverse = lax.rsqrt(variance + norm_eps)
    return centered * inverse, inverse


GELU_A = math.sqrt(2.0 / math.pi)
GELU_B = 0.044715


def gelu(v):
    return 0.5 * v * (1.0 + jnp.tanh(GELU_A * (v + GELU_B * v * v * v)))


def gelu_slope(v):
    t = jnp.tanh(GELU_A * (v + GELU_B * v * v * v))
    return 0.5 * (1.0 + t) + 0.5 * v * (1.0 - t * t) * GELU_A * (1.0 + 3.0 * GELU_B * v * v)


def lane_index(shape):
    return lax.broadcasted_iota(jnp.int32, shape, len(shape) - 1)


class Plane:
    def __init__(self, dp, mp, z, core):
        self.dp, self.mp, self.z, self.core = dp, mp, z, core

    def partners(self):
        return [
            ((self.dp ^ flip_core, self.mp ^ flip_mp), None)
            for flip_core in (0, 1)
            for flip_mp in range(4)
            if flip_core or flip_mp
        ]

    def routes(self, kind, source, target):
        dp, mp, z, core = self.dp, self.mp, self.z, self.core
        sends, fills = [], []
        for turn in range(4):
            if kind == "mp":
                if turn:
                    peer = mp ^ turn
                    sends.append((source, target.at[mp], (dp, peer), mp, turn, None))
                    fills.append((target.at[peer], peer, None))
            elif kind == "mp_split":
                if turn:
                    peer = mp ^ turn
                    sends.append((source.at[peer], target.at[mp], (dp, peer), mp, turn, None))
                    fills.append((target.at[peer], peer, None))
            elif kind == "to_work":
                device = (2 * z + turn % 2, 2 * (turn // 2) + core)
                here = jnp.logical_and(device[0] == dp, device[1] == mp)
                sends.append((source.at[turn], target.at[mp], device, mp, turn, here))
                own = jnp.logical_and(mp % 2 == core, mp == turn)
                fills.append((target.at[turn], turn, own))
            elif kind == "from_work":
                device = (2 * z + mp % 2, turn)
                slot = 2 * (mp // 2) + core
                here = jnp.logical_and(device[0] == dp, device[1] == mp)
                sends.append((source, target.at[slot], device, slot, turn, here))
                own = jnp.logical_and(2 * (turn // 2) + core == mp, turn % 2 == core)
                fills.append((target.at[turn], turn, own))
        return sends, fills

    def start(self, kind, source, target, sems):
        own_sem, send_sem, recv_sem = sems
        sends, _ = self.routes(kind, source, target)
        for piece, there, device, slot, turn, here in sends:
            copy = remote(piece, there, send_sem.at[turn], recv_sem.at[slot], device)
            if here is None:
                copy.start()
            else:
                pl.when(jnp.logical_not(here))(copy.start)
                pl.when(here)(pltpu.make_async_copy(piece, there, own_sem).start)

    def arrive(self, kind, source, target, sems):
        own_sem, send_sem, recv_sem = sems
        sends, fills = self.routes(kind, source, target)
        for there, slot, own in fills:
            piece = source if kind in ("mp", "from_work") else source.at[0]
            copy = remote(piece, there, send_sem.at[0], recv_sem.at[slot], (self.dp ^ 1, self.mp))
            if own is None:
                copy.wait_recv()
            else:
                pl.when(jnp.logical_not(own))(copy.wait_recv)
        for piece, there, device, slot, turn, here in sends:
            if here is not None:
                pl.when(here)(pltpu.make_async_copy(piece, there, own_sem).wait)

    def sent(self, kind, source, target, sems):
        own_sem, send_sem, recv_sem = sems
        sends, _ = self.routes(kind, source, target)
        for piece, there, device, slot, turn, here in sends:
            copy = remote(piece, there, send_sem.at[turn], recv_sem.at[slot], device)
            if here is None:
                copy.wait_send()
            else:
                pl.when(jnp.logical_not(here))(copy.wait_send)

    def move(self, back, source, target, sems):
        send_sem, recv_sem = sems
        dp, mp, z, core = self.dp, self.mp, self.z, self.core
        if back:
            device = (2 * z + mp % 2, 2 * (mp // 2) + core)
        else:
            device = (2 * z + mp % 2, 2 * (mp // 2) + core)
        here = jnp.logical_and(device[0] == dp, device[1] == mp)
        away = jnp.logical_not(here)
        far = remote(source, target, send_sem, recv_sem, device)
        near = pltpu.make_async_copy(source, target, recv_sem)

        def start():
            pl.when(away)(far.start)
            pl.when(here)(near.start)

        def arrive():
            pl.when(away)(far.wait_recv)
            pl.when(here)(near.wait)

        def sent():
            pl.when(away)(far.wait_send)

        return start, arrive, sent


class Keeper:
    def __init__(self, sems):
        self.sems = sems
        self.count = 0
        self.open = {}

    def put(self, name, source, target):
        copy = pltpu.make_async_copy(source, target, self.sems.at[self.count])
        self.count += 1
        copy.start()
        self.open[name] = copy

    def settle(self, *names):
        for name in names or tuple(self.open):
            if name in self.open:
                self.open.pop(name).wait()


def pixel_rows(block, gain, offset, out, tail, positions_from, count, channels):
    n, inverse = standard(block.astype(jnp.float32))
    result = n * gain + offset
    rows, whole = block.shape[0], channels // 128 * 128
    rest = channels - whole
    out[:, 0:whole] = result[:, 0:whole].astype(jnp.bfloat16)
    tail[:, 0:rest] = result[:, whole:channels]
    lane = lax.broadcasted_iota(jnp.int32, (rows, 128), 1) - rest
    slot = positions_from + lax.broadcasted_iota(jnp.int32, (rows, 128), 0)
    mask = jnp.where(slot < count, 0.0, NEG)
    ones = jnp.where(jnp.logical_or(lane == ONES, lane == LOW), 1.0, 0.0)
    extra = jnp.where(lane == MASK, mask, ones)
    out[:, whole : whole + 128] = jnp.where(lane < 0, tail[...], extra).astype(jnp.bfloat16)
    return n, inverse


def interleave(comm, compute, rate):
    at, due = 0, 0.0
    for after, thunk, microseconds in compute:
        while at < after:
            comm[at]()
            at += 1
        thunk()
        due = max(due, at) + rate * microseconds
        while at < min(due, len(comm)):
            comm[at]()
            at += 1
    while at < len(comm):
        comm[at]()
        at += 1


PIXEL_BLOCK = 512
FORWARD_RATE = 1.0


def forward_kernel(slabs, latents, cotangent, pixels, counts, pixel_gain, pixel_bias, line, layers):
    bf16, f32 = jnp.bfloat16, jnp.float32
    own_rows, width = latents.shape
    items, slots, channels = pixels.shape
    wide = channels + (-channels) % 128
    chunks = len(slabs)
    q_cols = slabs[0].shape[1]
    heads = width // HD
    all_rows = 2 * own_rows
    scale = 1.0 / math.sqrt(width)
    block_scale = 1.0 / math.sqrt(HD)
    kept = dict(
        query_in=((own_rows, width), bf16),
        px=((own_rows, wide), f32),
        after_cross=((own_rows, width), f32),
        cross_hidden_in=((own_rows, width), bf16),
        cross_hidden=((own_rows, width), f32),
        cross_active=((own_rows, width), bf16),
        result=((own_rows, width), bf16),
        qk=((4, own_rows, wide), bf16),
    )
    layer_kept = dict(
        current=((own_rows, width), f32),
        normed=((own_rows, width), bf16),
        qkv=((3, own_rows, width), bf16),
        kv_in=((2, own_rows, width), bf16),
        probs=((heads, own_rows, all_rows), bf16),
        context=((own_rows, width), bf16),
        middle=((own_rows, width), f32),
        hidden_in=((own_rows, width), bf16),
        hidden=((own_rows, width), f32),
        active=((own_rows, width), bf16),
    )
    scratch_types = dict(kept)
    scratch_types.update(layer_kept)
    names = list(scratch_types)
    out_names = list(kept) + [(name, l) for l in range(layers) for name in layer_kept]
    out_types = dict(kept)
    for l in range(layers):
        out_types.update({(name, l): layer_kept[name] for name in layer_kept})
    gathered_types = [
        jax.ShapeDtypeStruct((width, q_cols), bf16),
        jax.ShapeDtypeStruct((3, width, width), bf16),
    ] + [jax.ShapeDtypeStruct((6, width, width), bf16)] * layers

    def kernel(*refs):
        refs = list(refs)

        def take(n):
            found = refs[:n]
            del refs[:n]
            return found

        slab_refs = take(chunks)
        latents_ref, cot_ref, pixels_ref, counts_ref, gain_ref, bias_ref = take(6)
        gathered = take(chunks)
        (cot_work,) = take(1)
        outs = dict(zip(out_names, take(len(out_names))))
        v = types.SimpleNamespace(**dict(zip(names, take(len(names)))))
        called = types.SimpleNamespace(**{name: name for name in names})
        weights = take(chunks)
        latents_home, latents_work, pixels_v, xs, xs_tail, scores_v, acc, top, norms, px_send, px_in = take(11)
        gather_sems = take(9)
        load_sems, io_sems, keep_sems = take(3)
        qk_sems, px_sems, move_sems, kv_sems = take(3), take(3), take(2), take(2)
        vq, vc = weights[0], weights[1]
        gatherer = Gatherer(line, slab_refs, gathered, sems=gather_sems)
        dp, mp, z, core = gatherer.dp, gatherer.mp, gatherer.z, gatherer.core
        plane = Plane(dp, mp, z, core)
        keep = Keeper(keep_sems)
        partners = plane.partners() + [
            ((dp + 2, mp), z < line - 1),
            ((dp - 2, mp), z > 0),
        ]
        greet(partners)
        def store(name):
            keep.put(name, getattr(v, name), outs[name])

        home_copy = pltpu.make_async_copy(latents_ref, latents_home, io_sems.at[0])
        pixel_copy = pltpu.make_async_copy(pixels_ref, pixels_v, io_sems.at[1])
        home_copy.start()
        pixel_copy.start()
        move_start, move_arrive, move_sent = plane.move(
            False, latents_ref, latents_work, [s.at[0] for s in move_sems]
        )
        cot_start, cot_arrive, cot_sent = plane.move(
            False, cot_ref, cot_work, [s.at[1] for s in move_sems]
        )

        def load_copy(chunk, at):
            source, target = gathered[chunk], weights[chunk]
            if chunk == 0:
                rows = pl.ds(pl.multiple_of(at * 8 * 32, 256), 256)
                return pltpu.make_async_copy(
                    source.at[rows], target.at[rows], load_sems.at[chunk, at]
                )
            span = 256
            rows = pl.ds(pl.multiple_of(at * span, span), span)
            return pltpu.make_async_copy(
                source.at[:, rows], target.at[:, rows], load_sems.at[chunk, at]
            )

        gatherer.on_unit = lambda chunk, at: load_copy(chunk, at).start()

        def loaded(chunk):
            for at in range(line):
                load_copy(chunk, at).wait()

        def norm_rows(source, j, target):
            n, _ = standard(source[...].astype(f32))
            target[...] = (n * norms[j : j + 1, :] + norms[j + 6 : j + 7, :]).astype(bf16)

        def start_queries():
            loaded(0)
            raw = vq[:, width + 2 * wide :].astype(f32)
            norms[...] = raw.T[0:16, :]
            home_copy.wait()
            norm_rows(latents_home, 0, v.query_in)
            store(called.query_in)

            v.cross_hidden_in[...] = nt(v.query_in[...], vq[:, 0:width]).astype(bf16)
            qk = nn(v.cross_hidden_in[...], vq[:, width : width + wide]) * scale
            lane = lane_index(qk.shape)
            v.qk[mp] = jnp.where(lane == channels + MASK, 1.0, qk).astype(bf16)
            plane.start("mp", v.qk.at[mp], v.qk, qk_sems)
            move_start()

        def queries_here():
            plane.arrive("mp", v.qk.at[mp], v.qk, qk_sems)
            store(called.qk)

        def cross_blocks(item, first, last):
            if first == 0:
                acc[...] = jnp.zeros_like(acc)
                top[...] = jnp.full_like(top, NEG)
            queries = v.qk[2 * item : 2 * item + 2].reshape(all_rows, wide)

            def body(at, carry):
                begin = pl.multiple_of(at * PIXEL_BLOCK, PIXEL_BLOCK)
                block = pixels_v[item, pl.ds(begin, PIXEL_BLOCK), :]
                pixel_rows(
                    block,
                    gain_ref[...],
                    bias_ref[...],
                    xs,
                    xs_tail,
                    mp * slots + begin,
                    counts_ref[item],
                    channels,
                )
                scores = nt(queries, xs[...])
                old = top[:, 0:1]
                new = jnp.maximum(old, jnp.max(scores, axis=1, keepdims=True))
                lifted = jnp.exp(scores - new).astype(bf16)
                acc[...] = acc[...] * jnp.exp(old - new) + nn(lifted, xs[...])
                top[...] = jnp.broadcast_to(new, top.shape)
                return carry

            lax.fori_loop(first, last, body, 0)

        def cross_finish(item):
            def body(rows):
                high = top[rows, 0:1]
                rounded = high.astype(bf16).astype(f32)
                value = acc[rows, :] * jnp.exp(high - rounded)
                total = value[:, channels + ONES : channels + ONES + 1]
                total_high = total.astype(bf16).astype(f32)
                lane = lane_index(value.shape)
                value = jnp.where(lane == channels + MASK, rounded, value)
                value = jnp.where(lane == channels + LOW, total - total_high, value)
                scores_v[rows, :] = value.astype(bf16)

            loop(all_rows, 64, body)
            px_send[2 * item] = scores_v[0:own_rows, :]
            px_send[2 * item + 1] = scores_v[own_rows:all_rows, :]

        def send_px():
            plane.start("to_work", px_send, px_in, px_sems)

        def merge():
            plane.arrive("to_work", px_send, px_in, px_sems)
            move_arrive()

            def body(rows):
                parts = [px_in[j, rows, :].astype(f32) for j in range(4)]
                tops = [p[:, channels + MASK : channels + MASK + 1] for p in parts]
                totals = [
                    p[:, channels + ONES : channels + ONES + 1]
                    + p[:, channels + LOW : channels + LOW + 1]
                    for p in parts
                ]
                high = jnp.maximum(jnp.maximum(tops[0], tops[1]), jnp.maximum(tops[2], tops[3]))
                shares = [jnp.exp(t - high) for t in tops]
                total = sum(s * t for s, t in zip(shares, totals))
                px = sum(s * p for s, p in zip(shares, parts)) / total
                lane = lane_index(px.shape)
                px = jnp.where(lane < channels, px, 0.0)
                v.px[rows, :] = jnp.where(
                    lane == channels, high + jnp.log(total), px
                )
                px_in[0, rows, :] = px.astype(bf16)

            loop(own_rows, 64, body)
            store(called.px)

        def cross_context():
            loaded(1)

            v.cross_active[...] = nt(
                px_in[0], vq[:, width + wide : width + 2 * wide]
            ).astype(bf16)
            v.after_cross[...] = latents_work[...].astype(f32) + nt(v.cross_active[...], vc[2])
            store(called.after_cross)

        def cross_branch():
            norm_rows(v.after_cross, 1, v.cross_hidden_in)
            store(called.cross_hidden_in)
            hidden = nt(v.cross_hidden_in[...], vc[0])
            v.cross_hidden[...] = hidden
            v.cross_active[...] = gelu(hidden).astype(bf16)
            store(called.cross_hidden)
            store(called.cross_active)

        def cross_result():
            cot_start()
            v.current[...] = v.after_cross[...] + nt(v.cross_active[...], vc[1])

        def kv_copy(t, l):
            return remote(
                v.qkv.at[1 + t],
                v.kv_in.at[t],
                kv_sems[0].at[l, t],
                kv_sems[1].at[l, t],
                (dp ^ 1, mp),
            )

        def save(name, l):
            keep.put((name, l), getattr(v, name), outs[name, l])

        def done(name, l):
            if l:
                keep.settle((name, l - 1))

        def block_qkv(l):
            w = weights[2 + l]
            loaded(2 + l)
            save(called.current, l)
            done(called.normed, l)
            norm_rows(v.current, 2 + 2 * l, v.normed)
            save(called.normed, l)
            done(called.qkv, l)
            if l:
                done(called.kv_in, l)
                for t in range(2):
                    kv_copy(t, l - 1).wait_send()
                pl.semaphore_signal(
                    kv_free, inc=1, device_id=(dp ^ 1, mp), device_id_type=MESH_ID
                )
                pl.semaphore_wait(kv_free, 1)
            for t in range(2):
                v.qkv[1 + t] = nn(v.normed[...], w[1 + t]).astype(bf16)
                kv_copy(t, l).start()

        def block_q(l):
            v.qkv[0] = nn(v.normed[...], weights[2 + l][0]).astype(bf16)
            save(called.qkv, l)
            done(called.probs, l)
            done(called.context, l)
            for t in range(2):
                kv_copy(t, l).wait_recv()

        def block_attention(first, last):
            def body(h, carry):
                one_head(2 * h)
                one_head(2 * h + 1)
                return carry

            lax.fori_loop(first // 2, last // 2, body, 0)

        def one_head(h):
            at = pl.ds(pl.multiple_of(h * HD, HD), HD)
            queries = v.qkv[0, :, at]
            keys, values = v.qkv[1, :, at], v.qkv[2, :, at]
            keys_in, values_in = v.kv_in[0, :, at], v.kv_in[1, :, at]
            near = nt(queries, keys) * block_scale
            far = nt(queries, keys_in) * block_scale
            high = jnp.maximum(
                jnp.max(near, axis=1, keepdims=True), jnp.max(far, axis=1, keepdims=True)
            )
            near, far = jnp.exp(near - high), jnp.exp(far - high)
            inverse = 1.0 / (
                jnp.sum(near, axis=1, keepdims=True) + jnp.sum(far, axis=1, keepdims=True)
            )
            near, far = (near * inverse).astype(bf16), (far * inverse).astype(bf16)
            v.probs[h, :, 0:own_rows] = near
            v.probs[h, :, own_rows:all_rows] = far
            v.context[:, at] = (nn(near, values) + nn(far, values_in)).astype(bf16)

        def block_out(l):
            w = weights[2 + l]
            save(called.kv_in, l)
            save(called.probs, l)
            save(called.context, l)
            done(called.middle, l)
            v.middle[...] = v.current[...] + nt(v.context[...], w[3])
            save(called.middle, l)
            done(called.hidden_in, l)
            norm_rows(v.middle, 3 + 2 * l, v.hidden_in)
            save(called.hidden_in, l)

        def block_up(l):
            w = weights[2 + l]
            done(called.hidden, l)
            done(called.active, l)
            hidden = nn(v.hidden_in[...], w[4])
            v.hidden[...] = hidden
            v.active[...] = gelu(hidden).astype(bf16)
            save(called.hidden, l)
            save(called.active, l)
            keep.settle((called.current, l))
            v.current[...] = v.middle[...] + nt(v.active[...], w[5])
            if l == layers - 1:
                v.result[...] = v.current[...].astype(bf16)
                store(called.result)

        (kv_free,) = take(1)
        comm, marks = gatherer.schedule(range(chunks))
        pixel_blocks = slots // PIXEL_BLOCK
        work = [
            (marks[0], start_queries, 4),
            (0, lambda: (pixel_copy.wait(), queries_here()), 1),
        ]
        for item in range(items):
            for at in range(0, pixel_blocks, 2):
                work.append((0, functools.partial(cross_blocks, item, at, at + 2), 3.5))
            work.append((0, functools.partial(cross_finish, item), 1))
        work += [
            (0, send_px, 1),
            (marks[1], merge, 2),
            (marks[1], cross_context, 2),
            (0, cross_branch, 2),
            (0, cross_result, 2),
        ]
        for l in range(layers):
            work += [
                (marks[2 + l], functools.partial(block_qkv, l), 3),
                (0, functools.partial(block_q, l), 1),
                (0, functools.partial(block_attention, 0, heads // 2), 1.5),
                (0, functools.partial(block_attention, heads // 2, heads), 1.5),
                (0, functools.partial(block_out, l), 2),
                (0, functools.partial(block_up, l), 2),
            ]
        interleave(comm, work, FORWARD_RATE)
        plane.sent("mp", v.qk.at[mp], v.qk, qk_sems)
        plane.sent("to_work", px_send, px_in, px_sems)
        move_sent()
        cot_arrive()
        cot_sent()
        for t in range(2):
            kv_copy(t, layers - 1).wait_send()
        keep.settle()

    results = pl.pallas_call(
        kernel,
        out_shape=tuple(
            gathered_types
            + [jax.ShapeDtypeStruct(cotangent.shape, bf16)]
            + [jax.ShapeDtypeStruct(*out_types[name]) for name in out_names]
        ),
        in_specs=[ANY] * chunks
        + [ANY, ANY, ANY, pl.BlockSpec(memory_space=pltpu.SMEM)]
        + [pl.BlockSpec(memory_space=pltpu.VMEM)] * 2,
        out_specs=[ANY] * (chunks + 1 + len(out_names)),
        scratch_shapes=[pltpu.VMEM(*scratch_types[name]) for name in names]
        + [pltpu.VMEM(t.shape, t.dtype) for t in gathered_types]
        + [
            pltpu.VMEM((own_rows, width), bf16),
            pltpu.VMEM((own_rows, width), bf16),
            pltpu.VMEM(pixels.shape, bf16),
            pltpu.VMEM((PIXEL_BLOCK, wide), bf16),
            pltpu.VMEM((PIXEL_BLOCK, 128), f32),
            pltpu.VMEM((all_rows, wide), bf16),
            pltpu.VMEM((all_rows, wide), f32),
            pltpu.VMEM((all_rows, 128), f32),
            pltpu.VMEM((16, width), f32),
            pltpu.VMEM((4, own_rows, wide), bf16),
            pltpu.VMEM((4, own_rows, wide), bf16),
        ]
        + Gatherer.sem_shapes(chunks, line)
        + [DMA((chunks, line)), DMA((2,)), DMA((len(out_names),))]
        + [DMA(()), DMA((4,)), DMA((4,))] * 2
        + [DMA((2,)), DMA((2,))]
        + [DMA((layers, 2)), DMA((layers, 2))]
        + [pltpu.SemaphoreType.REGULAR],
        compiler_params=pltpu.CompilerParams(
            collective_id=0, has_side_effects=True, vmem_limit_bytes=63 * 1024 * 1024
        ),
        name="forward",
    )(*slabs, latents, cotangent, pixels, counts, pixel_gain, pixel_bias)
    return results[:chunks], results[chunks], dict(zip(out_names, results[chunks + 1 :]))


BACK_BLOCK = 512


def backward_kernel(
    gathered, kept, cotangent, result, latents, pixels, counts, pixel_gain, pixel_bias, line, layers
):
    bf16, f32 = jnp.bfloat16, jnp.float32
    own_rows, width = latents.shape
    items, slots, channels = pixels.shape
    wide = channels + (-channels) % 128
    q_cols = gathered[0].shape[1]
    cols_m = width // 4
    heads = width // HD
    all_rows = 2 * own_rows
    scale = 1.0 / math.sqrt(width)
    block_scale = 1.0 / math.sqrt(HD)
    own_cols = width // (8 * line)
    rows_d = width // (2 * line)
    gk_cols = 2 * wide + 128
    kept_names = list(kept)
    layer_names = [name[0] for name in kept_names if isinstance(name, tuple) and name[1] == 0]
    qk_name = next(name for name in kept_names if name == "qk")
    slabs = [(3, rows_d, cols_m)] * (2 * layers) + [(2, own_cols, width), (own_cols, gk_cols)]
    sets = [0, 1] * layers + [2, 3]
    chunks = len(slabs)
    c_chunk, gk_chunk = 2 * layers, 2 * layers + 1
    part_types = [jax.ShapeDtypeStruct((3, width, width), bf16)] * (2 * layers) + [
        jax.ShapeDtypeStruct((2, width, width), bf16),
        jax.ShapeDtypeStruct((width, gk_cols), bf16),
    ]
    reduced_types = [jax.ShapeDtypeStruct(s, f32) for s in slabs[:-1]]
    other_types = [
        jax.ShapeDtypeStruct((width, gk_cols), bf16),
        jax.ShapeDtypeStruct((own_rows, width), bf16),
        jax.ShapeDtypeStruct(pixels.shape, bf16),
        jax.ShapeDtypeStruct((own_rows, width), bf16),
    ]
    v_types = {name: (kept[name, 0].shape, kept[name, 0].dtype) for name in layer_names}
    v_types.update(
        dict(
            qk=(kept[qk_name].shape, bf16),
            weights=((6, width, width), bf16),
            stage=((4, width, 256), bf16),
            cot=((own_rows, width), f32),
            tmp=((own_rows, width), f32),
            low=((own_rows, width), bf16),
            turned=((width, own_rows), bf16),
            qkv_cot=((3, own_rows, width), bf16),
            kv_out=((2, own_rows, width), bf16),
            kv_in_cot=((layers, 2, own_rows, width), bf16),
            norms=((16, width), f32),
            grads=((16, width), f32),
            after_home=((own_rows, width), bf16),
            cv_all=((4, own_rows, wide), bf16),
            dsx_in=((4, own_rows, wide), bf16),
            block=((2, BACK_BLOCK, channels), bf16),
            out_block=((2, BACK_BLOCK, channels), bf16),
            xs=((BACK_BLOCK, wide), bf16),
            xs_tail=((BACK_BLOCK, 128), f32),
            pixel_sums=((16, channels), f32),
            gk_own=((own_cols, gk_cols), f32),
            gk_low=((own_cols, gk_cols), bf16),
        )
    )
    v_names = list(v_types)
    ins = list(gathered) + [kept[n] for n in kept_names]

    def kernel(*refs):
        refs = list(refs)

        def take(n):
            found = refs[:n]
            del refs[:n]
            return found

        g_refs = take(len(gathered))
        layer_refs = dict(zip(kept_names, take(len(kept_names))))
        kept_refs = types.SimpleNamespace(
            **{name: ref for name, ref in layer_refs.items() if not isinstance(name, tuple)}
        )
        cot_ref, result_ref, latents_ref, pixels_ref, counts_ref, gain_ref, bias_ref = take(7)
        parts = take(chunks)
        reduced = take(chunks - 1)
        gk_all, latent_grad_ref, pixel_grad_ref, out_ref = take(4)
        v = types.SimpleNamespace(**dict(zip(v_names, take(len(v_names)))))
        called = types.SimpleNamespace(**{name: name for name in v_names})
        v.low2 = v.active
        v.px = v.middle.at[:, pl.ds(0, wide)]
        v.cv = v.context.at[:, pl.ds(0, wide)]

        class Pieces:
            def __getitem__(self, piece):
                column = pl.multiple_of(piece % 2 * all_rows, all_rows)
                return v.kv_out.at[piece // 2, :, pl.ds(column, wide)]

        pieces = types.SimpleNamespace(at=Pieces())
        acc_parts = (
            (v.tmp.at[:, pl.ds(0, all_rows)], slice(0, own_rows)),
            (v.tmp.at[pl.ds(0, wide - own_rows), pl.ds(all_rows, all_rows)], slice(own_rows, wide)),
        )
        buffers = take(len(Reducer.buffer_shapes(slabs, sets, line)))
        reduce_sems = take(10)
        gather_sems = take(9)
        fetch_sems, stage_sems, block_sems, out_sems = take(4)
        kv_sems, cv_sems, dsx_sems, move_sems = take(2), take(3), take(3), take(2)
        reducer = Reducer(line, parts, slabs, reduced + [v.gk_own], sets, buffers, reduce_sems)
        gatherer = Gatherer(line, [v.gk_low], [gk_all], gather_sems)
        dp, mp, z, core = reducer.dp, reducer.mp, reducer.z, reducer.core
        plane = Plane(dp, mp, z, core)
        greet(
            plane.partners()
            + [((dp + 2, mp), z < line - 1), ((dp - 2, mp), z > 0)]
        )
        w = v.weights
        open_copies = {}
        numbered = []

        def fetch(tag, source, target):
            copy = pltpu.make_async_copy(source, target, fetch_sems.at[len(numbered)])
            numbered.append(tag)
            copy.start()
            open_copies[tag] = copy

        def here(*tags):
            for tag in tags:
                if tag in open_copies:
                    open_copies.pop(tag).wait()

        w_qkv, w_out, w_up, w_down = (0, 3), (3, 1), (4, 1), (5, 1)

        def fetch_weight(span, l):
            if l >= 0:
                part = pl.ds(*span)
                fetch((span, l), g_refs[2 + l].at[part], w.at[part])

        def fetch_kept(name, l):
            if l >= 0:
                fetch((name, l), layer_refs[name, l], getattr(v, name))

        stage_open = []

        def stage_out(at, value, target):
            n = value.shape[1]
            slot = v.stage.at[at, :, pl.ds(0, n)] if n < 256 else v.stage.at[at]
            slot[...] = value
            return pltpu.make_async_copy(slot, target, stage_sems.at[at])

        def settle_stage():
            while stage_open:
                stage_open.pop()()

        def grad_out(right, target):
            settle_stage()

            copies = []
            for m in range(4):
                copy = stage_out(m, nn(v.turned[...], right(m)).astype(bf16), target(m))
                copy.start()
                copies.append(copy)

            def settle():
                for copy in copies:
                    copy.wait()

            stage_open.append(settle)

        def layer_part(l, which):
            part = parts[2 * (layers - 1 - l) + (0 if which >= 3 else 1)]
            return lambda m: part.at[which % 3, :, lane_block(m)]

        def lane_block(m):
            return pl.ds(m * 256, 256)

        def turn(value):
            v.turned[...] = value[...].T

        def norm_back_into(source, j, add, write):
            gains = biases = jnp.zeros((1, width), f32)
            for first_row in range(0, own_rows, own_rows // 2):
                rows = slice(first_row, first_row + own_rows // 2)
                n, inverse = standard(source[rows, :].astype(f32))
                u = v.tmp[rows, :]
                scaled = u * v.norms[j : j + 1, :]
                first = jnp.mean(scaled, axis=1, keepdims=True)
                second = jnp.mean(scaled * n, axis=1, keepdims=True)
                write(rows, add(rows) + (scaled - first - n * second) * inverse)
                gains = gains + jnp.sum(u * n, axis=0, keepdims=True)
                biases = biases + jnp.sum(u, axis=0, keepdims=True)
            v.grads[j : j + 1, :] = gains
            v.grads[j + 6 : j + 7, :] = biases

        def into_cot(rows, value):
            v.cot[rows, :] = value

        def add_cot(rows):
            return v.cot[rows, :]

        def each(body):
            def step(m, carry):
                body(m)
                return carry

            lax.fori_loop(0, 4, step, 0)

        def begin():
            fetch(0, g_refs[0].at[:, pl.ds(width + 2 * wide, 128)], v.stage.at[0, :, pl.ds(0, 128)])
            fetch(1, cot_ref, v.low)
            out_start()
            last = layers - 1
            fetch_kept(called.active, last)
            fetch_weight(w_down, last)
            fetch_kept(called.hidden, last)
            fetch_kept(called.hidden_in, last)
            fetch_weight(w_up, last)
            fetch_kept(called.middle, last)
            fetch_weight(w_out, last)
            for name in (called.context, called.probs, called.qkv, called.kv_in, called.normed):
                fetch_kept(name, last)
            fetch_weight(w_qkv, last)
            fetch_kept(called.current, last)
            fetch(3, kept_refs.qk, v.qk)
            v.grads[...] = jnp.zeros_like(v.grads)
            here(0, 1)
            raw = v.stage[0, :, 0:128].astype(f32)
            v.norms[...] = raw.T[0:16, :]
            v.cot[...] = v.low[...].astype(f32)

        def branch_a(l):
            v.low[...] = v.cot[...].astype(bf16)
            turn(v.low)
            here((called.active, l))
            grad_out(lambda m: v.active[:, lane_block(m)], layer_part(l, 5))

        def branch_a2(l):
            here((w_down, l), (called.hidden, l))
            active_cot = nn(v.low[...], w[5])
            v.active[...] = (active_cot * gelu_slope(v.hidden[...])).astype(bf16)
            fetch_weight(w_down, l - 1)
            fetch_kept(called.hidden, l - 1)

        def branch_b(l):
            here((called.hidden_in, l))
            turn(v.hidden_in)
            fetch_kept(called.hidden_in, l - 1)
            grad_out(lambda m: v.active[:, lane_block(m)], layer_part(l, 4))

        def branch_b2(l):
            here((w_up, l), (called.middle, l))
            v.tmp[...] = nt(v.active[...], w[4])
            norm_back_into(v.middle, 3 + 2 * l, add_cot, into_cot)
            fetch_weight(w_up, l - 1)
            fetch_kept(called.active, l - 1)
            fetch_kept(called.middle, l - 1)

        def branch_c(l):
            v.low[...] = v.cot[...].astype(bf16)
            turn(v.low)
            here((called.context, l), (w_out, l))
            grad_out(lambda m: v.context[:, lane_block(m)], layer_part(l, 3))
            v.context[...] = nn(v.low[...], w[3]).astype(bf16)
            fetch_weight(w_out, l - 1)
            settle_stage()

        def kv_copy(t, l):
            return remote(
                v.kv_out.at[t],
                v.kv_in_cot.at[l, t],
                kv_sems[0].at[l, t],
                kv_sems[1].at[l, t],
                (dp ^ 1, mp),
            )

        def attention(l, first, last):
            if first == 0:
                here((called.probs, l), (called.qkv, l), (called.kv_in, l))
                if l < layers - 1:
                    for t in range(2):
                        kv_copy(t, l + 1).wait_send()

            def body(h, carry):
                one_head(2 * h)
                one_head(2 * h + 1)
                return carry

            lax.fori_loop(first // 2, last // 2, body, 0)
            if last == heads:
                for t in range(2):
                    kv_copy(t, l).start()
                for name in (called.context, called.probs, called.qkv, called.kv_in):
                    fetch_kept(name, l - 1)

        def one_head(h):
            at = pl.ds(pl.multiple_of(h * HD, HD), HD)
            queries = v.qkv[0, :, at]
            keys, values = v.qkv[1, :, at], v.qkv[2, :, at]
            keys_in, values_in = v.kv_in[0, :, at], v.kv_in[1, :, at]
            up = v.context[:, at]
            near_low = v.probs[h, :, 0:own_rows]
            far_low = v.probs[h, :, own_rows:all_rows]
            v.qkv_cot[2, :, at] = tn(near_low, up).astype(bf16)
            v.kv_out[1, :, at] = tn(far_low, up).astype(bf16)
            near, far = near_low.astype(f32), far_low.astype(f32)
            near_cot = near * nt(up, values)
            far_cot = far * nt(up, values_in)
            row = jnp.sum(near_cot, axis=1, keepdims=True) + jnp.sum(
                far_cot, axis=1, keepdims=True
            )
            near_cot = ((near_cot - near * row) * block_scale).astype(bf16)
            far_cot = ((far_cot - far * row) * block_scale).astype(bf16)
            v.qkv_cot[0, :, at] = (nn(near_cot, keys) + nn(far_cot, keys_in)).astype(bf16)
            v.qkv_cot[1, :, at] = tn(near_cot, queries).astype(bf16)
            v.kv_out[0, :, at] = tn(far_cot, queries).astype(bf16)

        def branch_d(l):
            here((called.normed, l))
            turn(v.normed)
            fetch_kept(called.normed, l - 1)
            grad_out(lambda m: v.qkv_cot[0, :, lane_block(m)], layer_part(l, 0))
            for t in range(2):
                kv_copy(t, l).wait_recv()
                v.qkv_cot[1 + t] = (
                    v.qkv_cot[1 + t].astype(f32) + v.kv_in_cot[l, t].astype(f32)
                ).astype(bf16)

        def branch_d2(l):
            for t in (1, 2):
                grad_out(lambda m, t=t: v.qkv_cot[t, :, lane_block(m)], layer_part(l, t))

        def branch_e(l):
            here((w_qkv, l), (called.current, l))
            v.tmp[...] = nt(v.qkv_cot[0], w[0]) + nt(v.qkv_cot[1], w[1]) + nt(v.qkv_cot[2], w[2])
            norm_back_into(v.current, 2 + 2 * l, add_cot, into_cot)
            fetch_weight(w_qkv, l - 1)
            fetch_kept(called.current, l - 1)
            settle_stage()

        def cross_begin():
            for k in range(3):
                fetch(4 + k, g_refs[1].at[k], w.at[k])
            fetch(7, g_refs[0].at[:, pl.ds(0, width)], w.at[3])
            fetch(8, g_refs[0].at[:, pl.ds(width, wide)], w.at[4, :, pl.ds(0, wide)])
            fetch(9, g_refs[0].at[:, pl.ds(width + wide, wide)], w.at[5, :, pl.ds(0, wide)])
            fetch(10, kept_refs.after_cross, v.current)
            fetch(11, kept_refs.cross_hidden_in, v.hidden_in)
            fetch(12, kept_refs.cross_active, v.normed)
            fetch(13, kept_refs.cross_hidden, v.middle)
            v.low[...] = v.cot[...].astype(bf16)
            turn(v.low)

        def cross_a():
            here(12)
            grad_out(
                lambda m: v.normed[:, lane_block(m)],
                lambda m: parts[c_chunk].at[1, :, lane_block(m)],
            )
            here(5, 13)

            active_cot = nn(v.low[...], w[1])
            v.low2[...] = (active_cot * gelu_slope(v.middle[...])).astype(bf16)

        def cross_b():
            turn(v.low2)
            here(11, 4)
            grad_out(
                lambda m: v.hidden_in[:, lane_block(m)],
                lambda m: parts[c_chunk].at[0, :, lane_block(m)],
            )

        def cross_b2():
            fetch(2, kept_refs.px, v.px)
            v.tmp[...] = nn(v.low2[...], w[0])
            here(10)
            norm_back_into(v.current, 1, add_cot, into_cot)
            v.low[...] = v.cot[...].astype(bf16)
            settle_stage()
            fetch(14, kept_refs.query_in, v.normed)
            fetch(15, latents_ref, v.hidden_in)

        home_start, home_arrive, home_sent = plane.move(
            True, v.low, v.after_home, [s.at[0] for s in move_sems]
        )
        out_start, out_arrive, out_sent = plane.move(
            True, result_ref, out_ref, [s.at[1] for s in move_sems]
        )

        def gk_columns(value, column):
            settle_stage()
            copies = [
                stage_out(0, value[:, 0:256], parts[gk_chunk].at[:, pl.ds(column, 256)]),
                stage_out(1, value[:, 256:wide], parts[gk_chunk].at[:, pl.ds(column + 256, wide - 256)]),
            ]
            for copy in copies:
                copy.start()
                stage_open.append(copy.wait)

        def cross_c():
            home_start()
            turn(v.low)
            here(2, 6, 9)
            lane = lane_index((own_rows, wide))
            px = v.px[...]
            px = jnp.where(lane < channels, px, 0.0)
            gk_columns(nn(v.turned[...], px.astype(bf16)).astype(bf16), wide)

            v.low2[...] = nn(v.low[...], w[2]).astype(bf16)
            cv = nn(v.low2[...], w[5, :, 0:wide]).astype(bf16).astype(f32)
            delta = jnp.sum(cv * px, axis=1, keepdims=True)
            logs = v.px[:, channels : channels + 1]

            def two(value):
                high = value.astype(bf16).astype(f32)
                return high, value - high

            delta_high, delta_low = two(-delta)
            log_high, log_low = two(logs)
            for at, value in (
                (ONES, delta_high),
                (LOW, delta_low),
                (3, log_high),
                (4, log_low),
            ):
                cv = jnp.where(lane == channels + at, value, cv)
            v.cv[...] = cv.astype(bf16)
            plane.start("from_work", v.cv, v.cv_all, cv_sems)

        def cross_d():
            plane.arrive("from_work", v.cv, v.cv_all, cv_sems)
            here(3)

            def body(m):
                cv = v.cv_all[m].astype(f32)
                qk = v.qk[m].astype(f32)
                lane = lane_index(qk.shape)
                qk = jnp.where(lane == channels + ONES, -cv[:, channels + 3 : channels + 4], qk)
                qk = jnp.where(lane == channels + LOW, -cv[:, channels + 4 : channels + 5], qk)
                v.qk[m] = qk.astype(bf16)

            each(body)
            v.pixel_sums[...] = jnp.zeros_like(v.pixel_sums)

        blocks = slots // BACK_BLOCK

        def block_in(item, at):
            rows = pl.ds(pl.multiple_of(at * BACK_BLOCK, BACK_BLOCK), BACK_BLOCK)
            return pltpu.make_async_copy(
                pixels_ref.at[item, rows], v.block.at[lax.rem(at, 2)], block_sems.at[lax.rem(at, 2)]
            )

        def block_out(item, at):
            rows = pl.ds(pl.multiple_of(at * BACK_BLOCK, BACK_BLOCK), BACK_BLOCK)
            return pltpu.make_async_copy(
                v.out_block.at[lax.rem(at, 2)],
                pixel_grad_ref.at[item, rows],
                out_sems.at[lax.rem(at, 2)],
            )

        def cross_blocks(item, first, last):
            block_in(item, first).start()
            if first == 0:
                v.tmp[...] = jnp.zeros_like(v.tmp)
            queries = v.qk[2 * item : 2 * item + 2].reshape(all_rows, wide)
            cvs = v.cv_all[2 * item : 2 * item + 2].reshape(all_rows, wide)

            def body(at, carry):
                slot = lax.rem(at, 2)
                block_in(item, at).wait()
                pl.when(at + 1 < last)(lambda: block_in(item, at + 1).start())
                gain = gain_ref[...]
                n, inverse = pixel_rows(
                    v.block[slot],
                    gain,
                    bias_ref[...],
                    v.xs,
                    v.xs_tail,
                    mp * slots + at * BACK_BLOCK,
                    counts_ref[item],
                    channels,
                )
                xs = v.xs[...]
                probs = jnp.exp(nt(xs, queries))
                score_cot = (probs * nt(xs, cvs)).astype(bf16)
                u = nn(score_cot, queries) + nn(probs.astype(bf16), cvs)
                sums = tn(xs, score_cot)
                for part, rows in acc_parts:
                    part[...] += sums[rows]
                u = u[:, 0:channels]
                scaled = u * gain
                mean = jnp.mean(scaled, axis=1, keepdims=True)
                second = jnp.mean(scaled * n, axis=1, keepdims=True)
                v.pixel_sums[0:1, :] += jnp.sum(u * n, axis=0, keepdims=True)
                v.pixel_sums[1:2, :] += jnp.sum(u, axis=0, keepdims=True)
                pl.when(at >= first + 2)(lambda: block_out(item, at - 2).wait())
                v.out_block[slot] = ((scaled - mean - n * second) * inverse).astype(bf16)
                block_out(item, at).start()
                return carry

            lax.fori_loop(first, last, body, 0)
            block_out(item, last - 2).wait()
            block_out(item, last - 1).wait()

        def cross_finish(item):
            whole = jnp.concatenate([part[...] for part, _ in acc_parts], axis=0)
            whole = (whole * scale).T
            lane = lane_index(whole.shape)
            whole = jnp.where(lane < channels, whole, 0.0).astype(bf16)
            if item == 0:
                for t in range(2):
                    kv_copy(t, 0).wait_send()
            for half in range(2):
                piece = pieces.at[2 * item + half]
                piece[...] = whole[half * own_rows : (half + 1) * own_rows]

        def send_dsx():
            plane.start("mp_split", pieces, v.dsx_in, dsx_sems)
            here(14)
            turn(v.normed)

        def home():
            plane.arrive("mp_split", pieces, v.dsx_in, dsx_sems)
            total = pieces.at[mp][...].astype(f32)
            for flip in range(1, 4):
                total = total + v.dsx_in[mp ^ flip].astype(f32)
            dsx = total.astype(bf16)
            gk_columns(nn(v.turned[...], dsx).astype(bf16), 0)
            here(7, 8, 15)
            home_sent()

            v.low2[...] = nt(dsx, w[4, :, 0:wide]).astype(bf16)
            v.tmp[...] = nn(v.low2[...], w[3])
            home_arrive()

            def write(rows, value):
                v.low[rows, :] = value.astype(bf16)

            norm_back_into(
                v.hidden_in, 0, lambda rows: v.after_home[rows, :].astype(f32), write
            )
            fetch(16, v.low, latent_grad_ref)
            v.grads[12:14, 0:channels] = v.pixel_sums[0:2, :]
            settle_stage()
            v.tmp[0:128, :] = jnp.zeros((128, width), f32)
            v.tmp[0:16, :] = v.grads[...]
            copy = stage_out(
                2, v.tmp[0:128, :].T.astype(bf16), parts[gk_chunk].at[:, pl.ds(2 * wide, 128)]
            )
            copy.start()
            copy.wait()

        work = [(begin, None, 3)]
        for l in reversed(range(layers)):
            rest = 2 * (layers - 1 - l)
            half = heads // 2
            work += [
                (functools.partial(branch_a, l), None, 1.6),
                (functools.partial(branch_a2, l), None, 1.2),
                (functools.partial(branch_b, l), None, 1.6),
                (functools.partial(branch_b2, l), None, 1.5),
                (functools.partial(branch_c, l), rest, 2.5),
                (functools.partial(attention, l, 0, half), None, 2),
                (functools.partial(attention, l, half, heads), None, 2),
                (functools.partial(branch_d, l), None, 2),
                (functools.partial(branch_d2, l), None, 2.6),
                (functools.partial(branch_e, l), rest + 1, 3.2),
            ]
        work += [
            (cross_begin, None, 0.5),
            (cross_a, None, 2.3),
            (cross_b, None, 1.6),
            (cross_b2, c_chunk, 1.3),
            (cross_c, None, 3),
            (cross_d, None, 0.5),
        ]
        for item in range(items):
            for at in range(0, blocks, 2):
                work.append((functools.partial(cross_blocks, item, at, at + 2), None, 4.6))
            work.append((functools.partial(cross_finish, item), None, 1))
        work += [(send_dsx, None, 0.5), (home, gk_chunk, 4)]
        comm = reducer.schedule(range(chunks))
        ready, at, due = {None}, 0, 0.0
        for thunk, makes, microseconds in work:
            thunk()
            if makes is not None:
                ready.add(makes)
            if len(ready) > 1:
                due = max(due, at) + BACK_RATE * microseconds
            while at < min(due, len(comm)) and comm[at][0] in ready:
                comm[at][1]()
                at += 1
        while at < len(comm):
            comm[at][1]()
            at += 1
        v.gk_low[...] = v.gk_own[...].astype(bf16)
        for thunk in gatherer.schedule([0])[0]:
            thunk()
        out_arrive()
        out_sent()
        plane.sent("from_work", v.cv, v.cv_all, cv_sems)
        plane.sent("mp_split", pieces, v.dsx_in, dsx_sems)
        here(*list(open_copies))

    vmem = pl.BlockSpec(memory_space=pltpu.VMEM)
    fetches = (layers * (len(layer_names) + 4)) + 20
    results = pl.pallas_call(
        kernel,
        out_shape=tuple(part_types + reduced_types + other_types),
        in_specs=[ANY] * (len(ins) + 4)
        + [pl.BlockSpec(memory_space=pltpu.SMEM), vmem, vmem],
        out_specs=[ANY] * chunks + [vmem] * (chunks - 1) + [ANY] * 4,
        scratch_shapes=[pltpu.VMEM(*v_types[name]) for name in v_names]
        + Reducer.buffer_shapes(slabs, sets, line)
        + Reducer.sem_shapes(chunks, line)
        + Gatherer.sem_shapes(1, line)
        + [DMA((fetches,)), DMA((4,)), DMA((2,)), DMA((2,))]
        + [DMA((layers, 2)), DMA((layers, 2))]
        + [DMA(()), DMA((4,)), DMA((4,))] * 2
        + [DMA((2,)), DMA((2,))],
        compiler_params=pltpu.CompilerParams(
            collective_id=1, has_side_effects=True, vmem_limit_bytes=63 * 1024 * 1024
        ),
        name="backward",
    )(*ins, cotangent, result, latents, pixels, counts, pixel_gain, pixel_bias)
    return results[chunks : 2 * chunks - 1], results[2 * chunks - 1 :]


BACK_RATE = 1.6


def fast_shards(
    latents,
    pixels,
    pixel_counts,
    cross_query,
    cross_key,
    cross_value,
    cross_out,
    cross_up,
    cross_down,
    block_qkv,
    block_out,
    block_up,
    block_down,
    norm_gains,
    norm_biases,
    pixel_gain,
    pixel_bias,
    cotangent,
):
    bf16, f32 = jnp.bfloat16, jnp.float32
    line = lax.axis_size("dp") // 2
    layers, rows_d, _, cols_m = block_qkv.shape
    own_rows, width = latents.shape
    channels = pixels.shape[2]
    own_cols = cross_query.shape[1]
    pad = (-channels) % 128
    wide = channels + pad

    def lanes(v):
        return jnp.pad(v, ((0, 0), (0, pad)))

    norms = jnp.concatenate([norm_gains, norm_biases], axis=0)
    norm_count = norm_gains.shape[0]
    slab_q = jnp.concatenate(
        [
            cross_query.T,
            lanes(cross_key.T),
            lanes(cross_value.T),
            jnp.pad(norms.T, ((0, 0), (0, 128 - 2 * norm_count))),
        ],
        axis=1,
    )
    slab_c = jnp.stack([cross_up.T, cross_down.T, cross_out.T], axis=0)
    slabs_l = [
        jnp.concatenate(
            [
                jnp.swapaxes(block_qkv[l], 0, 1),
                jnp.stack([block_out[l], block_up[l], block_down[l]], axis=0),
            ],
            axis=0,
        )
        for l in range(layers)
    ]
    gain_row, bias_row = pixel_gain.astype(f32)[None], pixel_bias.astype(f32)[None]
    gathered, cotangent_work, kept = forward_kernel(
        [slab_q, slab_c] + slabs_l,
        latents,
        cotangent,
        pixels,
        pixel_counts,
        gain_row,
        bias_row,
        line,
        layers,
    )
    result_name = next(name for name in kept if name == "result")
    result = kept.pop(result_name)
    reduced, (gk_all, latent_grad, pixel_grad, latents_out) = backward_kernel(
        gathered,
        kept,
        cotangent_work,
        result,
        latents,
        pixels,
        pixel_counts,
        gain_row,
        bias_row,
        line,
        layers,
    )
    value_t = gathered[0][:, width + wide : width + wide + channels]
    g_all = gk_all[:, :channels]
    k_all = gk_all[:, wide : wide + channels]
    small = gk_all[:, 2 * wide :].astype(f32)
    at = (lax.axis_index("dp") * 4 + lax.axis_index("mp")) * own_cols
    small_own = lax.dynamic_slice_in_dim(small, at, own_cols, 0)
    k_own = lax.dynamic_slice_in_dim(k_all, at, own_cols, 0)
    out_own = lax.dynamic_slice_in_dim(gathered[1][2], at, own_cols, 1)
    rest_grads = [reduced[2 * (layers - 1 - l)] for l in range(layers)]
    qkv_grads = [reduced[2 * (layers - 1 - l) + 1] for l in range(layers)]
    qkv_out = jnp.swapaxes(jnp.stack(qkv_grads, axis=0), 1, 2)
    out_out, up_out, down_out = [jnp.stack([g[k] for g in rest_grads], axis=0) for k in range(3)]
    return (
        latents_out,
        latent_grad,
        pixel_grad,
        matmul(g_all, cross_key),
        transposed_times(g_all, cross_query),
        transposed_times(k_all, out_own),
        times_transposed(value_t, k_own),
        reduced[2 * layers][0].T,
        reduced[2 * layers][1].T,
        qkv_out,
        out_out,
        up_out,
        down_out,
        small_own[:, :norm_count].T,
        small_own[:, norm_count : 2 * norm_count].T,
        small[:channels, 2 * norm_count],
        small[:channels, 2 * norm_count + 1],
    )


def fits(mesh):
    return mesh.shape["mp"] == 4 and mesh.shape["dp"] % 2 == 0


def solution(mesh):
    return jax.shard_map(
        fast_shards if fits(mesh) else shards,
        mesh=mesh,
        in_specs=(
            P(("dp", "mp"), None),
            P("dp", "mp", None),
            P("dp"),
            P(None, ("dp", "mp")),
            P(None, ("dp", "mp")),
            P(None, ("dp", "mp")),
            P(None, ("dp", "mp")),
            P(None, ("dp", "mp")),
            P(None, ("dp", "mp")),
            P(None, "dp", None, "mp"),
            P(None, "dp", "mp"),
            P(None, "dp", "mp"),
            P(None, "dp", "mp"),
            P(None, ("dp", "mp")),
            P(None, ("dp", "mp")),
            P(),
            P(),
            P(("dp", "mp"), None),
        ),
        out_specs=(
            P(("dp", "mp"), None),
            P(("dp", "mp"), None),
            P("dp", "mp", None),
            P(None, ("dp", "mp")),
            P(None, ("dp", "mp")),
            P(None, ("dp", "mp")),
            P(None, ("dp", "mp")),
            P(None, ("dp", "mp")),
            P(None, ("dp", "mp")),
            P(None, "dp", None, "mp"),
            P(None, "dp", "mp"),
            P(None, "dp", "mp"),
            P(None, "dp", "mp"),
            P(None, ("dp", "mp")),
            P(None, ("dp", "mp")),
            P(),
            P(),
        ),
        check_vma=False,
    )
```
